32 devices in a mesh: dp: 8 (over y, x, core), mp: 4 (over z).
Axes of the slice: x: 2, y: 2, z: 4, core: 2. Of those that a mesh axis runs over, the one named last changes fastest.
Arguments:
- block_in: bfloat16 [2048, 1024], P('dp'), may hold values from -6 to 6
- cotangent: bfloat16 [2048, 1024], P('dp'), may hold values from -6 to 6
- norm_gains: float32 [2, 1024], replicated, may hold values from 0.1 to 1.9
- col_weights: bfloat16 [5, 1024, 1024], P(None, None, 'mp'), may hold values from -0.1875 to 0.1875
- row_weights: bfloat16 [2, 1024, 1024], P(None, 'mp'), may hold values from -0.75 to 0.75
- mem_keys: bfloat16 [2, 4, 256, 128], P(None, 'mp'), may hold values from -0.125 to 0.125
- value_table: bfloat16 [65536, 1024], P(('dp', 'mp')), may hold values from -6 to 6
- col_down: bfloat16 [5, 8, 16, 1024], replicated, may hold values from -0.1875 to 0.1875
- col_up: bfloat16 [5, 8, 16, 1024], P(None, None, None, 'mp'), may hold values from -1.5 to 1.5
- row_down: bfloat16 [2, 8, 16, 1024], P(None, None, None, 'mp'), may hold values from -0.75 to 0.75
- row_up: bfloat16 [2, 8, 16, 1024], replicated, may hold values from -1.5 to 1.5
- segment_ids: int32 [8, 256], P('dp'), may hold values from 0 to 7, never falling along the last dimension, each value on 1 to 128 neighbouring positions
- adapter_ids: int32 [8], P('dp'), may hold values from 0 to 7, as said below
- pick_ids: int32 [2048, 4, 32], P('dp', 'mp'), may hold values from 0 to 65535, as said below
Outputs:
- block_out: bfloat16 [2048, 1024], P('dp')
- input_grad: float32 [2048, 1024], P('dp')
- table_grad: float32 [65536, 1024], P(('dp', 'mp'))
- col_down_grad: float32 [5, 8, 16, 1024], replicated
- col_up_grad: float32 [5, 8, 16, 1024], P(None, None, None, 'mp')
- row_down_grad: float32 [2, 8, 16, 1024], P(None, None, None, 'mp')
- row_up_grad: float32 [2, 8, 16, 1024], replicated
The draws below stay inside these ranges and needn't reach their ends.
Inputs may be any that keep to these rules, and one draw needn't show every extreme that they name: `pick_ids`: owner o, the device whose index over dp+mp is o, holds rows o * 2048 to (o + 1) * 2048 - 1. Among the picks of one memory head for one aligned block of 128 tokens of a sequence at most 256 lie in one owner's rows, and in every such block the same quarter of the owners holds exactly 256. `adapter_ids`: every adapter is named by exactly 1 sequence. `segment_ids`: along a sequence the document number never falls; a document holds at most 128 tokens, and one holds exactly that many.
All inputs are finite; a program needn't handle non-finite values.
Results may differ from the reference program's by a relative error of at most 0.018.
Values may be sent and summed in bfloat16 or wider, within the bound.
A program may use at most 192 MiB of HBM per device.

```python
import math
import jax
import jax.numpy as jnp
import numpy as np
from jax import lax

D = 1024
HEADS = 16
HEAD_DIM = 64
MHEADS = 4
SUBKEYS = 256
HALF = 128
RANK = 16
ADAPTERS = 8
PICKS = 32
DOCS = 8
MEM_BLK = 128
SEQ_LEN = 256
SEQS = 8
TOKENS = 2048
OWNERS = 32
ROWS = 65536
ROWS_DEV = 2048
CAP = 256


def draw_adapter_ids(key, part):
    order = jax.random.permutation(jax.random.fold_in(key, 21), SEQS)
    return (order % ADAPTERS).astype(jnp.int32)


def draw_pick_ids(key, part):
    order = jax.random.permutation(jax.random.fold_in(key, 11), OWNERS)
    crowded = (order < OWNERS // 4).astype(jnp.int32)
    slot_total = OWNERS * CAP
    per_block = MEM_BLK * PICKS
    block_total = SEQS * (SEQ_LEN // MEM_BLK) * MHEADS

    def one_block(block_key):
        noise_key, order_key, row_key = jax.random.split(block_key, 3)
        noise = jax.random.randint(noise_key, (OWNERS, CAP), 0, 1024)
        ranked = (noise + 2048 * crowded[:, None]).reshape(slot_total) * slot_total + jnp.arange(slot_total, dtype=jnp.int32)
        chosen = lax.top_k(ranked, per_block)[1]
        owner_id = chosen // CAP
        owner_id = owner_id[jax.random.permutation(order_key, per_block)]
        local_row = jax.random.randint(row_key, (per_block,), 0, ROWS_DEV)
        return (owner_id * ROWS_DEV + local_row).astype(jnp.int32)
    block_keys = jax.random.split(jax.random.fold_in(key, 12), block_total)
    blocks = jax.vmap(one_block)(block_keys)
    blocks = blocks.reshape(SEQS, SEQ_LEN // MEM_BLK, MHEADS, MEM_BLK, PICKS)
    return jnp.transpose(blocks, (0, 1, 3, 2, 4)).reshape(TOKENS, MHEADS, PICKS).astype(jnp.int32)


def levels(rng, shape, cuts, low, top_value):
    def one(dim, shards_of):
        draws = jax.random.uniform(jax.random.fold_in(jax.random.fold_in(rng, 6), dim), (shards_of,), jnp.float32, low / len(cuts), top_value / len(cuts))
        return jnp.repeat(jnp.exp(draws), shape[dim] // shards_of).reshape((-1,) + (1,) * (len(shape) - dim - 1))

    gain = one(*cuts[0])
    for cut in cuts[1:]:
        gain = gain * one(*cut)
    return gain


def length_profile(number_of, total, limit, skew):
    portions = [(1 << 20) // math.isqrt(grade ** skew) + 1 for grade in range(2, number_of + 1)]
    surplus, counts = total - limit - (number_of - 1), [1] * (number_of - 1)
    while surplus > 0:
        candidates = [i for i in range(number_of - 1) if counts[i] < limit]
        mass, remaining = sum([portions[i] for i in candidates]), surplus
        for i in candidates:
            more = min(limit - counts[i], max(1, remaining * portions[i] // mass), surplus)
            counts[i] = counts[i] + more
            surplus = surplus - more
    return np.array([limit] + counts)


def uneven_parts(rng, number_of, total, bound, slope):
    if number_of == 2:
        one = jax.random.randint(rng, (), max(1, total - bound), min(bound, total - 1) + 1)
        return jnp.stack([one, total - one])
    lengths = jnp.asarray(length_profile(number_of, total, bound, slope), jnp.int32)
    twos = (number_of - 1) // 2
    source_of, receiver = lengths[1:1 + 2 * twos:2], lengths[2:2 + 2 * twos:2]
    slack = jnp.minimum(source_of - 1, bound - receiver)
    passed = jax.random.randint(jax.random.fold_in(rng, 1), (twos,), 0, 1 << 20) % (slack + 1)
    lengths = lengths.at[1:1 + 2 * twos:2].set(source_of - passed).at[2:2 + 2 * twos:2].set(receiver + passed)
    return lengths[jax.random.permutation(jax.random.fold_in(rng, 2), number_of)]


def centred(key, dims, scale, bound, cuts=(), kind=jnp.bfloat16):
    entries = jax.random.normal(key, dims, jnp.float32) * scale
    if len(cuts) > 0:
        entries = levels(key, dims, cuts, -0.22, 0.18) * entries
    return jnp.clip(entries, min=-bound, max=bound).astype(kind)


def setup_inputs(seed: int = 0) -> dict:
    seeds = jax.random.split(jax.random.key(seed), 15)
    block_in = centred(seeds[0], (TOKENS, D), 1.0, 6.0, ((0, 8),))
    cotangent = centred(seeds[1], (TOKENS, D), 1.0, 6.0, ((0, 8),))
    norm_gains = jnp.clip(1.0 + 0.18 * jax.random.normal(seeds[2], (2, D), jnp.float32), 0.1, 1.9)
    col_weights = centred(seeds[3], (5, D, D), D ** -0.5, 0.1875, ((2, 4),))
    row_weights = centred(seeds[4], (2, D, D), (D // 16) ** -0.5, 0.75, ((1, 4),))
    mem_keys = centred(seeds[5], (2, MHEADS, SUBKEYS, HALF), (16 * HALF) ** -0.5, 0.125, ((1, 4),))
    value_table = centred(seeds[6], (ROWS, D), 1.0, 6.0, ((0, 32),))
    col_down = centred(seeds[7], (5, ADAPTERS, RANK, D), D ** -0.5, 0.1875)
    col_up = centred(seeds[8], (5, ADAPTERS, RANK, D), RANK ** -0.5, 1.5, ((3, 4),))
    row_down = centred(seeds[9], (2, ADAPTERS, RANK, D), (D // 16) ** -0.5, 0.75, ((3, 4),))
    row_up = centred(seeds[10], (2, ADAPTERS, RANK, D), RANK ** -0.5, 1.5)
    segment_ids = jax.vmap(lambda own: jnp.searchsorted(jnp.cumsum(uneven_parts(own, DOCS, SEQ_LEN, SEQ_LEN // 2, 2)), jnp.arange(SEQ_LEN), side="right"))(jax.random.split(seeds[11], SEQS)).reshape((SEQS, SEQ_LEN)).astype(jnp.int32)
    adapter_ids = draw_adapter_ids(jax.random.fold_in(seeds[14], 71), 0)
    pick_ids = draw_pick_ids(jax.random.fold_in(seeds[14], 71), 0)
    return dict(block_in=block_in, cotangent=cotangent, norm_gains=norm_gains, col_weights=col_weights, row_weights=row_weights, mem_keys=mem_keys, value_table=value_table, col_down=col_down, col_up=col_up, row_down=row_down, row_up=row_up, segment_ids=segment_ids, adapter_ids=adapter_ids, pick_ids=pick_ids)


EPSILON = 1e-05
ADAPT_SCALE = 0.5
HIGHEST = lax.Precision.HIGHEST

@jax.custom_vjp
def low(v):
    return lax.optimization_barrier(v.astype(jnp.bfloat16)).astype(jnp.float32)

@jax.custom_vjp
def low_back(v):
    return v

def low_keep(v):
    return (low(v), None)

def low_pass(kept, grad):
    return (grad,)

def back_keep(v):
    return (v, None)

def back_low(kept, grad):
    return (low(grad),)
low.defvjp(low_keep, low_pass)
low_back.defvjp(back_keep, back_low)

def matmul(left, right):
    return jnp.dot(left, right, precision=HIGHEST, preferred_element_type=jnp.float32)

def rms_scale(values):
    return lax.rsqrt(lax.optimization_barrier(jnp.mean(values * values, axis=-1, keepdims=True)) + EPSILON)

def block_forward(inputs, table, col_down, col_up, row_down, row_up, gains, col_weights, row_weights, mem_keys, segments, adapter, pick_seq):
    down_col = lax.dynamic_index_in_dim(col_down, adapter, 1, keepdims=False)
    up_col = lax.dynamic_index_in_dim(col_up, adapter, 1, keepdims=False)
    down_row = lax.dynamic_index_in_dim(row_down, adapter, 1, keepdims=False)
    up_row = lax.dynamic_index_in_dim(row_up, adapter, 1, keepdims=False)
    length = inputs.shape[0]

    def project(normed, index):
        low_rank = low(low_back(matmul(normed, down_col[index].T)))
        return matmul(normed, col_weights[index]) + ADAPT_SCALE * matmul(low_rank, up_col[index])
    scale_one = rms_scale(inputs)
    normed_one = low(inputs * scale_one * gains[0])
    queries = low(low_back(project(normed_one, 0))).reshape(length, HEADS, HEAD_DIM)
    keys_all = low(low_back(project(normed_one, 1))).reshape(length, HEADS, HEAD_DIM)
    values_all = low(low_back(project(normed_one, 2))).reshape(length, HEADS, HEAD_DIM)
    logits = low_back(jnp.einsum('thd,shd->hts', queries, keys_all, precision=HIGHEST) * 0.125)
    positions = jnp.arange(length, dtype=jnp.int32)
    allowed = (segments[:, None] == segments[None, :]) & (positions[None, :] <= positions[:, None])
    logits = jnp.where(allowed[None], logits, -1e+30)
    probs = low(jax.nn.softmax(logits, axis=-1))
    mixed = jnp.einsum('hts,shd->thd', probs, values_all, precision=HIGHEST).reshape(length, D)
    att_out = low(low_back(mixed))
    low_out = low(low_back(matmul(att_out, down_row[0].T)))
    resid = inputs + low_back(matmul(att_out, row_weights[0]) + ADAPT_SCALE * matmul(low_out, up_row[0]))
    scale_two = rms_scale(resid)
    normed_two = low(resid * scale_two * gains[1])
    mem_query = low(low_back(project(normed_two, 3))).reshape(length, MHEADS, 2 * HALF)
    first_sub = low_back(jnp.einsum('tmh,mkh->tmk', mem_query[:, :, :HALF], mem_keys[0], precision=HIGHEST))
    second_sub = low_back(jnp.einsum('tmh,mkh->tmk', mem_query[:, :, HALF:], mem_keys[1], precision=HIGHEST))
    first_idx = (pick_seq // SUBKEYS).astype(jnp.int32)
    second_idx = (pick_seq % SUBKEYS).astype(jnp.int32)
    scores = jnp.take_along_axis(first_sub, first_idx, axis=2) + jnp.take_along_axis(second_sub, second_idx, axis=2)
    weights = low(jax.nn.softmax(scores, axis=-1))

    def lookup(pair):
        weight_blk, pick_blk = pair
        return jnp.einsum('tmp,tmpd->td', weight_blk, table[pick_blk], precision=HIGHEST)
    num_blocks = length // MEM_BLK
    memory = lax.map(jax.checkpoint(lookup), (weights.reshape(num_blocks, MEM_BLK, MHEADS, PICKS), pick_seq.reshape(num_blocks, MEM_BLK, MHEADS, PICKS)))
    memory = low_back(memory.reshape(length, D))
    gate_pre = low_back(project(normed_two, 4))
    gated = low(memory * jax.nn.silu(gate_pre))
    low_branch = low(low_back(matmul(gated, down_row[1].T)))
    return resid + low_back(matmul(gated, row_weights[1]) + ADAPT_SCALE * matmul(low_branch, up_row[1]))

def reference(block_in, cotangent, norm_gains, col_weights, row_weights, mem_keys, value_table, col_down, col_up, row_down, row_up, segment_ids, adapter_ids, pick_ids):
    gains = norm_gains.astype(jnp.float32)
    col_float = col_weights.astype(jnp.float32)
    row_float = row_weights.astype(jnp.float32)
    keys_float = mem_keys.astype(jnp.float32)
    table = value_table.astype(jnp.float32)
    down_cols = col_down.astype(jnp.float32)
    up_cols = col_up.astype(jnp.float32)
    down_rows = row_down.astype(jnp.float32)
    up_rows = row_up.astype(jnp.float32)
    inputs_all = block_in.reshape(SEQS, SEQ_LEN, D)
    grads_all = cotangent.reshape(SEQS, SEQ_LEN, D)
    picks_all = pick_ids.reshape(SEQS, SEQ_LEN, MHEADS, PICKS)

    def step(carry, item):
        seq_in, seq_grad, segments, adapter, pick_seq = item

        def forward(inputs, table_arg, down_c, up_c, down_r, up_r):
            return block_forward(inputs, table_arg, down_c, up_c, down_r, up_r, gains, col_float, row_float, keys_float, segments, adapter, pick_seq)
        outputs, pullback = jax.vjp(forward, seq_in.astype(jnp.float32), table, down_cols, up_cols, down_rows, up_rows)
        grads = pullback(seq_grad.astype(jnp.float32))
        carry = tuple((total + part for total, part in zip(carry, grads[1:])))
        return (carry, (outputs.astype(jnp.bfloat16), grads[0]))
    start = (jnp.zeros_like(table), jnp.zeros_like(down_cols), jnp.zeros_like(up_cols), jnp.zeros_like(down_rows), jnp.zeros_like(up_rows))
    sums, (outputs, input_grads) = lax.scan(step, start, (inputs_all, grads_all, segment_ids, adapter_ids, picks_all))
    return (outputs.reshape(TOKENS, D), input_grads.reshape(TOKENS, D), sums[0], sums[1], sums[2], sums[3], sums[4])
```

```python
import functools
import jax
import jax.numpy as jnp
from jax import lax
from jax.experimental import pallas as pl
from jax.experimental.pallas import tpu as pltpu
from jax.sharding import PartitionSpec as P

HEAD_DIM = 64
LANES = 128


EPSILON = 1e-05
ADAPT_SCALE = 0.5


def matmul(left, right):
    return jnp.dot(left, right, preferred_element_type=jnp.float32)


def matmul_nt(left, right):
    return lax.dot_general(
        left, right, (((1,), (1,)), ((), ())), preferred_element_type=jnp.float32
    )


def matmul_tn(left, right):
    return lax.dot_general(
        left, right, (((0,), (0,)), ((), ())), preferred_element_type=jnp.float32
    )


def rms_scale(values):
    return lax.rsqrt(jnp.mean(values * values, axis=-1, keepdims=True) + EPSILON)


def silu_slope(gate):
    sigma = jax.nn.sigmoid(gate)
    return sigma * (1.0 + gate * (1.0 - sigma))


NT = (((1,), (1,)), ((), ()))
TN = (((0,), (0,)), ((), ()))


def split_rows(ids, base, rows):
    local = ids - base
    here = (local >= 0) & (local < rows)
    return jnp.where(here, local & (LANES - 1), 0), jnp.where(here, local >> 7, -1)


def spread_kernel(unroll, base_ref, ids_ref, w_ref, out_ref, lo_s, hi_s, w_s, tiles):
    brain = jnp.bfloat16
    tokens, rows = out_ref.shape
    high = rows // LANES
    pad = max(high, 16)
    lo, hi = split_rows(ids_ref[...], base_ref[0], rows)
    lo_s[...] = lo.astype(jnp.float32)
    hi_s[...] = hi.astype(jnp.float32)
    w_s[...] = w_ref[...].astype(jnp.float32)
    picks = ids_ref.shape[1]
    low_at = lax.broadcasted_iota(jnp.int32, (LANES, picks), 0).astype(jnp.float32).astype(brain)
    high_at = lax.broadcasted_iota(jnp.int32, (pad, picks), 0).astype(jnp.float32)
    empty = jnp.zeros((pad, picks), brain)

    def hot(t):
        lo = jnp.broadcast_to(lo_s[pl.ds(t, 1), :], (LANES, picks)).astype(brain)
        hi = jnp.broadcast_to(hi_s[pl.ds(t, 1), :], (pad, picks))
        w = jnp.broadcast_to(w_s[pl.ds(t, 1), :], (pad, picks))
        low_hot = jnp.where(lo == low_at, brain(1), brain(0))
        high_hot = jnp.where(hi == high_at, w, 0.0).astype(brain)
        return high_hot, low_hot

    def step(i, carry):
        for u in range(0, unroll, 2):
            t = i * unroll + u
            high_0, low_0 = hot(t)
            high_1, low_1 = hot(t + 1)
            left = jnp.concatenate(
                [
                    jnp.concatenate([high_0, empty], axis=1),
                    jnp.concatenate([empty, high_1], axis=1),
                ],
                axis=0,
            )
            right = jnp.concatenate([low_0, low_1], axis=1)
            tiles[pl.ds(t * pad, 2 * pad), :] = lax.dot_general(
                left, right, NT, preferred_element_type=jnp.float32
            )
        return carry

    lax.fori_loop(0, tokens // unroll, step, 0)
    for a in range(high):
        out_ref[:, a * LANES : (a + 1) * LANES] = tiles[pl.ds(a, tokens, stride=pad), :].astype(
            brain
        )


def spread(ids, weights, base, rows, block=128, unroll=32):
    tokens, picks = ids.shape
    pad = max(rows // LANES, 16)
    return pl.pallas_call(
        functools.partial(spread_kernel, unroll),
        grid=(tokens // block,),
        in_specs=[
            pl.BlockSpec(memory_space=pltpu.SMEM),
            pl.BlockSpec((block, picks), lambda i: (i, 0)),
            pl.BlockSpec((block, picks), lambda i: (i, 0)),
        ],
        out_specs=pl.BlockSpec((block, rows), lambda i: (i, 0)),
        out_shape=jax.ShapeDtypeStruct((tokens, rows), jnp.bfloat16),
        scratch_shapes=[pltpu.VMEM((block, picks), jnp.float32)] * 3
        + [pltpu.VMEM((block * pad, LANES), jnp.float32)],
        name="spread",
    )(base, ids, weights)


def answer_kernel(base_ref, grad_ref, table_ref, ids_ref, out_ref, all_s):
    rows = table_ref.shape[0]
    all_s[...] = lax.dot_general(
        grad_ref[...], table_ref[...], NT, preferred_element_type=jnp.float32
    )
    lo, hi = split_rows(ids_ref[...], base_ref[0], rows)
    total = jnp.zeros(ids_ref.shape, jnp.float32)
    for a in range(rows // LANES):
        found = jnp.take_along_axis(
            all_s[:, a * LANES : (a + 1) * LANES], lo, axis=1, mode="promise_in_bounds"
        )
        total = jnp.where(hi == a, found, total)
    out_ref[...] = total.astype(out_ref.dtype)


def answer(ids, grads, table, base, block=256):
    tokens, picks = ids.shape
    rows, width = table.shape
    return pl.pallas_call(
        answer_kernel,
        grid=(tokens // block,),
        in_specs=[
            pl.BlockSpec(memory_space=pltpu.SMEM),
            pl.BlockSpec((block, width), lambda i: (i, 0)),
            pl.BlockSpec((rows, width), lambda i: (0, 0)),
            pl.BlockSpec((block, picks), lambda i: (i, 0)),
        ],
        out_specs=pl.BlockSpec((block, picks), lambda i: (i, 0)),
        out_shape=jax.ShapeDtypeStruct((tokens, picks), jnp.float32),
        scratch_shapes=[pltpu.VMEM((block, rows), jnp.float32)],
        name="answer",
    )(base, grads, table, ids)


def pick_scores(picks, first, second, sub_count):
    columns = jnp.arange(sub_count, dtype=jnp.int32)
    hit_first = (picks // sub_count)[:, :, None] == columns
    hit_second = (picks % sub_count)[:, :, None] == columns
    scores = jnp.sum(jnp.where(hit_first, first[:, None, :], 0.0), axis=2)
    scores = scores + jnp.sum(jnp.where(hit_second, second[:, None, :], 0.0), axis=2)
    return (jax.nn.softmax(scores, axis=-1), hit_first, hit_second)


def per_device(
    block_in,
    cotangent,
    norm_gains,
    col_weights,
    row_weights,
    mem_keys,
    value_table,
    col_down,
    col_up,
    row_down,
    row_up,
    segment_ids,
    adapter_ids,
    pick_ids,
):
    floating = jnp.float32
    brain = jnp.bfloat16
    length = block_in.shape[0]
    col_width = col_weights.shape[2]
    heads_here = col_width // HEAD_DIM
    rows_here = value_table.shape[0]
    pick_tok = pick_ids[:, 0, :]
    query_rows = min(512, length)
    query_blocks = length // query_rows
    sub_count = mem_keys.shape[2]
    half_width = mem_keys.shape[3]
    adapter = adapter_ids[0]
    down_col = lax.dynamic_index_in_dim(col_down, adapter, 1, keepdims=False)
    up_col = lax.dynamic_index_in_dim(col_up, adapter, 1, keepdims=False)
    down_row = lax.dynamic_index_in_dim(row_down, adapter, 1, keepdims=False)
    up_row = lax.dynamic_index_in_dim(row_up, adapter, 1, keepdims=False)
    gain_one = norm_gains[0]
    gain_two = norm_gains[1]
    first_keys = mem_keys[0, 0]
    second_keys = mem_keys[1, 0]
    segments = segment_ids[0]
    positions = jnp.arange(length, dtype=jnp.int32)
    inputs = block_in.astype(floating)
    scale_one = rms_scale(inputs)
    normed_one = (inputs * scale_one * gain_one).astype(brain)
    low_att = jnp.einsum(
        "td,jrd->jtr", normed_one, down_col[:3], preferred_element_type=floating
    ).astype(brain)
    projected = jnp.einsum(
        "td,jde->jte", normed_one, col_weights[:3], preferred_element_type=floating
    )
    projected = projected + ADAPT_SCALE * jnp.einsum(
        "jtr,jre->jte", low_att, up_col[:3], preferred_element_type=floating
    )
    projected = projected.astype(brain)
    queries = projected[0].reshape(length, heads_here, HEAD_DIM)
    keys_here = projected[1].reshape(length, heads_here, HEAD_DIM)
    values_here = projected[2].reshape(length, heads_here, HEAD_DIM)

    def block_logits(start):
        rows_pos = start + jnp.arange(query_rows, dtype=jnp.int32)
        allowed = (segments[:, None] == segments[None, :]) & (
            positions[None, :] <= rows_pos[:, None]
        )
        logits = (
            jnp.einsum("thd,shd->hts", queries, keys_here, preferred_element_type=floating) * 0.125
        )
        return (queries, allowed, jnp.where(allowed[None], logits, -1e30))

    def attend(index):
        query_blk, allowed, logits = block_logits(index * query_rows)
        peak = jnp.max(logits, axis=-1, keepdims=True)
        expos = jnp.exp(logits - peak)
        total = jnp.sum(expos, axis=-1, keepdims=True)
        probs = expos / total
        mixed = jnp.einsum(
            "hts,shd->thd", probs.astype(brain), values_here, preferred_element_type=floating
        )
        return (
            mixed.reshape(query_rows, col_width).astype(brain),
            (peak + jnp.log(total))[:, :, 0],
        )

    att_out, log_totals = lax.map(attend, jnp.arange(query_blocks))
    att_out = att_out.reshape(length, col_width)
    att_part = matmul(att_out, row_weights[0])
    low_part = matmul_nt(att_out, down_row[0])
    att_sum, low_sum = lax.psum((att_part, low_part), "mp")
    low_out = low_sum.astype(brain)
    resid = inputs + att_sum + ADAPT_SCALE * matmul(low_out, up_row[0])
    scale_two = rms_scale(resid)
    normed_two = (resid * scale_two * gain_two).astype(brain)
    low_mem = jnp.einsum(
        "td,jrd->jtr", normed_two, down_col[3:], preferred_element_type=floating
    ).astype(brain)
    mem_query = (
        matmul(normed_two, col_weights[3]) + ADAPT_SCALE * matmul(low_mem[0], up_col[3])
    ).astype(brain)
    gate_pre = matmul(normed_two, col_weights[4]) + ADAPT_SCALE * matmul(low_mem[1], up_col[4])
    first_sub = matmul_nt(mem_query[:, :half_width], first_keys)
    second_sub = matmul_nt(mem_query[:, half_width:], second_keys)

    everyone = ("dp", "mp")
    base = (
        (lax.axis_index("dp") * lax.axis_size("mp") + lax.axis_index("mp")) * rows_here
    ).reshape(1)
    ids_all = lax.all_gather(
        lax.all_gather(pick_tok, "mp", axis=1, tiled=True), "dp", axis=0, tiled=True
    )
    weights, hit_first, hit_second = pick_scores(pick_tok, first_sub, second_sub, sub_count)
    weights_all = lax.all_gather(
        lax.all_gather(weights.astype(brain), "mp", axis=1, tiled=True), "dp", axis=0, tiled=True
    )
    gate_act = jax.nn.silu(gate_pre)
    low_branch_grad = (ADAPT_SCALE * matmul_nt(cotangent, up_row[1])).astype(brain)
    gated_grad = matmul_nt(cotangent, row_weights[1]) + matmul(low_branch_grad, down_row[1])
    mem_grad_cols = (gated_grad * gate_act).astype(brain)
    mem_grad = lax.all_gather(
        lax.all_gather(mem_grad_cols, "mp", axis=1, tiled=True), "dp", axis=0, tiled=True
    )
    spread_w = spread(ids_all, weights_all, base, rows_here)
    partial = matmul(spread_w, value_table).astype(brain)
    mem_cols = lax.psum_scatter(partial, "dp", scatter_dimension=0, tiled=True)
    mem_cols = lax.psum_scatter(mem_cols, "mp", scatter_dimension=1, tiled=True).astype(floating)
    answers = answer(ids_all, mem_grad, value_table, base)
    weight_grad = lax.psum_scatter(answers, "dp", scatter_dimension=0, tiled=True)
    weight_grad = lax.psum_scatter(weight_grad, "mp", scatter_dimension=1, tiled=True)
    table_grad = matmul_tn(spread_w, mem_grad)
    gated = (mem_cols * gate_act).astype(brain)
    branch_part = matmul(gated, row_weights[1])
    low_branch_part = matmul_nt(gated, down_row[1])
    branch_sum, low_branch_sum = (
        lax.psum(branch_part.astype(jnp.bfloat16), "mp").astype(jnp.float32),
        lax.psum(low_branch_part.astype(jnp.bfloat16), "mp").astype(jnp.float32),
    )
    low_branch = low_branch_sum.astype(brain)
    block_out = (resid + branch_sum + ADAPT_SCALE * matmul(low_branch, up_row[1])).astype(brain)
    out_grad = cotangent.astype(floating)
    grad_up_branch = ADAPT_SCALE * matmul_tn(low_branch, cotangent)
    grad_down_branch = matmul_tn(low_branch_grad, gated)
    gate_grad = (gated_grad * mem_cols * silu_slope(gate_pre)).astype(brain)
    score_grad = weights * (
        weight_grad - jnp.sum(weights * weight_grad, axis=-1, keepdims=True)
    )
    first_grad = jnp.sum(jnp.where(hit_first, score_grad[:, :, None], 0.0), axis=1).astype(brain)
    second_grad = jnp.sum(jnp.where(hit_second, score_grad[:, :, None], 0.0), axis=1).astype(brain)
    query_grad = jnp.concatenate(
        [matmul(first_grad, first_keys), matmul(second_grad, second_keys)], axis=1
    ).astype(brain)
    normed_two_part = matmul_nt(query_grad, col_weights[3]) + matmul_nt(gate_grad, col_weights[4])
    low_mem_part = ADAPT_SCALE * jnp.stack(
        [matmul_nt(query_grad, up_col[3]), matmul_nt(gate_grad, up_col[4])]
    )
    grad_up_mem = ADAPT_SCALE * jnp.stack(
        [matmul_tn(low_mem[0], query_grad), matmul_tn(low_mem[1], gate_grad)]
    )
    normed_two_grad, low_mem_grad = lax.psum((normed_two_part, low_mem_part), "mp")
    low_mem_grad = low_mem_grad.astype(brain)
    normed_two_grad = normed_two_grad + jnp.einsum(
        "jtr,jrd->td", low_mem_grad, down_col[3:], preferred_element_type=floating
    )
    grad_down_mem = jnp.einsum(
        "jtr,td->jrd", low_mem_grad, normed_two, preferred_element_type=floating
    )
    weighted_two = gain_two * normed_two_grad
    resid_grad = (
        out_grad
        + scale_two * weighted_two
        - resid * scale_two**3 * jnp.mean(resid * weighted_two, axis=-1, keepdims=True)
    )
    att_branch_grad = resid_grad.astype(brain)
    low_out_grad = (ADAPT_SCALE * matmul_nt(att_branch_grad, up_row[0])).astype(brain)
    grad_up_att = ADAPT_SCALE * matmul_tn(low_out, att_branch_grad)
    att_out_grad = (
        matmul_nt(att_branch_grad, row_weights[0]) + matmul(low_out_grad, down_row[0])
    ).astype(brain)
    grad_down_att = matmul_tn(low_out_grad, att_out)

    def attend_back(carry, index):
        key_acc, value_acc = carry
        start = index * query_rows
        query_blk, allowed, logits = block_logits(start)
        grad_blk = att_out_grad.reshape(query_rows, heads_here, HEAD_DIM)
        probs = jnp.where(allowed[None], jnp.exp(logits - log_totals[index][:, :, None]), 0.0)
        value_acc = value_acc + jnp.einsum(
            "hts,thd->shd", probs.astype(brain), grad_blk, preferred_element_type=floating
        )
        prob_grad = jnp.einsum(
            "thd,shd->hts", grad_blk, values_here, preferred_element_type=floating
        )
        logit_grad = (
            probs * (prob_grad - jnp.sum(probs * prob_grad, axis=-1, keepdims=True))
        ).astype(brain)
        query_part = 0.125 * jnp.einsum(
            "hts,shd->thd", logit_grad, keys_here, preferred_element_type=floating
        )
        key_acc = key_acc + 0.125 * jnp.einsum(
            "hts,thd->shd", logit_grad, query_blk, preferred_element_type=floating
        )
        return ((key_acc, value_acc), query_part.reshape(query_rows, col_width).astype(brain))

    empty = jnp.zeros((length, heads_here, HEAD_DIM), floating)
    (key_grad, value_grad), query_parts = lax.scan(
        attend_back, (empty, empty), jnp.arange(query_blocks)
    )
    proj_grad = jnp.stack(
        [
            query_parts.reshape(length, col_width),
            key_grad.reshape(length, col_width).astype(brain),
            value_grad.reshape(length, col_width).astype(brain),
        ]
    )
    normed_one_part = jnp.einsum(
        "jte,jde->td", proj_grad, col_weights[:3], preferred_element_type=floating
    )
    low_att_part = ADAPT_SCALE * jnp.einsum(
        "jte,jre->jtr", proj_grad, up_col[:3], preferred_element_type=floating
    )
    grad_up_qkv = ADAPT_SCALE * jnp.einsum(
        "jtr,jte->jre", low_att, proj_grad, preferred_element_type=floating
    )
    normed_one_grad, low_att_grad = (
        lax.psum(normed_one_part.astype(jnp.bfloat16), "mp").astype(jnp.float32),
        lax.psum(low_att_part.astype(jnp.bfloat16), "mp").astype(jnp.float32),
    )
    low_att_grad = low_att_grad.astype(brain)
    normed_one_grad = normed_one_grad + jnp.einsum(
        "jtr,jrd->td", low_att_grad, down_col[:3], preferred_element_type=floating
    )
    grad_down_qkv = jnp.einsum(
        "jtr,td->jrd", low_att_grad, normed_one, preferred_element_type=floating
    )
    weighted_one = gain_one * normed_one_grad
    input_grad = (
        resid_grad
        + scale_one * weighted_one
        - inputs * scale_one**3 * jnp.mean(inputs * weighted_one, axis=-1, keepdims=True)
    )
    chosen = (jnp.arange(col_down.shape[1], dtype=jnp.int32) == adapter).astype(floating)
    down_cols_all = (
        jnp.concatenate([grad_down_qkv, grad_down_mem], axis=0)[:, None]
        * chosen[None, :, None, None]
    )
    up_cols_all = (
        jnp.concatenate([grad_up_qkv, grad_up_mem], axis=0)[:, None] * chosen[None, :, None, None]
    )
    down_rows_all = (
        jnp.stack([grad_down_att, grad_down_branch])[:, None] * chosen[None, :, None, None]
    )
    up_rows_all = jnp.stack([grad_up_att, grad_up_branch])[:, None] * chosen[None, :, None, None]
    down_cols_sum, up_cols_sum, down_rows_sum, up_rows_sum = (
        lax.psum(down_cols_all.astype(jnp.bfloat16), "dp").astype(jnp.float32),
        lax.psum(up_cols_all.astype(jnp.bfloat16), "dp").astype(jnp.float32),
        lax.psum(down_rows_all.astype(jnp.bfloat16), "dp").astype(jnp.float32),
        lax.psum(up_rows_all.astype(jnp.bfloat16), "dp").astype(jnp.float32),
    )
    return (
        block_out,
        input_grad,
        table_grad,
        down_cols_sum,
        up_cols_sum,
        down_rows_sum,
        up_rows_sum,
    )


def solution(mesh):
    in_specs = (
        P("dp", None),
        P("dp", None),
        P(),
        P(None, None, "mp"),
        P(None, "mp", None),
        P(None, "mp", None, None),
        P(("dp", "mp"), None),
        P(),
        P(None, None, None, "mp"),
        P(None, None, None, "mp"),
        P(),
        P("dp", None),
        P("dp"),
        P("dp", "mp", None),
    )
    out_specs = (
        P("dp", None),
        P("dp", None),
        P(("dp", "mp"), None),
        P(),
        P(None, None, None, "mp"),
        P(None, None, None, "mp"),
        P(),
    )
    return jax.shard_map(
        per_device, mesh=mesh, in_specs=in_specs, out_specs=out_specs, check_vma=False
    )
```

```python
import functools
import jax
import jax.numpy as jnp
from jax import lax
from jax.experimental import pallas as pl
from jax.experimental.pallas import tpu as pltpu
from jax.sharding import PartitionSpec as P

HEAD_DIM = 64
LANES = 128


EPSILON = 1e-05
ADAPT_SCALE = 0.5


def matmul(left, right):
    return jnp.dot(left, right, preferred_element_type=jnp.float32)


def matmul_nt(left, right):
    return lax.dot_general(
        left, right, (((1,), (1,)), ((), ())), preferred_element_type=jnp.float32
    )


def matmul_tn(left, right):
    return lax.dot_general(
        left, right, (((0,), (0,)), ((), ())), preferred_element_type=jnp.float32
    )


def rms_scale(values):
    return lax.rsqrt(jnp.mean(values * values, axis=-1, keepdims=True) + EPSILON)


def silu_slope(gate):
    sigma = jax.nn.sigmoid(gate)
    return sigma * (1.0 + gate * (1.0 - sigma))


NT = (((1,), (1,)), ((), ()))
TN = (((0,), (0,)), ((), ()))


def split_rows(ids, base, rows):
    local = ids - base
    here = (local >= 0) & (local < rows)
    return jnp.where(here, local & (LANES - 1), 0), jnp.where(here, local >> 7, -1)


def spread_kernel(unroll, base_ref, ids_ref, w_ref, out_ref, lo_s, hi_s, w_s, tiles):
    brain = jnp.bfloat16
    tokens, rows = out_ref.shape
    high = rows // LANES
    pad = max(high, 16)
    lo, hi = split_rows(ids_ref[...], base_ref[0], rows)
    lo_s[...] = lo.astype(jnp.float32)
    hi_s[...] = hi.astype(jnp.float32)
    w_s[...] = w_ref[...].astype(jnp.float32)
    picks = ids_ref.shape[1]
    low_at = lax.broadcasted_iota(jnp.int32, (LANES, picks), 0).astype(jnp.float32).astype(brain)
    high_at = lax.broadcasted_iota(jnp.int32, (pad, picks), 0).astype(jnp.float32)
    empty = jnp.zeros((pad, picks), brain)

    def hot(t):
        lo = jnp.broadcast_to(lo_s[pl.ds(t, 1), :], (LANES, picks)).astype(brain)
        hi = jnp.broadcast_to(hi_s[pl.ds(t, 1), :], (pad, picks))
        w = jnp.broadcast_to(w_s[pl.ds(t, 1), :], (pad, picks))
        low_hot = jnp.where(lo == low_at, brain(1), brain(0))
        high_hot = jnp.where(hi == high_at, w, 0.0).astype(brain)
        return high_hot, low_hot

    def step(i, carry):
        for u in range(0, unroll, 2):
            t = i * unroll + u
            high_0, low_0 = hot(t)
            high_1, low_1 = hot(t + 1)
            left = jnp.concatenate(
                [
                    jnp.concatenate([high_0, empty], axis=1),
                    jnp.concatenate([empty, high_1], axis=1),
                ],
                axis=0,
            )
            right = jnp.concatenate([low_0, low_1], axis=1)
            tiles[pl.ds(t * pad, 2 * pad), :] = lax.dot_general(
                left, right, NT, preferred_element_type=jnp.float32
            )
        return carry

    lax.fori_loop(0, tokens // unroll, step, 0)
    for a in range(high):
        out_ref[:, a * LANES : (a + 1) * LANES] = tiles[pl.ds(a, tokens, stride=pad), :].astype(
            brain
        )


def spread(ids, weights, base, rows, block=128, unroll=32):
    tokens, picks = ids.shape
    pad = max(rows // LANES, 16)
    return pl.pallas_call(
        functools.partial(spread_kernel, unroll),
        grid=(tokens // block,),
        in_specs=[
            pl.BlockSpec(memory_space=pltpu.SMEM),
            pl.BlockSpec((block, picks), lambda i: (i, 0)),
            pl.BlockSpec((block, picks), lambda i: (i, 0)),
        ],
        out_specs=pl.BlockSpec((block, rows), lambda i: (i, 0)),
        out_shape=jax.ShapeDtypeStruct((tokens, rows), jnp.bfloat16),
        scratch_shapes=[pltpu.VMEM((block, picks), jnp.float32)] * 3
        + [pltpu.VMEM((block * pad, LANES), jnp.float32)],
        name="spread",
    )(base, ids, weights)


def answer_kernel(base_ref, grad_ref, table_ref, ids_ref, out_ref, all_s):
    rows = table_ref.shape[0]
    all_s[...] = lax.dot_general(
        grad_ref[...], table_ref[...], NT, preferred_element_type=jnp.float32
    )
    lo, hi = split_rows(ids_ref[...], base_ref[0], rows)
    total = jnp.zeros(ids_ref.shape, jnp.float32)
    for a in range(rows // LANES):
        found = jnp.take_along_axis(
            all_s[:, a * LANES : (a + 1) * LANES], lo, axis=1, mode="promise_in_bounds"
        )
        total = jnp.where(hi == a, found, total)
    out_ref[...] = total.astype(out_ref.dtype)


def answer(ids, grads, table, base, block=256):
    tokens, picks = ids.shape
    rows, width = table.shape
    return pl.pallas_call(
        answer_kernel,
        grid=(tokens // block,),
        in_specs=[
            pl.BlockSpec(memory_space=pltpu.SMEM),
            pl.BlockSpec((block, width), lambda i: (i, 0)),
            pl.BlockSpec((rows, width), lambda i: (0, 0)),
            pl.BlockSpec((block, picks), lambda i: (i, 0)),
        ],
        out_specs=pl.BlockSpec((block, picks), lambda i: (i, 0)),
        out_shape=jax.ShapeDtypeStruct((tokens, picks), jnp.float32),
        scratch_shapes=[pltpu.VMEM((block, rows), jnp.float32)],
        name="answer",
    )(base, grads, table, ids)


MESH = pl.DeviceIdType.MESH


def partner(index, bit):
    return index + bit - 2 * bit * ((index // bit) % 2)


def remote(src, dst, sems, slot, device):
    return pltpu.make_async_remote_copy(
        src_ref=src,
        dst_ref=dst,
        send_sem=sems.at[0, slot],
        recv_sem=sems.at[1, slot],
        device_id=device,
        device_id_type=MESH,
    )


def greet(devices):
    barrier = pltpu.get_barrier_semaphore()
    for device in devices:
        pl.semaphore_signal(barrier, inc=1, device_id=device, device_id_type=MESH)
    pl.semaphore_wait(barrier, len(devices))


def hot_rows(lo_s, hi_s, w_s, tiles, tokens, pad):
    brain = jnp.bfloat16
    picks = lo_s.shape[1]
    low_at = lax.broadcasted_iota(jnp.int32, (LANES, picks), 0).astype(jnp.float32).astype(brain)
    high_at = lax.broadcasted_iota(jnp.int32, (pad, picks), 0).astype(jnp.float32)
    empty = jnp.zeros((pad, picks), brain)

    def hot(t):
        lo = jnp.broadcast_to(lo_s[t : t + 1, :], (LANES, picks)).astype(brain)
        hi = jnp.broadcast_to(hi_s[t : t + 1, :], (pad, picks))
        w = jnp.broadcast_to(w_s[t : t + 1, :], (pad, picks))
        low_hot = jnp.where(lo == low_at, brain(1), brain(0))
        high_hot = jnp.where(hi == high_at, w, 0.0).astype(brain)
        return high_hot, low_hot

    for t in range(0, tokens, 2):
        high_0, low_0 = hot(t)
        high_1, low_1 = hot(t + 1)
        left = jnp.concatenate(
            [
                jnp.concatenate([high_0, empty], axis=1),
                jnp.concatenate([empty, high_1], axis=1),
            ],
            axis=0,
        )
        right = jnp.concatenate([low_0, low_1], axis=1)
        tiles[t * pad : (t + 2) * pad, :] = lax.dot_general(
            left, right, NT, preferred_element_type=jnp.float32
        )


def memory_kernel(
    seqs,
    parts,
    table_hbm,
    ids_hbm,
    weights_ref,
    grads_ref,
    memory_ref,
    answers_ref,
    table_grad_hbm,
    table_v,
    ids_v,
    w_all,
    g_all,
    spread_v,
    tiles,
    lo_s,
    hi_s,
    w_s,
    part_own,
    part_sib,
    got_core,
    got_x,
    got_y,
    got_z,
    ans_own,
    ans_sib,
    ans_core,
    ans_plane,
    ans_z,
    all_s,
    tg_v,
    local_sems,
    sems_w,
    sems_g,
    sems_m,
    sems_a,
):
    floating, brain = jnp.float32, jnp.bfloat16
    d = lax.axis_index("dp")
    m = lax.axis_index("mp")
    rows, width = table_v.shape
    picks_here, length = weights_ref.shape
    picks = picks_here * parts
    cols = width // parts
    half = length // 2
    core = partner(d, 1)
    x_side = partner(d, 2)
    y_side = partner(d, 4)
    corner = partner(x_side, 4)
    mine, chip_x, chip_y, chip_d = d // 2, x_side // 2, y_side // 2, corner // 2
    z_of = [lax.rem(m + k, parts) for k in range(parts)]
    table_in = pltpu.make_async_copy(table_hbm, table_v, local_sems.at[0])
    ids_in = pltpu.make_async_copy(ids_hbm, ids_v, local_sems.at[1])
    ids_in.start()
    table_in.start()
    at = lambda place: {"dp": place, "mp": m}
    deep = lambda k: {"dp": d, "mp": z_of[k]}
    greet(
        [deep(k) for k in range(1, parts)]
        + [at(x_side), at(y_side), at(corner), at(core)]
    )
    pick_rows = pl.ds(pl.multiple_of(m * picks_here, 16), picks_here)
    my_cols = pl.ds(pl.multiple_of(m * cols, LANES), cols)
    seq_rows = lambda s: pl.ds(pl.multiple_of(s * length, 16), length)
    w_all[d, pick_rows, :] = weights_ref[...]
    g_all[seq_rows(d), my_cols] = grads_ref[...]
    w_z = [
        remote(weights_ref, w_all.at[d, pick_rows, :], sems_w, k, deep(k)) for k in range(1, parts)
    ]
    g_z = [
        remote(grads_ref, g_all.at[seq_rows(d), my_cols], sems_g, k, deep(k))
        for k in range(1, parts)
    ]
    for c in w_z:
        c.start()
    for c in g_z:
        c.start()
    for c in w_z:
        c.wait_recv()
    w_plane = [
        remote(w_all.at[d], w_all.at[d], sems_w, 4 + i, at(p))
        for i, p in enumerate((x_side, y_side, corner, core))
    ]
    for c in w_plane:
        c.start()
    for c in w_plane[:3]:
        c.wait_recv()
    w_core = [
        remote(w_all.at[p], w_all.at[p], sems_w, 8 + i, at(core))
        for i, p in enumerate((x_side, y_side, corner))
    ]
    for c in w_core:
        c.start()
    w_plane[3].wait_recv()
    for c in w_core:
        c.wait_recv()
    ids_in.wait()

    block = lo_s.shape[0]
    base = (d * parts + m) * rows
    pad = tiles.shape[0] // block

    def build(i, carry):
        here = pl.ds(pl.multiple_of(i * block, block), block)
        lo, hi = split_rows(ids_v[here, :], base, rows)
        lo_s[...] = lo.astype(floating)
        hi_s[...] = hi.astype(floating)
        per_seq = length // block
        w_t = w_all[i // per_seq, :, pl.ds(pl.multiple_of((i % per_seq) * block, block), block)]
        w_s[...] = jnp.transpose(w_t.astype(floating))
        hot_rows(lo_s, hi_s, w_s, tiles, block, pad)
        for a in range(rows // LANES):
            spread_v[here, a * LANES : (a + 1) * LANES] = tiles[
                pl.ds(a, block, stride=pad), :
            ].astype(brain)
        return carry

    blocks = seqs * length // block
    cuts = [0, blocks // 8, (9 * blocks) // 16, (13 * blocks) // 16, blocks]
    lax.fori_loop(cuts[0], cuts[1], build, 0)
    for c in g_z:
        c.wait_recv()
    whole = lambda s: g_all.at[seq_rows(s)]
    part = lambda s, h: g_all.at[pl.ds(pl.multiple_of(s * length + h * half, 16), half)]
    g_one = [
        remote(whole(d), whole(d), sems_g, 4 + i, at(p)) for i, p in enumerate((x_side, y_side, core))
    ]
    for c in g_one:
        c.start()
    lax.fori_loop(cuts[1], cuts[2], build, 0)
    g_one[0].wait_recv()
    g_one[1].wait_recv()
    g_two = [
        remote(part(y_side, 0), part(y_side, 0), sems_g, 7, at(x_side)),
        remote(part(x_side, 1), part(x_side, 1), sems_g, 8, at(y_side)),
        remote(whole(x_side), whole(x_side), sems_g, 9, at(core)),
        remote(whole(y_side), whole(y_side), sems_g, 10, at(core)),
    ]
    for c in g_two:
        c.start()
    lax.fori_loop(cuts[2], cuts[3], build, 0)
    g_two[0].wait_recv()
    g_two[1].wait_recv()
    g_three = remote(whole(corner), whole(corner), sems_g, 11, at(core))
    g_three.start()
    lax.fori_loop(cuts[3], cuts[4], build, 0)

    table_in.wait()
    sib_core = core % 2

    def partial_of(seq):
        return jnp.dot(
            spread_v[seq_rows(seq), :], table_v[...], preferred_element_type=floating
        ).astype(brain)

    to_core = [
        remote(part_sib.at[c], got_core.at[c], sems_m, c, at(core)) for c in range(seqs // 2)
    ]
    for c in range(seqs // 2):
        part_sib[c] = partial_of(2 * c + sib_core)
        to_core[c].start()

    def own_part(c, carry):
        part_own[c] = partial_of(2 * c + d % 2)
        return carry

    lax.fori_loop(0, seqs // 2, own_part, 0)
    for c in to_core:
        c.wait_recv()

    def fold(c, carry):
        part_own[c] = (part_own[c].astype(floating) + got_core[c].astype(floating)).astype(brain)
        return carry

    lax.fori_loop(0, seqs // 2, fold, 0)
    upper, lower = pl.ds(0, half), pl.ds(half, half)
    m_one = [
        remote(part_own.at[chip_d, upper], got_x.at[0], sems_m, 4, at(x_side)),
        remote(part_own.at[chip_d, lower], got_y.at[0], sems_m, 5, at(y_side)),
        remote(part_own.at[chip_x, upper], got_x.at[1], sems_m, 6, at(x_side)),
        remote(part_own.at[chip_y, lower], got_y.at[1], sems_m, 7, at(y_side)),
    ]
    for c in m_one:
        c.start()

    for c in g_two[2:]:
        c.wait_recv()
    g_one[2].wait_recv()
    g_three.wait_recv()

    def answers_of(seq):
        all_s[...] = lax.dot_general(
            g_all[seq_rows(seq), :], table_v[...], NT, preferred_element_type=floating
        )
        lo, hi = split_rows(ids_v[seq_rows(seq), :], base, rows)
        total = jnp.zeros((length, picks), floating)
        for a in range(rows // LANES):
            found = jnp.take_along_axis(
                all_s[:, a * LANES : (a + 1) * LANES], lo, axis=1, mode="promise_in_bounds"
            )
            total = jnp.where(hi == a, found, total)
        return jnp.transpose(total).astype(brain)

    def sib_answers(c, carry):
        ans_sib[c] = answers_of(2 * c + sib_core)
        return carry

    def own_answers(c, carry):
        ans_own[c] = answers_of(2 * c + d % 2)
        return carry

    lax.fori_loop(0, seqs // 2, sib_answers, 0)
    a_core = remote(ans_sib, ans_core, sems_a, 0, at(core))
    a_core.start()
    m_one[0].wait_recv()
    m_one[1].wait_recv()
    part_own[chip_y, upper] = (
        part_own[chip_y, upper].astype(floating) + got_x[0].astype(floating)
    ).astype(brain)
    part_own[chip_x, lower] = (
        part_own[chip_x, lower].astype(floating) + got_y[0].astype(floating)
    ).astype(brain)
    m_two = [
        remote(part_own.at[chip_x, lower], got_x.at[2], sems_m, 8, at(x_side)),
        remote(part_own.at[chip_y, upper], got_y.at[2], sems_m, 9, at(y_side)),
    ]
    for c in m_two:
        c.start()
    lax.fori_loop(0, seqs // 2, own_answers, 0)
    a_core.wait_recv()
    ans_own[...] = (ans_own[...].astype(floating) + ans_core[...].astype(floating)).astype(brain)
    a_plane = [
        remote(ans_own.at[chip], ans_plane.at[i], sems_a, 1 + i, at(p))
        for i, (chip, p) in enumerate(((chip_x, x_side), (chip_y, y_side), (chip_d, corner)))
    ]
    for c in m_one[2:]:
        c.wait_recv()
    for c in m_two:
        c.wait_recv()
    part_own[mine, upper] = (
        part_own[mine, upper].astype(floating)
        + got_x[1].astype(floating)
        + got_y[2].astype(floating)
    ).astype(brain)
    part_own[mine, lower] = (
        part_own[mine, lower].astype(floating)
        + got_x[2].astype(floating)
        + got_y[1].astype(floating)
    ).astype(brain)
    cols_of = lambda k: pl.ds(pl.multiple_of(z_of[k] * cols, LANES), cols)
    m_z = [
        remote(part_own.at[mine, :, cols_of(k)], got_z.at[k - 1], sems_m, 9 + k, deep(k))
        for k in range(1, parts)
    ]
    for c in a_plane:
        c.start()
    for c in m_z:
        c.start()

    tg_block = tg_v.shape[1]

    def tg_out(i):
        return pltpu.make_async_copy(
            tg_v.at[i % 2],
            table_grad_hbm.at[pl.ds(pl.multiple_of(i * tg_block, tg_block), tg_block)],
            local_sems.at[2 + i % 2],
        )

    def tg_step(i):
        tg_v[i % 2] = lax.dot_general(
            spread_v[:, i * tg_block : (i + 1) * tg_block],
            g_all[...],
            TN,
            preferred_element_type=floating,
        )

    steps = rows // tg_block
    for i in range(steps):
        if i >= 2:
            tg_out(i - 2).wait()
        tg_step(i)
        tg_out(i).start()
        if i == steps // 4:
            for c in a_plane:
                c.wait_recv()
            ans_own[mine] = (
                ans_own[mine].astype(floating)
                + ans_plane[0].astype(floating)
                + ans_plane[1].astype(floating)
                + ans_plane[2].astype(floating)
            ).astype(brain)
            a_z = [
                remote(
                    ans_own.at[mine, pl.ds(pl.multiple_of(z_of[k] * picks_here, 16), picks_here)],
                    ans_z.at[k - 1],
                    sems_a,
                    3 + k,
                    deep(k),
                )
                for k in range(1, parts)
            ]
            for c in a_z:
                c.start()
    for c in a_z:
        c.wait_recv()
    answers_ref[...] = (
        ans_own[mine, pick_rows, :].astype(floating)
        + ans_z[0].astype(floating)
        + ans_z[1].astype(floating)
        + ans_z[2].astype(floating)
    )
    for c in m_z:
        c.wait_recv()
    memory_ref[...] = (
        part_own[mine, :, my_cols].astype(floating)
        + got_z[0].astype(floating)
        + got_z[1].astype(floating)
        + got_z[2].astype(floating)
    )
    for i in range(max(steps - 2, 0), steps):
        tg_out(i).wait()
    for c in w_z + g_z + w_plane + w_core + g_one + g_two + [g_three]:
        c.wait_send()
    for c in to_core + m_one + m_two + [a_core] + a_plane + m_z + a_z:
        c.wait_send()


def memory_call(seqs, parts, table, ids, weights_t, grads):
    rows, width = table.shape
    picks_here, length = weights_t.shape
    tokens, picks = ids.shape
    cols = width // parts
    block, tg_block = 128, 256
    pad = max(rows // LANES, 16)
    floating, brain = jnp.float32, jnp.bfloat16
    vmem = pl.BlockSpec(memory_space=pltpu.VMEM)
    anywhere = pl.BlockSpec(memory_space=pl.ANY)
    scratch = [
        ((rows, width), brain),
        ((tokens, picks), jnp.int32),
        ((seqs, picks, length), brain),
        ((tokens, width), brain),
        ((tokens, rows), brain),
        ((block * pad, LANES), floating),
        ((block, picks), floating),
        ((block, picks), floating),
        ((block, picks), floating),
        ((seqs // 2, length, width), brain),
        ((seqs // 2, length, width), brain),
        ((seqs // 2, length, width), brain),
        ((3, length // 2, width), brain),
        ((3, length // 2, width), brain),
        ((parts - 1, length, cols), brain),
        ((seqs // 2, picks, length), brain),
        ((seqs // 2, picks, length), brain),
        ((seqs // 2, picks, length), brain),
        ((3, picks, length), brain),
        ((parts - 1, picks_here, length), brain),
        ((length, rows), floating),
        ((2, tg_block, width), floating),
    ]
    return pl.pallas_call(
        functools.partial(memory_kernel, seqs, parts),
        in_specs=[anywhere, anywhere, vmem, vmem],
        out_specs=[vmem, vmem, anywhere],
        out_shape=[
            jax.ShapeDtypeStruct((length, cols), floating),
            jax.ShapeDtypeStruct((picks_here, length), floating),
            jax.ShapeDtypeStruct((rows, width), floating),
        ],
        scratch_shapes=[pltpu.VMEM(shape, kind) for shape, kind in scratch]
        + [
            pltpu.SemaphoreType.DMA((4,)),
            pltpu.SemaphoreType.DMA((2, 12)),
            pltpu.SemaphoreType.DMA((2, 12)),
            pltpu.SemaphoreType.DMA((2, 14)),
            pltpu.SemaphoreType.DMA((2, 8)),
        ],
        compiler_params=pltpu.CompilerParams(
            collective_id=0, has_side_effects=True, vmem_limit_bytes=58 * 2**20
        ),
        name="memory",
    )(table, ids, weights_t, grads)


def pick_scores(picks, first, second, sub_count):
    columns = jnp.arange(sub_count, dtype=jnp.int32)
    hit_first = (picks // sub_count)[:, :, None] == columns
    hit_second = (picks % sub_count)[:, :, None] == columns
    scores = jnp.sum(jnp.where(hit_first, first[:, None, :], 0.0), axis=2)
    scores = scores + jnp.sum(jnp.where(hit_second, second[:, None, :], 0.0), axis=2)
    return (jax.nn.softmax(scores, axis=-1), hit_first, hit_second)


def per_device(
    block_in,
    cotangent,
    norm_gains,
    col_weights,
    row_weights,
    mem_keys,
    value_table,
    col_down,
    col_up,
    row_down,
    row_up,
    segment_ids,
    adapter_ids,
    pick_ids,
):
    floating = jnp.float32
    brain = jnp.bfloat16
    length = block_in.shape[0]
    col_width = col_weights.shape[2]
    heads_here = col_width // HEAD_DIM
    rows_here = value_table.shape[0]
    pick_tok = pick_ids[:, 0, :]
    query_rows = min(512, length)
    query_blocks = length // query_rows
    sub_count = mem_keys.shape[2]
    half_width = mem_keys.shape[3]
    adapter = adapter_ids[0]
    down_col = lax.dynamic_index_in_dim(col_down, adapter, 1, keepdims=False)
    up_col = lax.dynamic_index_in_dim(col_up, adapter, 1, keepdims=False)
    down_row = lax.dynamic_index_in_dim(row_down, adapter, 1, keepdims=False)
    up_row = lax.dynamic_index_in_dim(row_up, adapter, 1, keepdims=False)
    gain_one = norm_gains[0]
    gain_two = norm_gains[1]
    first_keys = mem_keys[0, 0]
    second_keys = mem_keys[1, 0]
    segments = segment_ids[0]
    positions = jnp.arange(length, dtype=jnp.int32)
    inputs = block_in.astype(floating)
    scale_one = rms_scale(inputs)
    normed_one = (inputs * scale_one * gain_one).astype(brain)
    low_att = jnp.einsum(
        "td,jrd->jtr", normed_one, down_col[:3], preferred_element_type=floating
    ).astype(brain)
    projected = jnp.einsum(
        "td,jde->jte", normed_one, col_weights[:3], preferred_element_type=floating
    )
    projected = projected + ADAPT_SCALE * jnp.einsum(
        "jtr,jre->jte", low_att, up_col[:3], preferred_element_type=floating
    )
    projected = projected.astype(brain)
    queries = projected[0].reshape(length, heads_here, HEAD_DIM)
    keys_here = projected[1].reshape(length, heads_here, HEAD_DIM)
    values_here = projected[2].reshape(length, heads_here, HEAD_DIM)

    def block_logits(start):
        rows_pos = start + jnp.arange(query_rows, dtype=jnp.int32)
        allowed = (segments[:, None] == segments[None, :]) & (
            positions[None, :] <= rows_pos[:, None]
        )
        logits = (
            jnp.einsum("thd,shd->hts", queries, keys_here, preferred_element_type=floating) * 0.125
        )
        return (queries, allowed, jnp.where(allowed[None], logits, -1e30))

    def attend(index):
        query_blk, allowed, logits = block_logits(index * query_rows)
        peak = jnp.max(logits, axis=-1, keepdims=True)
        expos = jnp.exp(logits - peak)
        total = jnp.sum(expos, axis=-1, keepdims=True)
        probs = expos / total
        mixed = jnp.einsum(
            "hts,shd->thd", probs.astype(brain), values_here, preferred_element_type=floating
        )
        return (
            mixed.reshape(query_rows, col_width).astype(brain),
            (peak + jnp.log(total))[:, :, 0],
        )

    att_out, log_totals = lax.map(attend, jnp.arange(query_blocks))
    att_out = att_out.reshape(length, col_width)
    att_part = matmul(att_out, row_weights[0])
    low_part = matmul_nt(att_out, down_row[0])
    att_sum, low_sum = lax.psum((att_part, low_part), "mp")
    low_out = low_sum.astype(brain)
    resid = inputs + att_sum + ADAPT_SCALE * matmul(low_out, up_row[0])
    scale_two = rms_scale(resid)
    normed_two = (resid * scale_two * gain_two).astype(brain)
    low_mem = jnp.einsum(
        "td,jrd->jtr", normed_two, down_col[3:], preferred_element_type=floating
    ).astype(brain)
    mem_query = (
        matmul(normed_two, col_weights[3]) + ADAPT_SCALE * matmul(low_mem[0], up_col[3])
    ).astype(brain)
    gate_pre = matmul(normed_two, col_weights[4]) + ADAPT_SCALE * matmul(low_mem[1], up_col[4])
    first_sub = matmul_nt(mem_query[:, :half_width], first_keys)
    second_sub = matmul_nt(mem_query[:, half_width:], second_keys)

    everyone = ("dp", "mp")
    base = (
        (lax.axis_index("dp") * lax.axis_size("mp") + lax.axis_index("mp")) * rows_here
    ).reshape(1)
    ids_all = lax.all_gather(
        lax.all_gather(pick_tok, "mp", axis=1, tiled=True), "dp", axis=0, tiled=True
    )
    weights, hit_first, hit_second = pick_scores(pick_tok, first_sub, second_sub, sub_count)
    gate_act = jax.nn.silu(gate_pre)
    low_branch_grad = (ADAPT_SCALE * matmul_nt(cotangent, up_row[1])).astype(brain)
    gated_grad = matmul_nt(cotangent, row_weights[1]) + matmul(low_branch_grad, down_row[1])
    mem_grad_cols = (gated_grad * gate_act).astype(brain)
    seqs, parts = lax.axis_size("dp"), lax.axis_size("mp")
    if seqs == 8:
        mem_cols, answers_t, table_grad = memory_call(
            seqs, parts, value_table, ids_all, weights.astype(brain).T, mem_grad_cols
        )
        weight_grad = answers_t.T
    else:
        weights_all = lax.all_gather(
            lax.all_gather(weights.astype(brain), "mp", axis=1, tiled=True), "dp", axis=0, tiled=True
        )
        mem_grad = lax.all_gather(
            lax.all_gather(mem_grad_cols, "mp", axis=1, tiled=True), "dp", axis=0, tiled=True
        )
        spread_w = spread(ids_all, weights_all, base, rows_here)
        partial = matmul(spread_w, value_table).astype(brain)
        mem_cols = lax.psum_scatter(partial, "dp", scatter_dimension=0, tiled=True)
        mem_cols = lax.psum_scatter(mem_cols, "mp", scatter_dimension=1, tiled=True).astype(floating)
        answers = answer(ids_all, mem_grad, value_table, base)
        weight_grad = lax.psum_scatter(answers, "dp", scatter_dimension=0, tiled=True)
        weight_grad = lax.psum_scatter(weight_grad, "mp", scatter_dimension=1, tiled=True)
        table_grad = matmul_tn(spread_w, mem_grad)
    gated = (mem_cols * gate_act).astype(brain)
    branch_part = matmul(gated, row_weights[1])
    low_branch_part = matmul_nt(gated, down_row[1])
    branch_sum, low_branch_sum = (
        lax.psum(branch_part.astype(jnp.bfloat16), "mp").astype(jnp.float32),
        lax.psum(low_branch_part.astype(jnp.bfloat16), "mp").astype(jnp.float32),
    )
    low_branch = low_branch_sum.astype(brain)
    block_out = (resid + branch_sum + ADAPT_SCALE * matmul(low_branch, up_row[1])).astype(brain)
    out_grad = cotangent.astype(floating)
    grad_up_branch = ADAPT_SCALE * matmul_tn(low_branch, cotangent)
    grad_down_branch = matmul_tn(low_branch_grad, gated)
    gate_grad = (gated_grad * mem_cols * silu_slope(gate_pre)).astype(brain)
    score_grad = weights * (
        weight_grad - jnp.sum(weights * weight_grad, axis=-1, keepdims=True)
    )
    first_grad = jnp.sum(jnp.where(hit_first, score_grad[:, :, None], 0.0), axis=1).astype(brain)
    second_grad = jnp.sum(jnp.where(hit_second, score_grad[:, :, None], 0.0), axis=1).astype(brain)
    query_grad = jnp.concatenate(
        [matmul(first_grad, first_keys), matmul(second_grad, second_keys)], axis=1
    ).astype(brain)
    normed_two_part = matmul_nt(query_grad, col_weights[3]) + matmul_nt(gate_grad, col_weights[4])
    low_mem_part = ADAPT_SCALE * jnp.stack(
        [matmul_nt(query_grad, up_col[3]), matmul_nt(gate_grad, up_col[4])]
    )
    grad_up_mem = ADAPT_SCALE * jnp.stack(
        [matmul_tn(low_mem[0], query_grad), matmul_tn(low_mem[1], gate_grad)]
    )
    normed_two_grad, low_mem_grad = lax.psum((normed_two_part, low_mem_part), "mp")
    low_mem_grad = low_mem_grad.astype(brain)
    normed_two_grad = normed_two_grad + jnp.einsum(
        "jtr,jrd->td", low_mem_grad, down_col[3:], preferred_element_type=floating
    )
    grad_down_mem = jnp.einsum(
        "jtr,td->jrd", low_mem_grad, normed_two, preferred_element_type=floating
    )
    weighted_two = gain_two * normed_two_grad
    resid_grad = (
        out_grad
        + scale_two * weighted_two
        - resid * scale_two**3 * jnp.mean(resid * weighted_two, axis=-1, keepdims=True)
    )
    att_branch_grad = resid_grad.astype(brain)
    low_out_grad = (ADAPT_SCALE * matmul_nt(att_branch_grad, up_row[0])).astype(brain)
    grad_up_att = ADAPT_SCALE * matmul_tn(low_out, att_branch_grad)
    att_out_grad = (
        matmul_nt(att_branch_grad, row_weights[0]) + matmul(low_out_grad, down_row[0])
    ).astype(brain)
    grad_down_att = matmul_tn(low_out_grad, att_out)

    def attend_back(carry, index):
        key_acc, value_acc = carry
        start = index * query_rows
        query_blk, allowed, logits = block_logits(start)
        grad_blk = att_out_grad.reshape(query_rows, heads_here, HEAD_DIM)
        probs = jnp.where(allowed[None], jnp.exp(logits - log_totals[index][:, :, None]), 0.0)
        value_acc = value_acc + jnp.einsum(
            "hts,thd->shd", probs.astype(brain), grad_blk, preferred_element_type=floating
        )
        prob_grad = jnp.einsum(
            "thd,shd->hts", grad_blk, values_here, preferred_element_type=floating
        )
        logit_grad = (
            probs * (prob_grad - jnp.sum(probs * prob_grad, axis=-1, keepdims=True))
        ).astype(brain)
        query_part = 0.125 * jnp.einsum(
            "hts,shd->thd", logit_grad, keys_here, preferred_element_type=floating
        )
        key_acc = key_acc + 0.125 * jnp.einsum(
            "hts,thd->shd", logit_grad, query_blk, preferred_element_type=floating
        )
        return ((key_acc, value_acc), query_part.reshape(query_rows, col_width).astype(brain))

    empty = jnp.zeros((length, heads_here, HEAD_DIM), floating)
    (key_grad, value_grad), query_parts = lax.scan(
        attend_back, (empty, empty), jnp.arange(query_blocks)
    )
    proj_grad = jnp.stack(
        [
            query_parts.reshape(length, col_width),
            key_grad.reshape(length, col_width).astype(brain),
            value_grad.reshape(length, col_width).astype(brain),
        ]
    )
    normed_one_part = jnp.einsum(
        "jte,jde->td", proj_grad, col_weights[:3], preferred_element_type=floating
    )
    low_att_part = ADAPT_SCALE * jnp.einsum(
        "jte,jre->jtr", proj_grad, up_col[:3], preferred_element_type=floating
    )
    grad_up_qkv = ADAPT_SCALE * jnp.einsum(
        "jtr,jte->jre", low_att, proj_grad, preferred_element_type=floating
    )
    normed_one_grad, low_att_grad = (
        lax.psum(normed_one_part.astype(jnp.bfloat16), "mp").astype(jnp.float32),
        lax.psum(low_att_part.astype(jnp.bfloat16), "mp").astype(jnp.float32),
    )
    low_att_grad = low_att_grad.astype(brain)
    normed_one_grad = normed_one_grad + jnp.einsum(
        "jtr,jrd->td", low_att_grad, down_col[:3], preferred_element_type=floating
    )
    grad_down_qkv = jnp.einsum(
        "jtr,td->jrd", low_att_grad, normed_one, preferred_element_type=floating
    )
    weighted_one = gain_one * normed_one_grad
    input_grad = (
        resid_grad
        + scale_one * weighted_one
        - inputs * scale_one**3 * jnp.mean(inputs * weighted_one, axis=-1, keepdims=True)
    )
    chosen = (jnp.arange(col_down.shape[1], dtype=jnp.int32) == adapter).astype(floating)
    down_cols_all = (
        jnp.concatenate([grad_down_qkv, grad_down_mem], axis=0)[:, None]
        * chosen[None, :, None, None]
    )
    up_cols_all = (
        jnp.concatenate([grad_up_qkv, grad_up_mem], axis=0)[:, None] * chosen[None, :, None, None]
    )
    down_rows_all = (
        jnp.stack([grad_down_att, grad_down_branch])[:, None] * chosen[None, :, None, None]
    )
    up_rows_all = jnp.stack([grad_up_att, grad_up_branch])[:, None] * chosen[None, :, None, None]
    down_cols_sum, up_cols_sum, down_rows_sum, up_rows_sum = (
        lax.psum(down_cols_all.astype(jnp.bfloat16), "dp").astype(jnp.float32),
        lax.psum(up_cols_all.astype(jnp.bfloat16), "dp").astype(jnp.float32),
        lax.psum(down_rows_all.astype(jnp.bfloat16), "dp").astype(jnp.float32),
        lax.psum(up_rows_all.astype(jnp.bfloat16), "dp").astype(jnp.float32),
    )
    return (
        block_out,
        input_grad,
        table_grad,
        down_cols_sum,
        up_cols_sum,
        down_rows_sum,
        up_rows_sum,
    )


def solution(mesh):
    in_specs = (
        P("dp", None),
        P("dp", None),
        P(),
        P(None, None, "mp"),
        P(None, "mp", None),
        P(None, "mp", None, None),
        P(("dp", "mp"), None),
        P(),
        P(None, None, None, "mp"),
        P(None, None, None, "mp"),
        P(),
        P("dp", None),
        P("dp"),
        P("dp", "mp", None),
    )
    out_specs = (
        P("dp", None),
        P("dp", None),
        P(("dp", "mp"), None),
        P(),
        P(None, None, None, "mp"),
        P(None, None, None, "mp"),
        P(),
    )
    return jax.shard_map(
        per_device, mesh=mesh, in_specs=in_specs, out_specs=out_specs, check_vma=False
    )
```

```python
import functools
import jax
import jax.numpy as jnp
from jax import lax
from jax.experimental import pallas as pl
from jax.experimental.pallas import tpu as pltpu
from jax.sharding import PartitionSpec as P

HEAD_DIM = 64
LANES = 128


EPSILON = 1e-05
ADAPT_SCALE = 0.5


def matmul(left, right):
    return jnp.dot(left, right, preferred_element_type=jnp.float32)


def matmul_nt(left, right):
    return lax.dot_general(
        left, right, (((1,), (1,)), ((), ())), preferred_element_type=jnp.float32
    )


def matmul_tn(left, right):
    return lax.dot_general(
        left, right, (((0,), (0,)), ((), ())), preferred_element_type=jnp.float32
    )


def rms_scale(values):
    return lax.rsqrt(jnp.mean(values * values, axis=-1, keepdims=True) + EPSILON)


def silu_slope(gate):
    sigma = jax.nn.sigmoid(gate)
    return sigma * (1.0 + gate * (1.0 - sigma))


NT = (((1,), (1,)), ((), ()))
TN = (((0,), (0,)), ((), ()))


def split_rows(ids, base, rows):
    local = ids - base
    here = (local >= 0) & (local < rows)
    return jnp.where(here, local & (LANES - 1), 0), jnp.where(here, local >> 7, -1)


def spread_kernel(unroll, base_ref, ids_ref, w_ref, out_ref, lo_s, hi_s, w_s, tiles):
    brain = jnp.bfloat16
    tokens, rows = out_ref.shape
    high = rows // LANES
    pad = max(high, 16)
    lo, hi = split_rows(ids_ref[...], base_ref[0], rows)
    lo_s[...] = lo.astype(jnp.float32)
    hi_s[...] = hi.astype(jnp.float32)
    w_s[...] = w_ref[...].astype(jnp.float32)
    picks = ids_ref.shape[1]
    low_at = lax.broadcasted_iota(jnp.int32, (LANES, picks), 0).astype(jnp.float32).astype(brain)
    high_at = lax.broadcasted_iota(jnp.int32, (pad, picks), 0).astype(jnp.float32)
    empty = jnp.zeros((pad, picks), brain)

    def hot(t):
        lo = jnp.broadcast_to(lo_s[pl.ds(t, 1), :], (LANES, picks)).astype(brain)
        hi = jnp.broadcast_to(hi_s[pl.ds(t, 1), :], (pad, picks))
        w = jnp.broadcast_to(w_s[pl.ds(t, 1), :], (pad, picks))
        low_hot = jnp.where(lo == low_at, brain(1), brain(0))
        high_hot = jnp.where(hi == high_at, w, 0.0).astype(brain)
        return high_hot, low_hot

    def step(i, carry):
        for u in range(0, unroll, 2):
            t = i * unroll + u
            high_0, low_0 = hot(t)
            high_1, low_1 = hot(t + 1)
            left = jnp.concatenate(
                [
                    jnp.concatenate([high_0, empty], axis=1),
                    jnp.concatenate([empty, high_1], axis=1),
                ],
                axis=0,
            )
            right = jnp.concatenate([low_0, low_1], axis=1)
            tiles[pl.ds(t * pad, 2 * pad), :] = lax.dot_general(
                left, right, NT, preferred_element_type=jnp.float32
            )
        return carry

    lax.fori_loop(0, tokens // unroll, step, 0)
    for a in range(high):
        out_ref[:, a * LANES : (a + 1) * LANES] = tiles[pl.ds(a, tokens, stride=pad), :].astype(
            brain
        )


def spread(ids, weights, base, rows, block=128, unroll=32):
    tokens, picks = ids.shape
    pad = max(rows // LANES, 16)
    return pl.pallas_call(
        functools.partial(spread_kernel, unroll),
        grid=(tokens // block,),
        in_specs=[
            pl.BlockSpec(memory_space=pltpu.SMEM),
            pl.BlockSpec((block, picks), lambda i: (i, 0)),
            pl.BlockSpec((block, picks), lambda i: (i, 0)),
        ],
        out_specs=pl.BlockSpec((block, rows), lambda i: (i, 0)),
        out_shape=jax.ShapeDtypeStruct((tokens, rows), jnp.bfloat16),
        scratch_shapes=[pltpu.VMEM((block, picks), jnp.float32)] * 3
        + [pltpu.VMEM((block * pad, LANES), jnp.float32)],
        name="spread",
    )(base, ids, weights)


def answer_kernel(base_ref, grad_ref, table_ref, ids_ref, out_ref, all_s):
    rows = table_ref.shape[0]
    all_s[...] = lax.dot_general(
        grad_ref[...], table_ref[...], NT, preferred_element_type=jnp.float32
    )
    lo, hi = split_rows(ids_ref[...], base_ref[0], rows)
    total = jnp.zeros(ids_ref.shape, jnp.float32)
    for a in range(rows // LANES):
        found = jnp.take_along_axis(
            all_s[:, a * LANES : (a + 1) * LANES], lo, axis=1, mode="promise_in_bounds"
        )
        total = jnp.where(hi == a, found, total)
    out_ref[...] = total.astype(out_ref.dtype)


def answer(ids, grads, table, base, block=256):
    tokens, picks = ids.shape
    rows, width = table.shape
    return pl.pallas_call(
        answer_kernel,
        grid=(tokens // block,),
        in_specs=[
            pl.BlockSpec(memory_space=pltpu.SMEM),
            pl.BlockSpec((block, width), lambda i: (i, 0)),
            pl.BlockSpec((rows, width), lambda i: (0, 0)),
            pl.BlockSpec((block, picks), lambda i: (i, 0)),
        ],
        out_specs=pl.BlockSpec((block, picks), lambda i: (i, 0)),
        out_shape=jax.ShapeDtypeStruct((tokens, picks), jnp.float32),
        scratch_shapes=[pltpu.VMEM((block, rows), jnp.float32)],
        name="answer",
    )(base, grads, table, ids)


MESH = pl.DeviceIdType.MESH
SIDE = 128


class Refs:
    pass


def partner(index, bit):
    return index + bit - 2 * bit * ((index // bit) % 2)


def remote(src, dst, sems, slot, device):
    return pltpu.make_async_remote_copy(
        src_ref=src,
        dst_ref=dst,
        send_sem=sems.at[0, slot],
        recv_sem=sems.at[1, slot],
        device_id=device,
        device_id_type=MESH,
    )


def greet(devices):
    barrier = pltpu.get_barrier_semaphore()
    for device in devices:
        pl.semaphore_signal(barrier, inc=1, device_id=device, device_id_type=MESH)
    pl.semaphore_wait(barrier, len(devices))


def start(copies):
    for c in copies:
        c.start()


def arrive(copies):
    for c in copies:
        c.wait_recv()


def nt(left, right):
    return lax.dot_general(left, right, NT, preferred_element_type=jnp.float32)


def tn(left, right):
    return lax.dot_general(left, right, TN, preferred_element_type=jnp.float32)


def padded(values, rows=SIDE):
    return jnp.concatenate(
        [values, jnp.zeros((rows - values.shape[0], values.shape[1]), values.dtype)], axis=0
    )


def hot_rows(lo_s, hi_s, w_s, tiles, tokens, pad):
    brain = jnp.bfloat16
    picks = lo_s.shape[1]
    low_at = lax.broadcasted_iota(jnp.int32, (LANES, picks), 0).astype(jnp.float32).astype(brain)
    high_at = lax.broadcasted_iota(jnp.int32, (pad, picks), 0).astype(jnp.float32)
    empty = jnp.zeros((pad, picks), brain)

    def hot(t):
        lo = jnp.broadcast_to(lo_s[t : t + 1, :], (LANES, picks)).astype(brain)
        hi = jnp.broadcast_to(hi_s[t : t + 1, :], (pad, picks))
        w = jnp.broadcast_to(w_s[t : t + 1, :], (pad, picks))
        low_hot = jnp.where(lo == low_at, brain(1), brain(0))
        high_hot = jnp.where(hi == high_at, w, 0.0).astype(brain)
        return high_hot, low_hot

    for t in range(0, tokens, 2):
        high_0, low_0 = hot(t)
        high_1, low_1 = hot(t + 1)
        left = jnp.concatenate(
            [
                jnp.concatenate([high_0, empty], axis=1),
                jnp.concatenate([empty, high_1], axis=1),
            ],
            axis=0,
        )
        right = jnp.concatenate([low_0, low_1], axis=1)
        tiles[t * pad : (t + 2) * pad, :] = lax.dot_general(
            left, right, NT, preferred_element_type=jnp.float32
        )


def block_kernel(names, seqs, parts, *refs):
    n = Refs()
    for name, ref in zip(names, refs):
        setattr(n, name, ref)
    floating, brain = jnp.float32, jnp.bfloat16
    d = lax.axis_index("dp")
    m = lax.axis_index("mp")
    length, width = n.block_in.shape
    cols = width // parts
    quarter = length // parts
    rows = n.table_v.shape[0]
    picks_here = n.pick_ids.shape[1]
    picks = picks_here * parts
    half = length // 2
    subs = n.mem_keys.shape[2]
    half_width = n.mem_keys.shape[3]
    heads = cols // HEAD_DIM

    core, x_side, y_side = partner(d, 1), partner(d, 2), partner(d, 4)
    corner = partner(x_side, 4)
    mine, chip_x, chip_y, chip_d = d // 2, x_side // 2, y_side // 2, corner // 2
    z_of = [lax.rem(m + k, parts) for k in range(parts)]
    sent = []

    def at(place):
        return {"dp": place, "mp": m}

    def deep(k):
        return {"dp": d, "mp": z_of[k]}

    def go(copies):
        start(copies)
        sent.extend(copies)
        return copies

    def z_scatter(send, got, sems):
        return go([remote(send.at[z_of[k]], got.at[k - 1], sems, k, deep(k)) for k in range(1, parts)])

    def z_gather(ref, sems, slot=0):
        return go([remote(ref.at[m], ref.at[m], sems, slot + k, deep(k)) for k in range(1, parts)])

    def near_gather(ref, sems):
        places = (x_side, y_side, corner, core)
        return go([remote(ref.at[d], ref.at[d], sems, 4 + i, at(p)) for i, p in enumerate(places)])

    def core_gather(ref, sems):
        places = (x_side, y_side, corner)
        return go([remote(ref.at[p], ref.at[p], sems, 8 + i, at(core)) for i, p in enumerate(places)])

    table_in = pltpu.make_async_copy(n.table, n.table_v, n.local_sems.at[0])
    table_in.start()
    adapter = n.adapter_ids[0]

    n.pick_wide[...] = jnp.zeros(n.pick_wide.shape, jnp.int32)
    n.pick_wide[:, :picks_here] = n.pick_ids[...]
    pick_rows = pl.ds(pl.multiple_of(m * picks_here, 16), picks_here)
    n.picks_own[...] = (
        jnp.transpose(n.pick_wide[...].astype(floating))[:picks_here].astype(jnp.int32)
        + adapter * 65536
    )
    greet(
        [deep(k) for k in range(1, parts)] + [at(x_side), at(y_side), at(corner), at(core)]
    )
    i_z = go(
        [
            remote(n.picks_own, n.ids_t.at[d, pick_rows, :], n.sems_i, k, deep(k))
            for k in range(1, parts)
        ]
    )
    n.ids_t[d, pick_rows, :] = n.picks_own[...]

    inputs = n.block_in[...].astype(floating)
    gain_one, gain_two = n.norm_gains[0:1, :], n.norm_gains[1:2, :]
    scale_one = lax.rsqrt(jnp.mean(inputs * inputs, axis=1, keepdims=True) + EPSILON)
    normed_one = (inputs * scale_one * gain_one).astype(brain)
    n.normed_one[...] = normed_one
    rank = n.col_down.shape[2]
    down_att = jnp.concatenate([n.col_down[j, adapter] for j in range(3)], axis=0)
    down_mem = jnp.concatenate([n.col_down[j, adapter] for j in (3, 4)], axis=0)
    n.up_att[...] = jnp.zeros(n.up_att.shape, brain)
    n.up_mem[...] = jnp.zeros(n.up_mem.shape, brain)
    for j in range(3):
        n.up_att[j * rank : (j + 1) * rank, j * cols : (j + 1) * cols] = n.col_up[j, adapter]
    for j in range(2):
        n.up_mem[j * rank : (j + 1) * rank, j * cols : (j + 1) * cols] = n.col_up[3 + j, adapter]
    low_att = nt(normed_one, down_att).astype(brain)
    n.low_att[...] = low_att
    for j in range(3):
        n.proj[:, j * cols : (j + 1) * cols] = (
            jnp.dot(normed_one, n.col_weights[j], preferred_element_type=floating)
            + ADAPT_SCALE
            * jnp.dot(low_att, n.up_att[:, j * cols : (j + 1) * cols], preferred_element_type=floating)
        ).astype(brain)
    arrive(i_z)
    i_near = near_gather(n.ids_t, n.sems_i)

    segment = jnp.broadcast_to(n.segment_ids[...].astype(floating), (length, length))
    ahead = lax.broadcasted_iota(jnp.int32, (length, length), 1) <= lax.broadcasted_iota(
        jnp.int32, (length, length), 0
    )
    allowed = (segment == jnp.transpose(segment)) & ahead
    lane = lax.broadcasted_iota(jnp.int32, (length, LANES), 1)
    sides = LANES // HEAD_DIM

    def pair_of(which, pair):
        first = which * cols + pair * LANES
        return n.proj[:, first : first + LANES]

    for pair in range(heads // sides):
        query2, key2, value2 = (pair_of(w, pair) for w in range(3))
        mixed = jnp.zeros((length, LANES), floating)
        for side in range(sides):
            own = lane // HEAD_DIM == side
            logits = 0.125 * nt(jnp.where(own, query2, brain(0)), key2)
            logits = jnp.where(allowed, logits, -1e30)
            expos = jnp.exp(logits - jnp.max(logits, axis=1, keepdims=True))
            probs = expos / jnp.sum(expos, axis=1, keepdims=True)
            n.probs[pair * sides + side] = probs
            out = jnp.dot(probs.astype(brain), value2, preferred_element_type=floating)
            mixed = jnp.where(own, out, mixed)
        n.att_out[:, pair * LANES : (pair + 1) * LANES] = mixed.astype(brain)
    att_out = n.att_out[...]
    row_down = [n.row_down[j, adapter] for j in range(2)]
    row_up = [n.row_up[j, adapter] for j in range(2)]
    down_att_out = padded(row_down[0])
    low_part = nt(att_out, down_att_out)
    att_part = jnp.dot(att_out, n.row_weights[0], preferred_element_type=floating)
    att_part = att_part + ADAPT_SCALE * jnp.dot(
        low_part.astype(brain), padded(row_up[0]), preferred_element_type=floating
    )
    n.sum_send[0, :, :, :width] = att_part.astype(brain).reshape(parts, quarter, width)
    n.sum_send[0, :, :, width:] = low_part.astype(brain).reshape(parts, quarter, SIDE)
    r_att = z_scatter(n.sum_send.at[0], n.sum_got.at[0], n.sems_z.at[0])
    arrive(i_near[:3])
    i_core = core_gather(n.ids_t, n.sems_i)

    cotangent = n.cotangent[...]
    low_branch_grad = (ADAPT_SCALE * nt(cotangent, padded(row_up[1]))).astype(brain)
    n.low_branch_grad[...] = low_branch_grad
    n.gated_grad[...] = nt(cotangent, n.row_weights[1]) + jnp.dot(
        low_branch_grad, padded(row_down[1]), preferred_element_type=floating
    )
    arrive(i_near[3:])
    arrive(i_core)
    base = (d * parts + m) * rows

    def turn(s, carry):
        local = n.ids_t[s] % 65536 - base
        here = (local >= 0) & (local < rows)
        turned = jnp.transpose(jnp.where(here, local, -1).astype(floating)).astype(jnp.int32)
        n.ids_v[pl.ds(pl.multiple_of(s * length, 16), length), :] = turned
        n.who[s] = n.ids_t[s, 0:8, 0:LANES] // 65536
        return carry

    lax.fori_loop(0, seqs, turn, 0)

    my_rows = pl.ds(pl.multiple_of(m * quarter, 16), quarter)

    def total_of(i):
        total = n.sum_send[i, m].astype(floating)
        for k in range(parts - 1):
            total = total + n.sum_got[i, k].astype(floating)
        return total

    arrive(r_att)
    total = total_of(0)
    resid = n.block_in[my_rows, :].astype(floating) + total[:, :width]
    n.resid[...] = resid
    scale_two = lax.rsqrt(jnp.mean(resid * resid, axis=1, keepdims=True) + EPSILON)
    n.gath_two[m, :, :width] = (resid * scale_two * gain_two).astype(brain)
    n.gath_two[m, :, width:] = total[:, width:].astype(brain)
    arrive(z_gather(n.gath_two, n.sems_z.at[1]))

    normed_two = n.gath_two[:, :, :width].reshape(length, width)
    low_mem = nt(normed_two, down_mem).astype(brain)
    n.low_mem[...] = low_mem
    mem_query = (
        jnp.dot(normed_two, n.col_weights[3], preferred_element_type=floating)
        + ADAPT_SCALE * jnp.dot(low_mem, n.up_mem[:, :cols], preferred_element_type=floating)
    ).astype(brain)
    sub_one = nt(mem_query[:, :half_width], n.mem_keys[0, 0])
    sub_two = nt(mem_query[:, half_width:], n.mem_keys[1, 0])
    wide = n.pick_wide[...]

    def chosen(table, index):
        found = jnp.zeros(index.shape, floating)
        for c in range(subs // LANES):
            taken = jnp.take_along_axis(
                table[:, c * LANES : (c + 1) * LANES],
                index % LANES,
                axis=1,
                mode="promise_in_bounds",
            )
            found = jnp.where(index // LANES == c, taken, found)
        return found

    scores = chosen(sub_one, wide // subs) + chosen(sub_two, wide % subs)
    scores = jnp.where(lane < picks_here, scores, -1e30)
    expos = jnp.exp(scores - jnp.max(scores, axis=1, keepdims=True))
    weights = expos / jnp.sum(expos, axis=1, keepdims=True)
    n.weights_t[...] = jnp.transpose(weights)[:picks_here]
    n.weights_own[...] = n.weights_t[...].astype(brain)
    w_z = go(
        [
            remote(n.weights_own, n.w_all.at[d, pick_rows, :], n.sems_w, k, deep(k))
            for k in range(1, parts)
        ]
    )
    n.w_all[d, pick_rows, :] = n.weights_own[...]
    gate_pre = jnp.dot(
        normed_two, n.col_weights[4], preferred_element_type=floating
    ) + ADAPT_SCALE * jnp.dot(low_mem, n.up_mem[:, cols:], preferred_element_type=floating)
    n.gate_pre[...] = gate_pre
    sigma = 1.0 / (1.0 + jnp.exp(-gate_pre))
    n.grads_own[...] = (n.gated_grad[...] * (gate_pre * sigma)).astype(brain)
    my_cols = pl.ds(pl.multiple_of(m * cols, LANES), cols)

    def seq_rows(s):
        return pl.ds(pl.multiple_of(s * length, 16), length)

    g_z = go(
        [
            remote(n.grads_own, n.g_all.at[seq_rows(d), my_cols], n.sems_g, k, deep(k))
            for k in range(1, parts)
        ]
    )
    n.g_all[seq_rows(d), my_cols] = n.grads_own[...]
    arrive(w_z)
    w_near = near_gather(n.w_all, n.sems_w)
    arrive(w_near[:3])
    w_core = core_gather(n.w_all, n.sems_w)
    arrive(w_near[3:])
    arrive(w_core)

    block = n.lo_s.shape[0]
    pad = n.tiles.shape[0] // block

    def build(i, carry):
        here = pl.ds(pl.multiple_of(i * block, block), block)
        local = n.ids_v[here, :]
        n.lo_s[...] = jnp.where(local < 0, 0, local & (LANES - 1)).astype(floating)
        n.hi_s[...] = (local >> 7).astype(floating)
        per_seq = length // block
        w_t = n.w_all[i // per_seq, :, pl.ds(pl.multiple_of((i % per_seq) * block, block), block)]
        n.w_s[...] = jnp.transpose(w_t.astype(floating))
        hot_rows(n.lo_s, n.hi_s, n.w_s, n.tiles, block, pad)
        for a in range(rows // LANES):
            n.spread_v[here, a * LANES : (a + 1) * LANES] = n.tiles[
                pl.ds(a, block, stride=pad), :
            ].astype(brain)
        return carry

    blocks = seqs * length // block
    cuts = [0, blocks // 8, (9 * blocks) // 16, (13 * blocks) // 16, blocks]
    lax.fori_loop(cuts[0], cuts[1], build, 0)
    arrive(g_z)

    def whole(s):
        return n.g_all.at[seq_rows(s)]

    def part(s, h):
        return n.g_all.at[pl.ds(pl.multiple_of(s * length + h * half, 16), half)]

    g_one = go(
        [
            remote(whole(d), whole(d), n.sems_g, 4 + i, at(p))
            for i, p in enumerate((x_side, y_side, core))
        ]
    )
    lax.fori_loop(cuts[1], cuts[2], build, 0)
    arrive(g_one[:2])
    g_two = go(
        [
            remote(part(y_side, 0), part(y_side, 0), n.sems_g, 7, at(x_side)),
            remote(part(x_side, 1), part(x_side, 1), n.sems_g, 8, at(y_side)),
            remote(whole(x_side), whole(x_side), n.sems_g, 9, at(core)),
            remote(whole(y_side), whole(y_side), n.sems_g, 10, at(core)),
        ]
    )
    lax.fori_loop(cuts[2], cuts[3], build, 0)
    arrive(g_two[:2])
    g_three = go([remote(whole(corner), whole(corner), n.sems_g, 11, at(core))])
    lax.fori_loop(cuts[3], cuts[4], build, 0)

    table_in.wait()
    sib_core = core % 2

    def partial_of(seq):
        return jnp.dot(
            n.spread_v[seq_rows(seq), :], n.table_v[...], preferred_element_type=floating
        ).astype(brain)

    to_core = []
    for c in range(seqs // 2):
        n.part_sib[c] = partial_of(2 * c + sib_core)
        to_core += go([remote(n.part_sib.at[c], n.got_core.at[c], n.sems_m, c, at(core))])

    def own_part(c, carry):
        n.part_own[c] = partial_of(2 * c + d % 2)
        return carry

    lax.fori_loop(0, seqs // 2, own_part, 0)
    arrive(to_core)

    def fold(c, carry):
        n.part_own[c] = (n.part_own[c].astype(floating) + n.got_core[c].astype(floating)).astype(
            brain
        )
        return carry

    lax.fori_loop(0, seqs // 2, fold, 0)
    upper, lower = pl.ds(0, half), pl.ds(half, half)
    m_one = go(
        [
            remote(n.part_own.at[chip_d, upper], n.got_x.at[0], n.sems_m, 4, at(x_side)),
            remote(n.part_own.at[chip_d, lower], n.got_y.at[0], n.sems_m, 5, at(y_side)),
            remote(n.part_own.at[chip_x, upper], n.got_x.at[1], n.sems_m, 6, at(x_side)),
            remote(n.part_own.at[chip_y, lower], n.got_y.at[1], n.sems_m, 7, at(y_side)),
        ]
    )

    arrive(g_two[2:])
    arrive(g_one[2:])
    arrive(g_three)

    def answers_of(seq):
        n.all_s[...] = nt(n.g_all[seq_rows(seq), :], n.table_v[...])
        local = n.ids_v[seq_rows(seq), :]
        lo, hi = jnp.where(local < 0, 0, local & (LANES - 1)), local >> 7
        total = jnp.zeros((length, picks), floating)
        for a in range(rows // LANES):
            found = jnp.take_along_axis(
                n.all_s[:, a * LANES : (a + 1) * LANES], lo, axis=1, mode="promise_in_bounds"
            )
            total = jnp.where(hi == a, found, total)
        return jnp.transpose(total).astype(brain)

    def sib_answers(c, carry):
        n.ans_sib[c] = answers_of(2 * c + sib_core)
        return carry

    def own_answers(c, carry):
        n.ans_own[c] = answers_of(2 * c + d % 2)
        return carry

    lax.fori_loop(0, seqs // 2, sib_answers, 0)
    a_core = go([remote(n.ans_sib, n.ans_core, n.sems_a, 0, at(core))])
    arrive(m_one[:2])
    n.part_own[chip_y, upper] = (
        n.part_own[chip_y, upper].astype(floating) + n.got_x[0].astype(floating)
    ).astype(brain)
    n.part_own[chip_x, lower] = (
        n.part_own[chip_x, lower].astype(floating) + n.got_y[0].astype(floating)
    ).astype(brain)
    m_two = go(
        [
            remote(n.part_own.at[chip_x, lower], n.got_x.at[2], n.sems_m, 8, at(x_side)),
            remote(n.part_own.at[chip_y, upper], n.got_y.at[2], n.sems_m, 9, at(y_side)),
        ]
    )
    lax.fori_loop(0, seqs // 2, own_answers, 0)
    arrive(a_core)
    n.ans_own[...] = (n.ans_own[...].astype(floating) + n.ans_core[...].astype(floating)).astype(
        brain
    )
    a_plane = go(
        [
            remote(n.ans_own.at[chip], n.ans_plane.at[i], n.sems_a, 1 + i, at(p))
            for i, (chip, p) in enumerate(((chip_x, x_side), (chip_y, y_side), (chip_d, corner)))
        ]
    )
    arrive(m_one[2:])
    arrive(m_two)
    n.part_own[mine, upper] = (
        n.part_own[mine, upper].astype(floating)
        + n.got_x[1].astype(floating)
        + n.got_y[2].astype(floating)
    ).astype(brain)
    n.part_own[mine, lower] = (
        n.part_own[mine, lower].astype(floating)
        + n.got_x[2].astype(floating)
        + n.got_y[1].astype(floating)
    ).astype(brain)

    def cols_of(k):
        return pl.ds(pl.multiple_of(z_of[k] * cols, LANES), cols)

    m_z = go(
        [
            remote(n.part_own.at[mine, :, cols_of(k)], n.got_z.at[k - 1], n.sems_m, 9 + k, deep(k))
            for k in range(1, parts)
        ]
    )

    tg_block = n.tg_v.shape[1]
    tg_steps = rows // tg_block

    def tg_out(i):
        return pltpu.make_async_copy(
            n.tg_v.at[i % 2],
            n.table_grad.at[pl.ds(i * tg_block, tg_block)],
            n.local_sems.at[1 + i % 2],
        )

    def table_grad_steps(first, last):
        for i in range(first, last):
            if i >= 2:
                tg_out(i - 2).wait()
            n.tg_v[i % 2] = tn(
                n.spread_v[:, i * tg_block : (i + 1) * tg_block], n.g_all[...]
            ).astype(brain)
            tg_out(i).start()

    tg_cuts = [0, tg_steps // 4, tg_steps // 2, 3 * tg_steps // 4, tg_steps]
    table_grad_steps(tg_cuts[0], tg_cuts[1])
    arrive(a_plane)
    answered = n.ans_own[mine].astype(floating)
    for k in range(3):
        answered = answered + n.ans_plane[k].astype(floating)
    n.ans_own[mine] = answered.astype(brain)
    a_z = go(
        [
            remote(
                n.ans_own.at[mine, pl.ds(pl.multiple_of(z_of[k] * picks_here, 16), picks_here)],
                n.ans_z.at[k - 1],
                n.sems_a,
                3 + k,
                deep(k),
            )
            for k in range(1, parts)
        ]
    )
    table_grad_steps(tg_cuts[1], tg_cuts[2])

    arrive(a_z)
    weight_grad = n.ans_own[mine, pick_rows, :].astype(floating)
    for k in range(parts - 1):
        weight_grad = weight_grad + n.ans_z[k].astype(floating)
    weights_t = n.weights_t[...]
    n.score_grad[...] = weights_t * (
        weight_grad - jnp.sum(weights_t * weight_grad, axis=0, keepdims=True)
    )
    turned = jnp.transpose(n.pick_wide[...].astype(floating))[:picks_here].astype(jnp.int32)
    n.first_t[...] = (turned // subs).astype(floating)
    n.second_t[...] = (turned % subs).astype(floating)
    sub_block = 64

    def gather_subs(i, carry):
        top = pl.multiple_of(i * sub_block, sub_block)
        key_at = (lax.broadcasted_iota(jnp.int32, (sub_block, length), 0) + top).astype(floating)
        for index, out in ((n.first_t, n.first_grad), (n.second_t, n.second_grad)):
            total = jnp.zeros((sub_block, length), floating)
            for p in range(picks_here):
                total = total + jnp.where(
                    key_at == index[p : p + 1, :], n.score_grad[p : p + 1, :], 0.0
                )
            out[pl.ds(top, sub_block), :] = total.astype(brain)
        return carry

    lax.fori_loop(0, subs // sub_block, gather_subs, 0)
    query_grad = jnp.concatenate(
        [
            tn(n.first_grad[...], n.mem_keys[0, 0]),
            tn(n.second_grad[...], n.mem_keys[1, 0]),
        ],
        axis=1,
    ).astype(brain)
    arrive(m_z)
    memory = n.part_own[mine, :, my_cols].astype(floating)
    for k in range(parts - 1):
        memory = memory + n.got_z[k].astype(floating)
    gate_pre = n.gate_pre[...]
    sigma = 1.0 / (1.0 + jnp.exp(-gate_pre))
    gate_grad = (n.gated_grad[...] * memory * (sigma * (1.0 + gate_pre * (1.0 - sigma)))).astype(
        brain
    )
    mem_grads = jnp.concatenate([query_grad, gate_grad], axis=1)
    low_mem_part = ADAPT_SCALE * nt(mem_grads, padded(n.up_mem[...]))
    two_part = (
        nt(query_grad, n.col_weights[3])
        + nt(gate_grad, n.col_weights[4])
        + jnp.dot(low_mem_part.astype(brain), padded(down_mem), preferred_element_type=floating)
    )
    n.sum_send[1, :, :, :width] = two_part.astype(brain).reshape(parts, quarter, width)
    n.sum_send[1, :, :, width:] = low_mem_part.astype(brain).reshape(parts, quarter, SIDE)
    r_two = z_scatter(n.sum_send.at[1], n.sum_got.at[1], n.sems_z.at[2])

    gated = (memory * (gate_pre * sigma)).astype(brain)
    low_branch_part = nt(gated, padded(row_down[1]))
    branch_part = jnp.dot(gated, n.row_weights[1], preferred_element_type=floating)
    branch_part = branch_part + ADAPT_SCALE * jnp.dot(
        low_branch_part.astype(brain), padded(row_up[1]), preferred_element_type=floating
    )
    n.sum_send[2, :, :, :width] = branch_part.astype(brain).reshape(parts, quarter, width)
    n.sum_send[2, :, :, width:] = low_branch_part.astype(brain).reshape(parts, quarter, SIDE)
    low_mem = n.low_mem[...]
    up_mem_grad = ADAPT_SCALE * tn(low_mem, mem_grads)
    for j in range(2):
        n.narrow[d, (3 + j) * rank : (4 + j) * rank, :] = up_mem_grad[
            j * rank : (j + 1) * rank, j * cols : (j + 1) * cols
        ].astype(brain)
    n.narrow[d, 6 * rank : 7 * rank, :] = tn(n.low_branch_grad[...], gated)[:rank].astype(brain)
    table_grad_steps(tg_cuts[2], tg_cuts[3])
    arrive(r_two)
    total = total_of(1)
    resid = n.resid[...]
    scale_two = lax.rsqrt(jnp.mean(resid * resid, axis=1, keepdims=True) + EPSILON)
    weighted = gain_two * total[:, :width]
    resid_grad = (
        n.cotangent[my_rows, :].astype(floating)
        + scale_two * weighted
        - resid * scale_two**3 * jnp.mean(resid * weighted, axis=1, keepdims=True)
    )
    n.resid_grad[...] = resid_grad
    n.gath_grad[m, :, :width] = resid_grad.astype(brain)
    n.gath_grad[m, :, width:] = total[:, width:].astype(brain)
    q_grad = z_gather(n.gath_grad, n.sems_z.at[3])
    table_grad_steps(tg_cuts[3], tg_cuts[4])
    arrive(q_grad)
    r_branch = z_scatter(n.sum_send.at[2], n.sum_got.at[2], n.sems_z.at[4])

    branch_grad = n.gath_grad[:, :, :width].reshape(length, width)
    low_out_grad = (ADAPT_SCALE * nt(branch_grad, padded(row_up[0]))).astype(brain)
    att_out_grad = (
        nt(branch_grad, n.row_weights[0])
        + jnp.dot(low_out_grad, padded(row_down[0]), preferred_element_type=floating)
    ).astype(brain)
    for pair in range(heads // sides):
        query2, key2, value2 = (pair_of(w, pair) for w in range(3))
        out2 = att_out_grad[:, pair * LANES : (pair + 1) * LANES]
        grads2 = [jnp.zeros((length, LANES), floating)] * 3
        for side in range(sides):
            own = lane // HEAD_DIM == side
            probs = n.probs[pair * sides + side]
            prob_grad = nt(jnp.where(own, out2, brain(0)), value2)
            logit_grad = (
                probs * (prob_grad - jnp.sum(probs * prob_grad, axis=1, keepdims=True))
            ).astype(brain)
            made = (
                0.125 * jnp.dot(logit_grad, key2, preferred_element_type=floating),
                0.125 * tn(logit_grad, query2),
                tn(probs.astype(brain), out2),
            )
            grads2 = [jnp.where(own, new, old) for new, old in zip(made, grads2)]
        for w in range(3):
            first = w * cols + pair * LANES
            n.proj_grad[:, first : first + LANES] = grads2[w].astype(brain)
    proj_grad = n.proj_grad[...]
    low_att_part = ADAPT_SCALE * nt(proj_grad, padded(n.up_att[...]))
    one_part = jnp.dot(low_att_part.astype(brain), padded(down_att), preferred_element_type=floating)
    for j in range(3):
        one_part = one_part + nt(n.proj_grad[:, j * cols : (j + 1) * cols], n.col_weights[j])
    n.sum_send[3, :, :, :width] = one_part.astype(brain).reshape(parts, quarter, width)
    n.sum_send[3, :, :, width:] = low_att_part.astype(brain).reshape(parts, quarter, SIDE)
    r_one = z_scatter(n.sum_send.at[3], n.sum_got.at[3], n.sems_z.at[5])

    up_att_grad = ADAPT_SCALE * tn(n.low_att[...], proj_grad)
    for j in range(3):
        n.narrow[d, j * rank : (j + 1) * rank, :] = up_att_grad[
            j * rank : (j + 1) * rank, j * cols : (j + 1) * cols
        ].astype(brain)
    n.narrow[d, 5 * rank : 6 * rank, :] = tn(low_out_grad, n.att_out[...])[:rank].astype(brain)
    low_mem_grad = n.gath_grad[:, :, width:].reshape(length, SIDE)
    normed_two = n.gath_two[:, :, :width].reshape(length, width)
    n.early[d, : 2 * rank, :] = tn(low_mem_grad, normed_two)[: 2 * rank].astype(brain)
    low_out = n.gath_two[:, :, width:].reshape(length, SIDE)
    n.early[d, 2 * rank :, :] = (ADAPT_SCALE * tn(low_out, branch_grad))[:rank].astype(brain)
    n_near = near_gather(n.narrow, n.sems_b.at[0])
    e_near = near_gather(n.early, n.sems_b.at[1])
    arrive(r_branch)
    total = total_of(2)
    n.gath_out[m] = (n.resid[...] + total[:, :width]).astype(brain)
    n.gath_low[0, m] = total[:, width:].astype(brain)
    q_low = z_gather(n.gath_low.at[0], n.sems_z.at[6])
    arrive(r_one)
    total = total_of(3)
    n.gath_low[1, m] = total[:, width:].astype(brain)
    q_low_att = z_gather(n.gath_low.at[1], n.sems_z.at[7])
    weighted = gain_one * total[:, :width]
    inputs = n.block_in[my_rows, :].astype(floating)
    scale_one = lax.rsqrt(jnp.mean(inputs * inputs, axis=1, keepdims=True) + EPSILON)
    n.gath_in[m] = (
        n.resid_grad[...]
        + scale_one * weighted
        - inputs * scale_one**3 * jnp.mean(inputs * weighted, axis=1, keepdims=True)
    ).astype(brain)
    q_in = z_gather(n.gath_in, n.sems_z.at[8])
    q_out = z_gather(n.gath_out, n.sems_z.at[9])
    arrive(n_near[:3])
    arrive(e_near[:3])
    n_core = core_gather(n.narrow, n.sems_b.at[0])
    e_core = core_gather(n.early, n.sems_b.at[1])
    arrive(q_low)
    low_branch = n.gath_low[0].reshape(length, SIDE)
    n.late[d, 3 * rank :, :] = (ADAPT_SCALE * tn(low_branch, n.cotangent[...]))[:rank].astype(brain)
    arrive(q_low_att)
    low_att_grad = n.gath_low[1].reshape(length, SIDE)
    n.late[d, : 3 * rank, :] = tn(low_att_grad, n.normed_one[...])[: 3 * rank].astype(brain)
    l_near = near_gather(n.late, n.sems_b.at[2])
    arrive(n_near[3:] + e_near[3:] + n_core + e_core)
    arrive(l_near[:3])
    l_core = core_gather(n.late, n.sems_b.at[2])
    arrive(l_near[3:])
    arrive(l_core)

    def place(a, carry):
        wide_late = jnp.zeros(n.late.shape[1:], brain)
        wide_early = jnp.zeros(n.early.shape[1:], brain)
        thin = jnp.zeros(n.narrow.shape[1:], brain)
        for s in range(seqs):
            is_it = (n.who[s, 0:1, 0:1] == a).astype(floating).astype(brain)
            wide_late = wide_late + n.late[s] * is_it
            wide_early = wide_early + n.early[s] * is_it
            thin = thin + n.narrow[s] * is_it
        for j in range(3):
            n.col_down_grad[j, a] = wide_late[j * rank : (j + 1) * rank]
            n.col_up_grad[j, a] = thin[j * rank : (j + 1) * rank]
        for j in range(2):
            n.col_down_grad[3 + j, a] = wide_early[j * rank : (j + 1) * rank]
            n.col_up_grad[3 + j, a] = thin[(3 + j) * rank : (4 + j) * rank]
            n.row_down_grad[j, a] = thin[(5 + j) * rank : (6 + j) * rank]
        n.row_up_grad[0, a] = wide_early[2 * rank :]
        n.row_up_grad[1, a] = wide_late[3 * rank :]
        return carry

    lax.fori_loop(0, n.col_down.shape[1], place, 0)
    arrive(q_in)
    n.input_grad[...] = n.gath_in[...].reshape(length, width)
    arrive(q_out)
    n.block_out[...] = n.gath_out[...].reshape(length, width)
    for i in range(max(tg_steps - 2, 0), tg_steps):
        tg_out(i).wait()
    for c in sent:
        c.wait_send()


def whole_block(args, seqs, parts):
    floating, brain, whole = jnp.float32, jnp.bfloat16, jnp.int32
    given = Refs()
    given.__dict__.update(args)
    length, width = given.block_in.shape
    rows = given.table.shape[0]
    cols, quarter = width // parts, length // parts
    picks_here = given.pick_ids.shape[1]
    picks = picks_here * parts
    rank = given.col_down.shape[2]
    subs = given.mem_keys.shape[2]
    tokens = seqs * length
    block, tg_block = 128, 256
    pad = max(rows // LANES, 16)
    vmem = pl.BlockSpec(memory_space=pltpu.VMEM)
    anywhere = pl.BlockSpec(memory_space=pl.ANY)
    places = dict(adapter_ids=pl.BlockSpec(memory_space=pltpu.SMEM), table=anywhere)
    outs = dict(
        block_out=((length, width), brain),
        input_grad=((length, width), brain),
        table_grad=((rows, width), brain),
        col_down_grad=(given.col_down.shape, brain),
        col_up_grad=(given.col_up.shape, brain),
        row_down_grad=(given.row_down.shape, brain),
        row_up_grad=(given.row_up.shape, brain),
    )
    chips = seqs // 2
    scratch = dict(
        table_v=((rows, width), brain),
        pick_wide=((length, LANES), whole),
        picks_own=((picks_here, length), whole),
        ids_t=((seqs, picks, length), whole),
        ids_v=((tokens, picks), whole),
        who=((seqs, 8, LANES), whole),
        normed_one=((length, width), brain),
        up_att=((3 * rank, 3 * cols), brain),
        up_mem=((2 * rank, 2 * cols), brain),
        low_att=((length, 3 * rank), brain),
        low_mem=((length, 2 * rank), brain),
        proj=((length, 3 * cols), brain),
        proj_grad=((length, 3 * cols), brain),
        probs=((cols // HEAD_DIM, length, length), floating),
        att_out=((length, cols), brain),
        sum_send=((4, parts, quarter, width + SIDE), brain),
        sum_got=((4, parts - 1, quarter, width + SIDE), brain),
        low_branch_grad=((length, SIDE), brain),
        gated_grad=((length, cols), floating),
        resid=((quarter, width), floating),
        resid_grad=((quarter, width), floating),
        gath_two=((parts, quarter, width + SIDE), brain),
        gath_grad=((parts, quarter, width + SIDE), brain),
        gath_out=((parts, quarter, width), brain),
        gath_in=((parts, quarter, width), brain),
        gath_low=((2, parts, quarter, SIDE), brain),
        weights_t=((picks_here, length), floating),
        weights_own=((picks_here, length), brain),
        w_all=((seqs, picks, length), brain),
        gate_pre=((length, cols), floating),
        grads_own=((length, cols), brain),
        g_all=((tokens, width), brain),
        spread_v=((tokens, rows), brain),
        tiles=((block * pad, LANES), floating),
        lo_s=((block, picks), floating),
        hi_s=((block, picks), floating),
        w_s=((block, picks), floating),
        part_own=((chips, length, width), brain),
        part_sib=((chips, length, width), brain),
        got_core=((chips, length, width), brain),
        got_x=((3, length // 2, width), brain),
        got_y=((3, length // 2, width), brain),
        got_z=((parts - 1, length, cols), brain),
        ans_own=((chips, picks, length), brain),
        ans_sib=((chips, picks, length), brain),
        ans_core=((chips, picks, length), brain),
        ans_plane=((3, picks, length), brain),
        ans_z=((parts - 1, picks_here, length), brain),
        all_s=((length, rows), floating),
        tg_v=((2, tg_block, width), brain),
        score_grad=((picks_here, length), floating),
        first_t=((picks_here, length), floating),
        second_t=((picks_here, length), floating),
        first_grad=((subs, length), brain),
        second_grad=((subs, length), brain),
        narrow=((seqs, 7 * rank, cols), brain),
        early=((seqs, 3 * rank, width), brain),
        late=((seqs, 4 * rank, width), brain),
    )
    semaphores = dict(
        local_sems=(3,),
        sems_i=(2, 12),
        sems_w=(2, 12),
        sems_g=(2, 12),
        sems_m=(2, 14),
        sems_a=(2, 8),
        sems_z=(10, 2, 4),
        sems_b=(3, 2, 12),
    )
    names = [*args, *outs, *scratch, *semaphores]
    return pl.pallas_call(
        functools.partial(block_kernel, names, seqs, parts),
        in_specs=[places.get(name, vmem) for name in args],
        out_specs=[anywhere if name == "table_grad" else vmem for name in outs],
        out_shape=[jax.ShapeDtypeStruct(*made) for made in outs.values()],
        scratch_shapes=[pltpu.VMEM(*made) for made in scratch.values()]
        + [pltpu.SemaphoreType.DMA(shape) for shape in semaphores.values()],
        compiler_params=pltpu.CompilerParams(
            collective_id=0, has_side_effects=True, vmem_limit_bytes=62 * 2**20
        ),
        name="whole_block",
    )(*args.values())


def pick_scores(picks, first, second, sub_count):
    columns = jnp.arange(sub_count, dtype=jnp.int32)
    hit_first = (picks // sub_count)[:, :, None] == columns
    hit_second = (picks % sub_count)[:, :, None] == columns
    scores = jnp.sum(jnp.where(hit_first, first[:, None, :], 0.0), axis=2)
    scores = scores + jnp.sum(jnp.where(hit_second, second[:, None, :], 0.0), axis=2)
    return (jax.nn.softmax(scores, axis=-1), hit_first, hit_second)


def per_device(
    block_in,
    cotangent,
    norm_gains,
    col_weights,
    row_weights,
    mem_keys,
    value_table,
    col_down,
    col_up,
    row_down,
    row_up,
    segment_ids,
    adapter_ids,
    pick_ids,
):
    floating = jnp.float32
    brain = jnp.bfloat16
    length = block_in.shape[0]
    col_width = col_weights.shape[2]
    heads_here = col_width // HEAD_DIM
    rows_here = value_table.shape[0]
    pick_tok = pick_ids[:, 0, :]
    query_rows = min(512, length)
    query_blocks = length // query_rows
    sub_count = mem_keys.shape[2]
    half_width = mem_keys.shape[3]
    adapter = adapter_ids[0]
    down_col = lax.dynamic_index_in_dim(col_down, adapter, 1, keepdims=False)
    up_col = lax.dynamic_index_in_dim(col_up, adapter, 1, keepdims=False)
    down_row = lax.dynamic_index_in_dim(row_down, adapter, 1, keepdims=False)
    up_row = lax.dynamic_index_in_dim(row_up, adapter, 1, keepdims=False)
    gain_one = norm_gains[0]
    gain_two = norm_gains[1]
    first_keys = mem_keys[0, 0]
    second_keys = mem_keys[1, 0]
    segments = segment_ids[0]
    positions = jnp.arange(length, dtype=jnp.int32)
    inputs = block_in.astype(floating)
    scale_one = rms_scale(inputs)
    normed_one = (inputs * scale_one * gain_one).astype(brain)
    low_att = jnp.einsum(
        "td,jrd->jtr", normed_one, down_col[:3], preferred_element_type=floating
    ).astype(brain)
    projected = jnp.einsum(
        "td,jde->jte", normed_one, col_weights[:3], preferred_element_type=floating
    )
    projected = projected + ADAPT_SCALE * jnp.einsum(
        "jtr,jre->jte", low_att, up_col[:3], preferred_element_type=floating
    )
    projected = projected.astype(brain)
    queries = projected[0].reshape(length, heads_here, HEAD_DIM)
    keys_here = projected[1].reshape(length, heads_here, HEAD_DIM)
    values_here = projected[2].reshape(length, heads_here, HEAD_DIM)

    def block_logits(start):
        rows_pos = start + jnp.arange(query_rows, dtype=jnp.int32)
        allowed = (segments[:, None] == segments[None, :]) & (
            positions[None, :] <= rows_pos[:, None]
        )
        logits = (
            jnp.einsum("thd,shd->hts", queries, keys_here, preferred_element_type=floating) * 0.125
        )
        return (queries, allowed, jnp.where(allowed[None], logits, -1e30))

    def attend(index):
        query_blk, allowed, logits = block_logits(index * query_rows)
        peak = jnp.max(logits, axis=-1, keepdims=True)
        expos = jnp.exp(logits - peak)
        total = jnp.sum(expos, axis=-1, keepdims=True)
        probs = expos / total
        mixed = jnp.einsum(
            "hts,shd->thd", probs.astype(brain), values_here, preferred_element_type=floating
        )
        return (
            mixed.reshape(query_rows, col_width).astype(brain),
            (peak + jnp.log(total))[:, :, 0],
        )

    att_out, log_totals = lax.map(attend, jnp.arange(query_blocks))
    att_out = att_out.reshape(length, col_width)
    att_part = matmul(att_out, row_weights[0])
    low_part = matmul_nt(att_out, down_row[0])
    att_sum, low_sum = lax.psum((att_part, low_part), "mp")
    low_out = low_sum.astype(brain)
    resid = inputs + att_sum + ADAPT_SCALE * matmul(low_out, up_row[0])
    scale_two = rms_scale(resid)
    normed_two = (resid * scale_two * gain_two).astype(brain)
    low_mem = jnp.einsum(
        "td,jrd->jtr", normed_two, down_col[3:], preferred_element_type=floating
    ).astype(brain)
    mem_query = (
        matmul(normed_two, col_weights[3]) + ADAPT_SCALE * matmul(low_mem[0], up_col[3])
    ).astype(brain)
    gate_pre = matmul(normed_two, col_weights[4]) + ADAPT_SCALE * matmul(low_mem[1], up_col[4])
    first_sub = matmul_nt(mem_query[:, :half_width], first_keys)
    second_sub = matmul_nt(mem_query[:, half_width:], second_keys)

    everyone = ("dp", "mp")
    base = (
        (lax.axis_index("dp") * lax.axis_size("mp") + lax.axis_index("mp")) * rows_here
    ).reshape(1)
    ids_all = lax.all_gather(
        lax.all_gather(pick_tok, "mp", axis=1, tiled=True), "dp", axis=0, tiled=True
    )
    weights, hit_first, hit_second = pick_scores(pick_tok, first_sub, second_sub, sub_count)
    weights_all = lax.all_gather(
        lax.all_gather(weights.astype(brain), "mp", axis=1, tiled=True), "dp", axis=0, tiled=True
    )
    gate_act = jax.nn.silu(gate_pre)
    low_branch_grad = (ADAPT_SCALE * matmul_nt(cotangent, up_row[1])).astype(brain)
    gated_grad = matmul_nt(cotangent, row_weights[1]) + matmul(low_branch_grad, down_row[1])
    mem_grad_cols = (gated_grad * gate_act).astype(brain)
    mem_grad = lax.all_gather(
        lax.all_gather(mem_grad_cols, "mp", axis=1, tiled=True), "dp", axis=0, tiled=True
    )
    spread_w = spread(ids_all, weights_all, base, rows_here)
    partial = matmul(spread_w, value_table).astype(brain)
    mem_cols = lax.psum_scatter(partial, "dp", scatter_dimension=0, tiled=True)
    mem_cols = lax.psum_scatter(mem_cols, "mp", scatter_dimension=1, tiled=True).astype(floating)
    answers = answer(ids_all, mem_grad, value_table, base)
    weight_grad = lax.psum_scatter(answers, "dp", scatter_dimension=0, tiled=True)
    weight_grad = lax.psum_scatter(weight_grad, "mp", scatter_dimension=1, tiled=True)
    table_grad = matmul_tn(spread_w, mem_grad)
    gated = (mem_cols * gate_act).astype(brain)
    branch_part = matmul(gated, row_weights[1])
    low_branch_part = matmul_nt(gated, down_row[1])
    branch_sum, low_branch_sum = (
        lax.psum(branch_part.astype(jnp.bfloat16), "mp").astype(jnp.float32),
        lax.psum(low_branch_part.astype(jnp.bfloat16), "mp").astype(jnp.float32),
    )
    low_branch = low_branch_sum.astype(brain)
    block_out = (resid + branch_sum + ADAPT_SCALE * matmul(low_branch, up_row[1])).astype(brain)
    out_grad = cotangent.astype(floating)
    grad_up_branch = ADAPT_SCALE * matmul_tn(low_branch, cotangent)
    grad_down_branch = matmul_tn(low_branch_grad, gated)
    gate_grad = (gated_grad * mem_cols * silu_slope(gate_pre)).astype(brain)
    score_grad = weights * (
        weight_grad - jnp.sum(weights * weight_grad, axis=-1, keepdims=True)
    )
    first_grad = jnp.sum(jnp.where(hit_first, score_grad[:, :, None], 0.0), axis=1).astype(brain)
    second_grad = jnp.sum(jnp.where(hit_second, score_grad[:, :, None], 0.0), axis=1).astype(brain)
    query_grad = jnp.concatenate(
        [matmul(first_grad, first_keys), matmul(second_grad, second_keys)], axis=1
    ).astype(brain)
    normed_two_part = matmul_nt(query_grad, col_weights[3]) + matmul_nt(gate_grad, col_weights[4])
    low_mem_part = ADAPT_SCALE * jnp.stack(
        [matmul_nt(query_grad, up_col[3]), matmul_nt(gate_grad, up_col[4])]
    )
    grad_up_mem = ADAPT_SCALE * jnp.stack(
        [matmul_tn(low_mem[0], query_grad), matmul_tn(low_mem[1], gate_grad)]
    )
    normed_two_grad, low_mem_grad = lax.psum((normed_two_part, low_mem_part), "mp")
    low_mem_grad = low_mem_grad.astype(brain)
    normed_two_grad = normed_two_grad + jnp.einsum(
        "jtr,jrd->td", low_mem_grad, down_col[3:], preferred_element_type=floating
    )
    grad_down_mem = jnp.einsum(
        "jtr,td->jrd", low_mem_grad, normed_two, preferred_element_type=floating
    )
    weighted_two = gain_two * normed_two_grad
    resid_grad = (
        out_grad
        + scale_two * weighted_two
        - resid * scale_two**3 * jnp.mean(resid * weighted_two, axis=-1, keepdims=True)
    )
    att_branch_grad = resid_grad.astype(brain)
    low_out_grad = (ADAPT_SCALE * matmul_nt(att_branch_grad, up_row[0])).astype(brain)
    grad_up_att = ADAPT_SCALE * matmul_tn(low_out, att_branch_grad)
    att_out_grad = (
        matmul_nt(att_branch_grad, row_weights[0]) + matmul(low_out_grad, down_row[0])
    ).astype(brain)
    grad_down_att = matmul_tn(low_out_grad, att_out)

    def attend_back(carry, index):
        key_acc, value_acc = carry
        start = index * query_rows
        query_blk, allowed, logits = block_logits(start)
        grad_blk = att_out_grad.reshape(query_rows, heads_here, HEAD_DIM)
        probs = jnp.where(allowed[None], jnp.exp(logits - log_totals[index][:, :, None]), 0.0)
        value_acc = value_acc + jnp.einsum(
            "hts,thd->shd", probs.astype(brain), grad_blk, preferred_element_type=floating
        )
        prob_grad = jnp.einsum(
            "thd,shd->hts", grad_blk, values_here, preferred_element_type=floating
        )
        logit_grad = (
            probs * (prob_grad - jnp.sum(probs * prob_grad, axis=-1, keepdims=True))
        ).astype(brain)
        query_part = 0.125 * jnp.einsum(
            "hts,shd->thd", logit_grad, keys_here, preferred_element_type=floating
        )
        key_acc = key_acc + 0.125 * jnp.einsum(
            "hts,thd->shd", logit_grad, query_blk, preferred_element_type=floating
        )
        return ((key_acc, value_acc), query_part.reshape(query_rows, col_width).astype(brain))

    empty = jnp.zeros((length, heads_here, HEAD_DIM), floating)
    (key_grad, value_grad), query_parts = lax.scan(
        attend_back, (empty, empty), jnp.arange(query_blocks)
    )
    proj_grad = jnp.stack(
        [
            query_parts.reshape(length, col_width),
            key_grad.reshape(length, col_width).astype(brain),
            value_grad.reshape(length, col_width).astype(brain),
        ]
    )
    normed_one_part = jnp.einsum(
        "jte,jde->td", proj_grad, col_weights[:3], preferred_element_type=floating
    )
    low_att_part = ADAPT_SCALE * jnp.einsum(
        "jte,jre->jtr", proj_grad, up_col[:3], preferred_element_type=floating
    )
    grad_up_qkv = ADAPT_SCALE * jnp.einsum(
        "jtr,jte->jre", low_att, proj_grad, preferred_element_type=floating
    )
    normed_one_grad, low_att_grad = (
        lax.psum(normed_one_part.astype(jnp.bfloat16), "mp").astype(jnp.float32),
        lax.psum(low_att_part.astype(jnp.bfloat16), "mp").astype(jnp.float32),
    )
    low_att_grad = low_att_grad.astype(brain)
    normed_one_grad = normed_one_grad + jnp.einsum(
        "jtr,jrd->td", low_att_grad, down_col[:3], preferred_element_type=floating
    )
    grad_down_qkv = jnp.einsum(
        "jtr,td->jrd", low_att_grad, normed_one, preferred_element_type=floating
    )
    weighted_one = gain_one * normed_one_grad
    input_grad = (
        resid_grad
        + scale_one * weighted_one
        - inputs * scale_one**3 * jnp.mean(inputs * weighted_one, axis=-1, keepdims=True)
    )
    chosen = (jnp.arange(col_down.shape[1], dtype=jnp.int32) == adapter).astype(floating)
    down_cols_all = (
        jnp.concatenate([grad_down_qkv, grad_down_mem], axis=0)[:, None]
        * chosen[None, :, None, None]
    )
    up_cols_all = (
        jnp.concatenate([grad_up_qkv, grad_up_mem], axis=0)[:, None] * chosen[None, :, None, None]
    )
    down_rows_all = (
        jnp.stack([grad_down_att, grad_down_branch])[:, None] * chosen[None, :, None, None]
    )
    up_rows_all = jnp.stack([grad_up_att, grad_up_branch])[:, None] * chosen[None, :, None, None]
    down_cols_sum, up_cols_sum, down_rows_sum, up_rows_sum = (
        lax.psum(down_cols_all.astype(jnp.bfloat16), "dp").astype(jnp.float32),
        lax.psum(up_cols_all.astype(jnp.bfloat16), "dp").astype(jnp.float32),
        lax.psum(down_rows_all.astype(jnp.bfloat16), "dp").astype(jnp.float32),
        lax.psum(up_rows_all.astype(jnp.bfloat16), "dp").astype(jnp.float32),
    )
    return (
        block_out,
        input_grad,
        table_grad,
        down_cols_sum,
        up_cols_sum,
        down_rows_sum,
        up_rows_sum,
    )


def fused(
    block_in,
    cotangent,
    norm_gains,
    col_weights,
    row_weights,
    mem_keys,
    value_table,
    col_down,
    col_up,
    row_down,
    row_up,
    segment_ids,
    adapter_ids,
    pick_ids,
):
    args = dict(
        block_in=block_in,
        cotangent=cotangent,
        norm_gains=norm_gains,
        col_weights=col_weights,
        row_weights=row_weights,
        mem_keys=mem_keys,
        table=value_table,
        col_down=col_down,
        col_up=col_up,
        row_down=row_down,
        row_up=row_up,
        segment_ids=segment_ids,
        adapter_ids=adapter_ids,
        pick_ids=pick_ids[:, 0, :],
    )
    outs = whole_block(args, lax.axis_size("dp"), lax.axis_size("mp"))
    return (outs[0], *(out.astype(jnp.float32) for out in outs[1:]))


def solution(mesh):
    in_specs = (
        P("dp", None),
        P("dp", None),
        P(),
        P(None, None, "mp"),
        P(None, "mp", None),
        P(None, "mp", None, None),
        P(("dp", "mp"), None),
        P(),
        P(None, None, None, "mp"),
        P(None, None, None, "mp"),
        P(),
        P("dp", None),
        P("dp"),
        P("dp", "mp", None),
    )
    out_specs = (
        P("dp", None),
        P("dp", None),
        P(("dp", "mp"), None),
        P(),
        P(None, None, None, "mp"),
        P(None, None, None, "mp"),
        P(),
    )
    step = fused if mesh.shape["dp"] == 8 else per_device
    return jax.shard_map(
        step, mesh=mesh, in_specs=in_specs, out_specs=out_specs, check_vma=False
    )
```

```python
import functools
import jax
import jax.numpy as jnp
from jax import lax
from jax.experimental import pallas as pl
from jax.experimental.pallas import tpu as pltpu
from jax.sharding import PartitionSpec as P

HEAD_DIM = 64
LANES = 128


EPSILON = 1e-05
ADAPT_SCALE = 0.5


def matmul(left, right):
    return jnp.dot(left, right, preferred_element_type=jnp.float32)


def matmul_nt(left, right):
    return lax.dot_general(
        left, right, (((1,), (1,)), ((), ())), preferred_element_type=jnp.float32
    )


def matmul_tn(left, right):
    return lax.dot_general(
        left, right, (((0,), (0,)), ((), ())), preferred_element_type=jnp.float32
    )


def rms_scale(values):
    return lax.rsqrt(jnp.mean(values * values, axis=-1, keepdims=True) + EPSILON)


def silu_slope(gate):
    sigma = jax.nn.sigmoid(gate)
    return sigma * (1.0 + gate * (1.0 - sigma))


NT = (((1,), (1,)), ((), ()))
TN = (((0,), (0,)), ((), ()))


def split_rows(ids, base, rows):
    local = ids - base
    here = (local >= 0) & (local < rows)
    return jnp.where(here, local & (LANES - 1), 0), jnp.where(here, local >> 7, -1)


def spread_kernel(unroll, base_ref, ids_ref, w_ref, out_ref, lo_s, hi_s, w_s, tiles):
    brain = jnp.bfloat16
    tokens, rows = out_ref.shape
    high = rows // LANES
    pad = max(high, 16)
    lo, hi = split_rows(ids_ref[...], base_ref[0], rows)
    lo_s[...] = lo.astype(jnp.float32)
    hi_s[...] = hi.astype(jnp.float32)
    w_s[...] = w_ref[...].astype(jnp.float32)
    picks = ids_ref.shape[1]
    low_at = lax.broadcasted_iota(jnp.int32, (LANES, picks), 0).astype(jnp.float32).astype(brain)
    high_at = lax.broadcasted_iota(jnp.int32, (pad, picks), 0).astype(jnp.float32)
    empty = jnp.zeros((pad, picks), brain)

    def hot(t):
        lo = jnp.broadcast_to(lo_s[pl.ds(t, 1), :], (LANES, picks)).astype(brain)
        hi = jnp.broadcast_to(hi_s[pl.ds(t, 1), :], (pad, picks))
        w = jnp.broadcast_to(w_s[pl.ds(t, 1), :], (pad, picks))
        low_hot = jnp.where(lo == low_at, brain(1), brain(0))
        high_hot = jnp.where(hi == high_at, w, 0.0).astype(brain)
        return high_hot, low_hot

    def step(i, carry):
        for u in range(0, unroll, 2):
            t = i * unroll + u
            high_0, low_0 = hot(t)
            high_1, low_1 = hot(t + 1)
            left = jnp.concatenate(
                [
                    jnp.concatenate([high_0, empty], axis=1),
                    jnp.concatenate([empty, high_1], axis=1),
                ],
                axis=0,
            )
            right = jnp.concatenate([low_0, low_1], axis=1)
            tiles[pl.ds(t * pad, 2 * pad), :] = lax.dot_general(
                left, right, NT, preferred_element_type=jnp.float32
            )
        return carry

    lax.fori_loop(0, tokens // unroll, step, 0)
    for a in range(high):
        out_ref[:, a * LANES : (a + 1) * LANES] = tiles[pl.ds(a, tokens, stride=pad), :].astype(
            brain
        )


def spread(ids, weights, base, rows, block=128, unroll=32):
    tokens, picks = ids.shape
    pad = max(rows // LANES, 16)
    return pl.pallas_call(
        functools.partial(spread_kernel, unroll),
        grid=(tokens // block,),
        in_specs=[
            pl.BlockSpec(memory_space=pltpu.SMEM),
            pl.BlockSpec((block, picks), lambda i: (i, 0)),
            pl.BlockSpec((block, picks), lambda i: (i, 0)),
        ],
        out_specs=pl.BlockSpec((block, rows), lambda i: (i, 0)),
        out_shape=jax.ShapeDtypeStruct((tokens, rows), jnp.bfloat16),
        scratch_shapes=[pltpu.VMEM((block, picks), jnp.float32)] * 3
        + [pltpu.VMEM((block * pad, LANES), jnp.float32)],
        name="spread",
    )(base, ids, weights)


def answer_kernel(base_ref, grad_ref, table_ref, ids_ref, out_ref, all_s):
    rows = table_ref.shape[0]
    all_s[...] = lax.dot_general(
        grad_ref[...], table_ref[...], NT, preferred_element_type=jnp.float32
    )
    lo, hi = split_rows(ids_ref[...], base_ref[0], rows)
    total = jnp.zeros(ids_ref.shape, jnp.float32)
    for a in range(rows // LANES):
        found = jnp.take_along_axis(
            all_s[:, a * LANES : (a + 1) * LANES], lo, axis=1, mode="promise_in_bounds"
        )
        total = jnp.where(hi == a, found, total)
    out_ref[...] = total.astype(out_ref.dtype)


def answer(ids, grads, table, base, block=256):
    tokens, picks = ids.shape
    rows, width = table.shape
    return pl.pallas_call(
        answer_kernel,
        grid=(tokens // block,),
        in_specs=[
            pl.BlockSpec(memory_space=pltpu.SMEM),
            pl.BlockSpec((block, width), lambda i: (i, 0)),
            pl.BlockSpec((rows, width), lambda i: (0, 0)),
            pl.BlockSpec((block, picks), lambda i: (i, 0)),
        ],
        out_specs=pl.BlockSpec((block, picks), lambda i: (i, 0)),
        out_shape=jax.ShapeDtypeStruct((tokens, picks), jnp.float32),
        scratch_shapes=[pltpu.VMEM((block, rows), jnp.float32)],
        name="answer",
    )(base, grads, table, ids)


MESH = pl.DeviceIdType.MESH
SIDE = 128


class Refs:
    pass


def partner(index, bit):
    return index + bit - 2 * bit * ((index // bit) % 2)


def remote(src, dst, sems, slot, device):
    return pltpu.make_async_remote_copy(
        src_ref=src,
        dst_ref=dst,
        send_sem=sems.at[0, slot],
        recv_sem=sems.at[1, slot],
        device_id=device,
        device_id_type=MESH,
    )


def greet(devices):
    barrier = pltpu.get_barrier_semaphore()
    for device in devices:
        pl.semaphore_signal(barrier, inc=1, device_id=device, device_id_type=MESH)
    pl.semaphore_wait(barrier, len(devices))


def start(copies):
    for c in copies:
        c.start()


def arrive(copies):
    for c in copies:
        c.wait_recv()


def nt(left, right):
    return lax.dot_general(left, right, NT, preferred_element_type=jnp.float32)


def tn(left, right):
    return lax.dot_general(left, right, TN, preferred_element_type=jnp.float32)


def padded(values, rows=SIDE):
    return jnp.concatenate(
        [values, jnp.zeros((rows - values.shape[0], values.shape[1]), values.dtype)], axis=0
    )


def hot_rows(lo_s, hi_s, w_s, tiles, tokens, pad):
    brain = jnp.bfloat16
    picks = lo_s.shape[1]
    low_at = lax.broadcasted_iota(jnp.int32, (LANES, picks), 0).astype(jnp.float32).astype(brain)
    high_at = lax.broadcasted_iota(jnp.int32, (pad, picks), 0).astype(jnp.float32)
    empty = jnp.zeros((pad, picks), brain)

    def hot(t):
        lo = jnp.broadcast_to(lo_s[t : t + 1, :], (LANES, picks)).astype(brain)
        hi = jnp.broadcast_to(hi_s[t : t + 1, :], (pad, picks))
        w = jnp.broadcast_to(w_s[t : t + 1, :], (pad, picks))
        low_hot = jnp.where(lo == low_at, brain(1), brain(0))
        high_hot = jnp.where(hi == high_at, w, 0.0).astype(brain)
        return high_hot, low_hot

    for t in range(0, tokens, 2):
        high_0, low_0 = hot(t)
        high_1, low_1 = hot(t + 1)
        left = jnp.concatenate(
            [
                jnp.concatenate([high_0, empty], axis=1),
                jnp.concatenate([empty, high_1], axis=1),
            ],
            axis=0,
        )
        right = jnp.concatenate([low_0, low_1], axis=1)
        tiles[t * pad : (t + 2) * pad, :] = lax.dot_general(
            left, right, NT, preferred_element_type=jnp.float32
        )


def block_kernel(names, seqs, parts, *refs):
    n = Refs()
    for name, ref in zip(names, refs):
        setattr(n, name, ref)
    floating, brain = jnp.float32, jnp.bfloat16
    d = lax.axis_index("dp")
    m = lax.axis_index("mp")
    length, width = n.block_in.shape
    cols = width // parts
    quarter = length // parts
    rows = n.table_v.shape[0]
    picks_here = n.pick_ids.shape[1]
    picks = picks_here * parts
    half = length // 2
    subs = n.mem_keys.shape[0] // 2
    half_width = n.mem_keys.shape[1]
    heads = cols // HEAD_DIM

    core, x_side, y_side = partner(d, 1), partner(d, 2), partner(d, 4)
    corner = partner(x_side, 4)
    mine, chip_x, chip_y, chip_d = d // 2, x_side // 2, y_side // 2, corner // 2
    z_of = [lax.rem(m + k, parts) for k in range(parts)]
    sent = []

    def at(place):
        return {"dp": place, "mp": m}

    def deep(k):
        return {"dp": d, "mp": z_of[k]}

    def go(copies):
        start(copies)
        sent.extend(copies)
        return copies

    def z_scatter(send, got, sems):
        return go([remote(send.at[z_of[k]], got.at[k - 1], sems, k, deep(k)) for k in range(1, parts)])

    def z_gather(ref, sems, slot=0):
        return go([remote(ref.at[m], ref.at[m], sems, slot + k, deep(k)) for k in range(1, parts)])

    def near_gather(ref, sems):
        places = (x_side, y_side, corner, core)
        return go([remote(ref.at[d], ref.at[d], sems, 4 + i, at(p)) for i, p in enumerate(places)])

    def core_gather(ref, sems):
        places = (x_side, y_side, corner)
        return go([remote(ref.at[p], ref.at[p], sems, 8 + i, at(core)) for i, p in enumerate(places)])

    slot_of = [lax.rem(c - m + parts, parts) for c in range(parts)]

    def local(src, dst, slot):
        copy = pltpu.make_async_copy(src, dst, n.local_sems.at[slot])
        copy.start()
        return copy

    devices = [deep(k) for k in range(1, parts)] + [at(p) for p in (x_side, y_side, corner, core)]
    barrier = pltpu.get_barrier_semaphore()
    for device in devices:
        pl.semaphore_signal(barrier, inc=1, device_id=device, device_id_type=MESH)
    wide_in = [
        local(ref, held, 9 + i)
        for i, (ref, held) in enumerate(
            (
                (n.col_down_in, n.col_down),
                (n.col_up_in, n.col_up),
                (n.row_down_in, n.row_down),
                (n.row_up_in, n.row_up),
                (n.cotangent_in, n.cotangent),
            )
        )
    ]
    qkv_in = local(n.col_weights.at[pl.ds(0, 3)], n.qkv, 0)
    own_in = [
        local(n.row_weights.at[0], n.full_out.at[0], 1),
        local(n.row_weights.at[1], n.full_branch.at[0], 2),
        local(n.col_weights.at[4], n.full_gate.at[0], 3),
        local(n.col_weights.at[3], n.full_query.at[0], 4),
        local(n.mem_keys, n.full_keys.at[0], 5),
    ]
    table_in = local(n.table, n.table_v, 6)
    adapter = n.adapter_ids[0]
    rank = n.col_down.shape[2]

    n.pick_wide[...] = jnp.zeros(n.pick_wide.shape, jnp.int32)
    n.pick_wide[:, :picks_here] = n.pick_ids[...]
    pick_rows = pl.ds(pl.multiple_of(m * picks_here, 16), picks_here)
    n.picks_own[...] = (
        jnp.transpose(n.pick_wide[...].astype(floating))[:picks_here].astype(jnp.int32)
        + adapter * 65536
    )
    for copy in wide_in[:4]:
        copy.wait()
    for i in range(2):
        n.small[m, i * rank : (i + 1) * rank, :] = n.col_up[3 + i, adapter]
        n.small[m, (2 + i) * rank : (3 + i) * rank, :] = n.row_down[i, adapter]
    pl.semaphore_wait(barrier, len(devices))

    class Plane:
        def __init__(self, sems, whole, half):
            self.sems, self.whole, self.half = sems, whole, half

        def one(self):
            places = (x_side, y_side, core)
            self.a = go(
                [
                    remote(self.whole(d), self.whole(d), self.sems, 4 + i, at(p))
                    for i, p in enumerate(places)
                ]
            )

        def two(self):
            arrive(self.a[:2])
            moves = (
                (self.half(y_side, 0), x_side),
                (self.half(x_side, 1), y_side),
                (self.whole(x_side), core),
                (self.whole(y_side), core),
            )
            self.b = go(
                [remote(ref, ref, self.sems, 7 + i, at(p)) for i, (ref, p) in enumerate(moves)]
            )

        def three(self):
            arrive(self.b[:2])
            ref = self.whole(corner)
            self.c = go([remote(ref, ref, self.sems, 11, at(core))])

        def done(self):
            arrive(self.a[2:] + self.b[2:] + self.c)

    class Weights(Plane):
        def __init__(self, sems, own, full):
            chunk = full.shape[1] // seqs
            self.own, self.full, self.chunk = own, full, chunk

            def rows_of(p, h, count):
                return pl.ds(pl.multiple_of(p * chunk + h * (chunk // 2), 16), count)

            super().__init__(
                sems,
                lambda p: full.at[pl.ds(1, parts - 1), rows_of(p, 0, chunk), :],
                lambda p, h: full.at[pl.ds(1, parts - 1), rows_of(p, h, chunk // 2), :],
            )
            self.here = rows_of(d, 0, chunk)

        def deep(self):
            self.z = go(
                [
                    remote(
                        self.own.at[self.here],
                        self.full.at[parts - k, self.here],
                        self.sems,
                        k,
                        deep(k),
                    )
                    for k in range(1, parts)
                ]
            )

        def one(self):
            arrive(self.z)
            super().one()

    out_w = Weights(n.sems_f.at[0], n.row_weights.at[0], n.full_out)
    branch_w = Weights(n.sems_f.at[1], n.row_weights.at[1], n.full_branch)
    gate_w = Weights(n.sems_f.at[2], n.col_weights.at[4], n.full_gate)
    query_w = Weights(n.sems_f.at[3], n.col_weights.at[3], n.full_query)
    keys_w = Weights(n.sems_f.at[4], n.mem_keys, n.full_keys)

    i_z = go(
        [
            remote(n.picks_own, n.ids_t.at[d, pick_rows, :], n.sems_i, k, deep(k))
            for k in range(1, parts)
        ]
    )
    small_z = z_gather(n.small, n.sems_z.at[0])
    out_w.deep()
    n.ids_t[d, pick_rows, :] = n.picks_own[...]

    inputs = n.block_in[...].astype(floating)
    gain_one, gain_two = n.norm_gains[0:1, :], n.norm_gains[1:2, :]
    scale_one = lax.rsqrt(jnp.mean(inputs * inputs, axis=1, keepdims=True) + EPSILON)
    normed_one = (inputs * scale_one * gain_one).astype(brain)
    n.normed_one[...] = normed_one
    down_att = jnp.concatenate([n.col_down[j, adapter] for j in range(3)], axis=0)
    down_mem = jnp.concatenate([n.col_down[j, adapter] for j in (3, 4)], axis=0)
    n.up_att[...] = jnp.zeros(n.up_att.shape, brain)
    n.up_mem[...] = jnp.zeros(n.up_mem.shape, brain)
    for j in range(3):
        n.up_att[j * rank : (j + 1) * rank, j * cols : (j + 1) * cols] = n.col_up[j, adapter]
    for j in range(2):
        n.up_mem[j * rank : (j + 1) * rank, j * cols : (j + 1) * cols] = n.col_up[3 + j, adapter]
    low_att = nt(normed_one, down_att).astype(brain)
    n.low_att[...] = low_att
    qkv_in.wait()
    for j in range(3):
        n.proj[:, j * cols : (j + 1) * cols] = (
            jnp.dot(normed_one, n.qkv[j], preferred_element_type=floating)
            + ADAPT_SCALE
            * jnp.dot(low_att, n.up_att[:, j * cols : (j + 1) * cols], preferred_element_type=floating)
        ).astype(brain)
    arrive(i_z)
    i_near = near_gather(n.ids_t, n.sems_i)
    own_in[0].wait()
    out_w.one()

    segment = jnp.broadcast_to(n.segment_ids[...].astype(floating), (length, length))
    ahead = lax.broadcasted_iota(jnp.int32, (length, length), 1) <= lax.broadcasted_iota(
        jnp.int32, (length, length), 0
    )
    allowed = (segment == jnp.transpose(segment)) & ahead
    lane = lax.broadcasted_iota(jnp.int32, (length, LANES), 1)
    sides = LANES // HEAD_DIM

    def pair_of(which, pair):
        first = which * cols + pair * LANES
        return n.proj[:, first : first + LANES]

    for pair in range(heads // sides):
        query2, key2, value2 = (pair_of(w, pair) for w in range(3))
        mixed = jnp.zeros((length, LANES), floating)
        for side in range(sides):
            own = lane // HEAD_DIM == side
            logits = 0.125 * nt(jnp.where(own, query2, brain(0)), key2)
            logits = jnp.where(allowed, logits, -1e30)
            expos = jnp.exp(logits - jnp.max(logits, axis=1, keepdims=True))
            probs = expos / jnp.sum(expos, axis=1, keepdims=True)
            n.probs[pair * sides + side] = probs
            out = jnp.dot(probs.astype(brain), value2, preferred_element_type=floating)
            mixed = jnp.where(own, out, mixed)
        n.att_out[:, pair * LANES : (pair + 1) * LANES] = mixed.astype(brain)
    my_cols = pl.ds(pl.multiple_of(m * cols, LANES), cols)
    att_z = go(
        [
            remote(n.att_out, n.att_all.at[:, my_cols], n.sems_z.at[1], k, deep(k))
            for k in range(1, parts)
        ]
    )
    n.att_all[:, my_cols] = n.att_out[...]
    arrive(i_near[:3])
    i_core = core_gather(n.ids_t, n.sems_i)
    out_w.two()
    row_down = [n.row_down[j, adapter] for j in range(2)]
    row_up = [n.row_up[j, adapter] for j in range(2)]

    wide_in[4].wait()
    cotangent = n.cotangent[...]
    low_branch_grad = (ADAPT_SCALE * nt(cotangent, padded(row_up[1]))).astype(brain)
    n.low_branch_grad[...] = low_branch_grad
    own_in[1].wait()
    n.gated_own[...] = nt(cotangent, n.full_branch[0]) + jnp.dot(
        low_branch_grad, padded(row_down[1]), preferred_element_type=floating
    )
    out_w.three()
    arrive(i_near[3:])
    arrive(i_core)
    base = (d * parts + m) * rows

    def turn(s, carry):
        local = n.ids_t[s] % 65536 - base
        here = (local >= 0) & (local < rows)
        turned = jnp.transpose(jnp.where(here, local, -1).astype(floating)).astype(jnp.int32)
        n.ids_v[pl.ds(pl.multiple_of(s * length, 16), length), :] = turned
        n.who[s] = n.ids_t[s, 0:8, 0:LANES] // 65536
        return carry

    lax.fori_loop(0, seqs, turn, 0)
    arrive(small_z)

    def over_slots(values, full):
        total = jnp.zeros((values.shape[0], width), floating)
        for c in range(parts):
            total = total + jnp.dot(
                values[:, c * cols : (c + 1) * cols],
                full[slot_of[c]],
                preferred_element_type=floating,
            )
        return total

    def small_of(i):
        return padded(
            jnp.concatenate(
                [n.small[c, i * rank : (i + 1) * rank, :] for c in range(parts)], axis=1
            )
        )

    out_w.done()
    arrive(att_z)
    att_all = n.att_all[...]
    low_out = nt(att_all, small_of(2)).astype(brain)
    n.low_out[...] = low_out
    resid = (
        n.block_in[...].astype(floating)
        + over_slots(att_all, n.full_out)
        + ADAPT_SCALE * jnp.dot(low_out, padded(row_up[0]), preferred_element_type=floating)
    )
    n.resid[...] = resid
    scale_two = lax.rsqrt(jnp.mean(resid * resid, axis=1, keepdims=True) + EPSILON)
    normed_two = (resid * scale_two * gain_two).astype(brain)
    n.normed_two[...] = normed_two

    own_in[3].wait()
    own_in[4].wait()
    low_mem = nt(normed_two, down_mem).astype(brain)
    n.low_mem[...] = low_mem
    mem_query = (
        jnp.dot(normed_two, n.full_query[0], preferred_element_type=floating)
        + ADAPT_SCALE * jnp.dot(low_mem, n.up_mem[:, :cols], preferred_element_type=floating)
    ).astype(brain)
    sub_one = nt(mem_query[:, :half_width], n.full_keys[0, :subs])
    sub_two = nt(mem_query[:, half_width:], n.full_keys[0, subs:])
    wide = n.pick_wide[...]

    def chosen(table, index):
        found = jnp.zeros(index.shape, floating)
        for c in range(subs // LANES):
            taken = jnp.take_along_axis(
                table[:, c * LANES : (c + 1) * LANES],
                index % LANES,
                axis=1,
                mode="promise_in_bounds",
            )
            found = jnp.where(index // LANES == c, taken, found)
        return found

    scores = chosen(sub_one, wide // subs) + chosen(sub_two, wide % subs)
    scores = jnp.where(lane < picks_here, scores, -1e30)
    expos = jnp.exp(scores - jnp.max(scores, axis=1, keepdims=True))
    weights = expos / jnp.sum(expos, axis=1, keepdims=True)
    n.weights_t[...] = jnp.transpose(weights)[:picks_here]
    n.weights_own[...] = n.weights_t[...].astype(brain)
    w_z = go(
        [
            remote(n.weights_own, n.w_all.at[d, pick_rows, :], n.sems_w, k, deep(k))
            for k in range(1, parts)
        ]
    )
    n.w_all[d, pick_rows, :] = n.weights_own[...]
    own_in[2].wait()
    gate_pre = jnp.dot(
        normed_two, n.full_gate[0], preferred_element_type=floating
    ) + ADAPT_SCALE * jnp.dot(low_mem, n.up_mem[:, cols:], preferred_element_type=floating)
    sigma = 1.0 / (1.0 + jnp.exp(-gate_pre))
    n.grads_own[...] = (n.gated_own[...] * (gate_pre * sigma)).astype(brain)

    def seq_rows(s):
        return pl.ds(pl.multiple_of(s * length, 16), length)

    g_z = go(
        [
            remote(n.grads_own, n.g_all.at[seq_rows(d), my_cols], n.sems_g, k, deep(k))
            for k in range(1, parts)
        ]
    )
    n.g_all[seq_rows(d), my_cols] = n.grads_own[...]
    arrive(w_z)
    w_near = near_gather(n.w_all, n.sems_w)

    block = n.lo_s.shape[0]
    pad = n.tiles.shape[0] // block

    per_seq = length // block

    def build(i, carry):
        order = i // per_seq
        mask = (2 * order) % seqs + (2 * order) // seqs
        seq = sum(((d // b + mask // b) % 2) * b for b in (1, 2, 4))
        first = (i % per_seq) * block
        here = pl.ds(pl.multiple_of(seq * length + first, block), block)
        local = n.ids_v[here, :]
        n.lo_s[...] = jnp.where(local < 0, 0, local & (LANES - 1)).astype(floating)
        n.hi_s[...] = (local >> 7).astype(floating)
        w_t = n.w_all[seq, :, pl.ds(pl.multiple_of(first, block), block)]
        n.w_s[...] = jnp.transpose(w_t.astype(floating))
        hot_rows(n.lo_s, n.hi_s, n.w_s, n.tiles, block, pad)
        for a in range(rows // LANES):
            n.spread_v[here, a * LANES : (a + 1) * LANES] = n.tiles[
                pl.ds(a, block, stride=pad), :
            ].astype(brain)
        return carry

    blocks = seqs * per_seq
    lax.fori_loop(0, per_seq, build, 0)
    arrive(w_near[:3])
    w_core = core_gather(n.w_all, n.sems_w)
    lax.fori_loop(per_seq, 2 * per_seq, build, 0)
    grads_g = Plane(
        n.sems_g,
        lambda s: n.g_all.at[seq_rows(s)],
        lambda s, h: n.g_all.at[pl.ds(pl.multiple_of(s * length + h * half, 16), half)],
    )
    arrive(g_z)
    grads_g.one()
    branch_w.deep()
    gate_w.deep()
    lax.fori_loop(2 * per_seq, 3 * per_seq, build, 0)
    arrive(w_near[3:])
    arrive(w_core)
    lax.fori_loop(3 * per_seq, 5 * per_seq, build, 0)
    grads_g.two()
    query_w.deep()
    keys_w.deep()
    lax.fori_loop(5 * per_seq, 7 * per_seq, build, 0)
    grads_g.three()
    branch_w.one()
    gate_w.one()
    lax.fori_loop(7 * per_seq, blocks, build, 0)

    table_in.wait()
    sib_core = core % 2

    def partial_of(seq):
        return jnp.dot(
            n.spread_v[seq_rows(seq), :], n.table_v[...], preferred_element_type=floating
        ).astype(brain)

    to_core = []
    for i, chip in enumerate((chip_d, chip_x, chip_y, mine)):
        n.part_sib[chip] = partial_of(2 * chip + sib_core)
        to_core += go(
            [remote(n.part_sib.at[chip], n.got_core.at[chip], n.sems_m, i, at(core))]
        )

    upper, lower = pl.ds(0, half), pl.ds(half, half)

    branch_w.two()
    gate_w.two()
    m_one = []
    for i, chip in enumerate((chip_d, chip_x, chip_y, mine)):
        n.part_own[chip] = partial_of(2 * chip + d % 2)
        arrive(to_core[i : i + 1])
        n.part_own[chip] = (
            n.part_own[chip].astype(floating) + n.got_core[chip].astype(floating)
        ).astype(brain)
        if i == 0:
            m_one += go(
                [
                    remote(n.part_own.at[chip, upper], n.got_x.at[0], n.sems_m, 4, at(x_side)),
                    remote(n.part_own.at[chip, lower], n.got_y.at[0], n.sems_m, 5, at(y_side)),
                ]
            )
        if i == 1:
            m_one += go(
                [remote(n.part_own.at[chip, upper], n.got_x.at[1], n.sems_m, 6, at(x_side))]
            )
        if i == 2:
            m_one += go(
                [remote(n.part_own.at[chip, lower], n.got_y.at[1], n.sems_m, 7, at(y_side))]
            )

    grads_g.done()

    def answers_of(seq):
        n.all_s[:, :rows] = nt(n.g_all[seq_rows(seq), :], n.table_v[...])
        local = n.ids_v[seq_rows(seq), :]
        lo, hi = jnp.where(local < 0, 0, local & (LANES - 1)), local >> 7
        total = jnp.zeros((length, picks), floating)
        for a in range(rows // LANES):
            found = jnp.take_along_axis(
                n.all_s[:, a * LANES : (a + 1) * LANES], lo, axis=1, mode="promise_in_bounds"
            )
            total = jnp.where(hi == a, found, total)
        return jnp.transpose(total).astype(brain)

    def sib_answers(c, carry):
        n.ans_sib[c] = answers_of(2 * c + sib_core)
        return carry

    def own_answers(c, carry):
        n.ans_own[c] = answers_of(2 * c + d % 2)
        return carry

    lax.fori_loop(0, seqs // 2, sib_answers, 0)
    branch_w.three()
    gate_w.three()
    a_core = go([remote(n.ans_sib, n.ans_core, n.sems_a, 0, at(core))])
    arrive(m_one[:2])
    n.part_own[chip_y, upper] = (
        n.part_own[chip_y, upper].astype(floating) + n.got_x[0].astype(floating)
    ).astype(brain)
    n.part_own[chip_x, lower] = (
        n.part_own[chip_x, lower].astype(floating) + n.got_y[0].astype(floating)
    ).astype(brain)
    m_two = go(
        [
            remote(n.part_own.at[chip_x, lower], n.got_x.at[2], n.sems_m, 8, at(x_side)),
            remote(n.part_own.at[chip_y, upper], n.got_y.at[2], n.sems_m, 9, at(y_side)),
        ]
    )
    lax.fori_loop(0, seqs // 2, own_answers, 0)
    arrive(a_core)
    n.ans_own[...] = (n.ans_own[...].astype(floating) + n.ans_core[...].astype(floating)).astype(
        brain
    )
    a_plane = go(
        [
            remote(n.ans_own.at[chip], n.ans_plane.at[i], n.sems_a, 1 + i, at(p))
            for i, (chip, p) in enumerate(((chip_x, x_side), (chip_y, y_side), (chip_d, corner)))
        ]
    )
    arrive(m_one[2:])
    arrive(m_two)
    n.part_own[mine, upper] = (
        n.part_own[mine, upper].astype(floating)
        + n.got_x[1].astype(floating)
        + n.got_y[2].astype(floating)
    ).astype(brain)
    n.part_own[mine, lower] = (
        n.part_own[mine, lower].astype(floating)
        + n.got_x[2].astype(floating)
        + n.got_y[1].astype(floating)
    ).astype(brain)

    def cols_of(k):
        return pl.ds(pl.multiple_of(z_of[k] * cols, LANES), cols)

    m_z = go(
        [
            remote(n.part_own.at[mine, :, cols_of(k)], n.got_z.at[k - 1], n.sems_m, 9 + k, deep(k))
            for k in range(1, parts)
        ]
    )

    tg_block = n.tg_v.shape[1]
    tg_steps = rows // tg_block

    def tg_out(i):
        return pltpu.make_async_copy(
            n.tg_v.at[i % 2],
            n.table_grad.at[pl.ds(i * tg_block, tg_block)],
            n.local_sems.at[7 + i % 2],
        )

    def table_grad_steps(first, last):
        for i in range(first, last):
            if i >= 2:
                tg_out(i - 2).wait()
            n.tg_v[i % 2] = tn(
                n.spread_v[:, i * tg_block : (i + 1) * tg_block], n.g_all[...]
            ).astype(brain)
            tg_out(i).start()

    query_w.one()
    keys_w.one()
    weave = iter(range(tg_steps))

    def table_grad_some(count):
        for _ in range(count):
            i = next(weave)
            table_grad_steps(i, i + 1)

    table_grad_some(1)
    arrive(a_plane)
    answered = n.ans_own[mine].astype(floating)
    for k in range(3):
        answered = answered + n.ans_plane[k].astype(floating)
    n.ans_own[mine] = answered.astype(brain)
    a_z = go(
        [
            remote(
                n.ans_own.at[mine, pl.ds(pl.multiple_of(z_of[k] * picks_here, 16), picks_here)],
                n.ans_z.at[k - 1],
                n.sems_a,
                3 + k,
                deep(k),
            )
            for k in range(1, parts)
        ]
    )
    branch_w.done()
    gate_w.done()
    cotangent = n.cotangent[...]
    normed_two = n.normed_two[...]
    low_branch_grad = n.low_branch_grad[...]
    low_mem = n.low_mem[...]
    for c in range(parts):
        here = slice(c * cols, (c + 1) * cols)
        n.all_s[:, here] = nt(cotangent, n.full_branch[slot_of[c]]) + jnp.dot(
            low_branch_grad,
            padded(n.small[c, 3 * rank : 4 * rank, :]),
            preferred_element_type=floating,
        )
        n.all_s[:, width + c * cols : width + (c + 1) * cols] = jnp.dot(
            normed_two, n.full_gate[slot_of[c]], preferred_element_type=floating
        ) + ADAPT_SCALE * jnp.dot(
            low_mem[:, rank:], n.small[c, rank : 2 * rank, :], preferred_element_type=floating
        )
    query_w.two()
    keys_w.two()

    arrive(a_z)
    weight_grad = n.ans_own[mine, pick_rows, :].astype(floating)
    for k in range(parts - 1):
        weight_grad = weight_grad + n.ans_z[k].astype(floating)
    weights_t = n.weights_t[...]
    n.score_all[m] = (
        weights_t * (weight_grad - jnp.sum(weights_t * weight_grad, axis=0, keepdims=True))
    ).astype(brain)
    s_z = z_gather(n.score_all, n.sems_z.at[2])
    rows_picked = n.ids_t[d] % 65536
    n.first_t[...] = (rows_picked // subs).astype(floating)
    n.second_t[...] = (rows_picked % subs).astype(floating)
    table_grad_some(1)
    arrive(m_z)
    memory = n.part_own[mine, :, my_cols].astype(floating)
    for k in range(parts - 1):
        memory = memory + n.got_z[k].astype(floating)
    n.mem_own[...] = memory.astype(brain)
    mem_z = go(
        [
            remote(n.mem_own, n.mem_all.at[:, my_cols], n.sems_z.at[3], k, deep(k))
            for k in range(1, parts)
        ]
    )
    n.mem_all[:, my_cols] = n.mem_own[...]

    query_w.three()
    keys_w.three()
    table_grad_some(1)
    query_w.done()
    keys_w.done()
    arrive(s_z)
    n.score_f[...] = n.score_all[...].reshape(picks, length).astype(floating)
    sub_block = subs // 2

    def gather_subs(head, carry):
        for top in range(0, subs, sub_block):
            key_at = (
                (lax.broadcasted_iota(jnp.int32, (sub_block, length), 0) + top)
                .astype(floating)
                .astype(brain)
            )
            ones = jnp.zeros((sub_block, length), brain)
            twos = jnp.zeros((sub_block, length), brain)
            for p in range(picks_here):
                row = pl.ds(head * picks_here + p, 1)
                score = jnp.broadcast_to(n.score_f[row, :], key_at.shape).astype(brain)
                one = jnp.broadcast_to(n.first_t[row, :], key_at.shape).astype(brain)
                two = jnp.broadcast_to(n.second_t[row, :], key_at.shape).astype(brain)
                ones = ones + jnp.where(key_at == one, score, brain(0))
                twos = twos + jnp.where(key_at == two, score, brain(0))
            n.sub_grads[0, top : top + sub_block, :] = ones
            n.sub_grads[1, top : top + sub_block, :] = twos
        for i in range(2):
            first = pl.multiple_of(head * cols + i * half_width, LANES)
            n.query_grad[:, pl.ds(first, half_width)] = tn(
                n.sub_grads[i], n.full_keys[lax.rem(head - m + parts, parts), i * subs : (i + 1) * subs]
            ).astype(brain)
        return carry

    lax.fori_loop(0, parts, gather_subs, 0)
    table_grad_some(2)
    arrive(mem_z)
    for c in range(parts):
        here = slice(c * cols, (c + 1) * cols)
        memory = n.mem_all[:, here].astype(floating)
        gate_pre = n.all_s[:, width + c * cols : width + (c + 1) * cols]
        sigma = 1.0 / (1.0 + jnp.exp(-gate_pre))
        n.gated[:, here] = (memory * (gate_pre * sigma)).astype(brain)
        n.gate_grad[:, here] = (
            n.all_s[:, here] * memory * (sigma * (1.0 + gate_pre * (1.0 - sigma)))
        ).astype(brain)
    query_grad, gate_grad, gated = n.query_grad[...], n.gate_grad[...], n.gated[...]
    low_mem_grads = [
        (ADAPT_SCALE * nt(grads, small_of(i))).astype(brain)
        for i, grads in enumerate((query_grad, gate_grad))
    ]
    two_grad = jnp.dot(
        low_mem_grads[0], padded(n.col_down[3, adapter]), preferred_element_type=floating
    ) + jnp.dot(low_mem_grads[1], padded(n.col_down[4, adapter]), preferred_element_type=floating)
    for c in range(parts):
        here = slice(c * cols, (c + 1) * cols)
        two_grad = two_grad + nt(query_grad[:, here], n.full_query[slot_of[c]])
        two_grad = two_grad + nt(gate_grad[:, here], n.full_gate[slot_of[c]])
    resid = n.resid[...]
    scale_two = lax.rsqrt(jnp.mean(resid * resid, axis=1, keepdims=True) + EPSILON)
    weighted = gain_two * two_grad
    resid_grad = (
        cotangent.astype(floating)
        + scale_two * weighted
        - resid * scale_two**3 * jnp.mean(resid * weighted, axis=1, keepdims=True)
    )
    n.all_s[:, :width] = resid_grad
    branch_grad = resid_grad.astype(brain)
    n.att_all[...] = branch_grad

    low_out_grad = (ADAPT_SCALE * nt(branch_grad, padded(row_up[0]))).astype(brain)
    att_out_grad = (
        nt(branch_grad, n.full_out[0])
        + jnp.dot(low_out_grad, padded(row_down[0]), preferred_element_type=floating)
    ).astype(brain)
    for pair in range(heads // sides):
        query2, key2, value2 = (pair_of(w, pair) for w in range(3))
        out2 = att_out_grad[:, pair * LANES : (pair + 1) * LANES]
        grads2 = [jnp.zeros((length, LANES), floating)] * 3
        for side in range(sides):
            own = lane // HEAD_DIM == side
            probs = n.probs[pair * sides + side]
            prob_grad = nt(jnp.where(own, out2, brain(0)), value2)
            logit_grad = (
                probs * (prob_grad - jnp.sum(probs * prob_grad, axis=1, keepdims=True))
            ).astype(brain)
            made = (
                0.125 * jnp.dot(logit_grad, key2, preferred_element_type=floating),
                0.125 * tn(logit_grad, query2),
                tn(probs.astype(brain), out2),
            )
            grads2 = [jnp.where(own, new, old) for new, old in zip(made, grads2)]
        for w in range(3):
            first = w * cols + pair * LANES
            n.proj_grad[:, first : first + LANES] = grads2[w].astype(brain)
    proj_grad = n.proj_grad[...]
    low_att_part = ADAPT_SCALE * nt(proj_grad, padded(n.up_att[...]))
    one_part = jnp.dot(low_att_part.astype(brain), padded(down_att), preferred_element_type=floating)
    for j in range(3):
        one_part = one_part + nt(n.proj_grad[:, j * cols : (j + 1) * cols], n.qkv[j])
    n.sum_send[:, :, :width] = one_part.astype(brain).reshape(parts, quarter, width)
    n.sum_send[:, :, width:] = low_att_part.astype(brain).reshape(parts, quarter, SIDE)
    r_one = z_scatter(n.sum_send, n.sum_got, n.sems_z.at[4])

    branch_grad, gated = n.att_all[...], n.gated[...]
    low_branch = nt(gated, small_of(3)).astype(brain)
    branch = over_slots(gated, n.full_branch)
    branch = branch + ADAPT_SCALE * jnp.dot(
        low_branch, padded(row_up[1]), preferred_element_type=floating
    )
    n.block_out[...] = (n.resid[...] + branch).astype(brain)
    n.early[d, 3 * rank :, :] = (ADAPT_SCALE * tn(low_branch, n.cotangent[...]))[:rank].astype(brain)
    up_att_grad = ADAPT_SCALE * tn(n.low_att[...], proj_grad)
    for j in range(3):
        n.narrow[d, j * rank : (j + 1) * rank, :] = up_att_grad[
            j * rank : (j + 1) * rank, j * cols : (j + 1) * cols
        ].astype(brain)
    for j, grads in enumerate((n.query_grad, n.gate_grad)):
        n.narrow[d, (3 + j) * rank : (4 + j) * rank, :] = (
            ADAPT_SCALE * tn(n.low_mem[...], grads[:, my_cols])
        )[j * rank : (j + 1) * rank].astype(brain)
    n.narrow[d, 5 * rank : 6 * rank, :] = tn(low_out_grad, n.att_out[...])[:rank].astype(brain)
    n.narrow[d, 6 * rank : 7 * rank, :] = tn(n.low_branch_grad[...], n.gated[:, my_cols])[
        :rank
    ].astype(brain)
    for j in range(2):
        n.early[d, j * rank : (j + 1) * rank, :] = tn(low_mem_grads[j], n.normed_two[...])[
            :rank
        ].astype(brain)
    n.early[d, 2 * rank : 3 * rank, :] = (ADAPT_SCALE * tn(n.low_out[...], branch_grad))[
        :rank
    ].astype(brain)
    n_near = near_gather(n.narrow, n.sems_b.at[0])
    e_near = near_gather(n.early, n.sems_b.at[1])
    table_grad_some(2)
    arrive(r_one)
    my_rows = pl.ds(pl.multiple_of(m * quarter, 16), quarter)
    total = n.sum_send[m].astype(floating)
    for k in range(parts - 1):
        total = total + n.sum_got[k].astype(floating)
    n.gath_low[m] = total[:, width:].astype(brain)
    q_low_att = z_gather(n.gath_low, n.sems_z.at[5])
    weighted = gain_one * total[:, :width]
    inputs = n.block_in[my_rows, :].astype(floating)
    scale_one = lax.rsqrt(jnp.mean(inputs * inputs, axis=1, keepdims=True) + EPSILON)
    n.gath_in[m] = (
        n.all_s[my_rows, :width]
        + scale_one * weighted
        - inputs * scale_one**3 * jnp.mean(inputs * weighted, axis=1, keepdims=True)
    ).astype(brain)
    q_in = z_gather(n.gath_in, n.sems_z.at[6])
    arrive(n_near[:3])
    arrive(e_near[:3])
    n_core = core_gather(n.narrow, n.sems_b.at[0])
    e_core = core_gather(n.early, n.sems_b.at[1])
    arrive(q_low_att)
    low_att_grad = n.gath_low[...].reshape(length, SIDE)
    n.late[d] = tn(low_att_grad, n.normed_one[...])[: 3 * rank].astype(brain)
    l_near = near_gather(n.late, n.sems_b.at[2])
    table_grad_some(tg_steps - 7)
    arrive(n_near[3:] + e_near[3:] + n_core + e_core)
    arrive(l_near[:3])
    l_core = core_gather(n.late, n.sems_b.at[2])
    arrive(l_near[3:])
    arrive(l_core)

    def place(a, carry):
        wide_late = jnp.zeros(n.late.shape[1:], brain)
        wide_early = jnp.zeros(n.early.shape[1:], brain)
        thin = jnp.zeros(n.narrow.shape[1:], brain)
        for s in range(seqs):
            is_it = (n.who[s, 0:1, 0:1] == a).astype(floating).astype(brain)
            wide_late = wide_late + n.late[s] * is_it
            wide_early = wide_early + n.early[s] * is_it
            thin = thin + n.narrow[s] * is_it
        for j in range(3):
            n.col_down_grad[j, a] = wide_late[j * rank : (j + 1) * rank]
            n.col_up_grad[j, a] = thin[j * rank : (j + 1) * rank]
        for j in range(2):
            n.col_down_grad[3 + j, a] = wide_early[j * rank : (j + 1) * rank]
            n.col_up_grad[3 + j, a] = thin[(3 + j) * rank : (4 + j) * rank]
            n.row_down_grad[j, a] = thin[(5 + j) * rank : (6 + j) * rank]
            n.row_up_grad[j, a] = wide_early[(2 + j) * rank : (3 + j) * rank]
        return carry

    lax.fori_loop(0, n.col_down.shape[1], place, 0)
    arrive(q_in)
    n.input_grad[...] = n.gath_in[...].reshape(length, width)
    for i in range(max(tg_steps - 2, 0), tg_steps):
        tg_out(i).wait()
    for c in sent:
        c.wait_send()


def whole_block(args, seqs, parts):
    floating, brain, whole = jnp.float32, jnp.bfloat16, jnp.int32
    given = Refs()
    given.__dict__.update(args)
    length, width = given.block_in.shape
    rows = given.table.shape[0]
    cols, quarter = width // parts, length // parts
    picks_here = given.pick_ids.shape[1]
    picks = picks_here * parts
    rank = given.col_down_in.shape[2]
    subs = given.mem_keys.shape[0] // 2
    tokens = seqs * length
    block, tg_block = 128, 256
    pad = max(rows // LANES, 16)
    vmem = pl.BlockSpec(memory_space=pltpu.VMEM)
    anywhere = pl.BlockSpec(memory_space=pl.ANY)
    inside = dict(
        adapter_ids=pl.BlockSpec(memory_space=pltpu.SMEM),
        block_in=vmem,
        norm_gains=vmem,
        segment_ids=vmem,
        pick_ids=vmem,
    )
    outs = dict(
        block_out=((length, width), brain),
        input_grad=((length, width), brain),
        table_grad=((rows, width), brain),
        col_down_grad=(given.col_down_in.shape, brain),
        col_up_grad=(given.col_up_in.shape, brain),
        row_down_grad=(given.row_down_in.shape, brain),
        row_up_grad=(given.row_up_in.shape, brain),
    )
    chips = seqs // 2
    scratch = dict(
        table_v=((rows, width), brain),
        pick_wide=((length, LANES), whole),
        picks_own=((picks_here, length), whole),
        ids_t=((seqs, picks, length), whole),
        ids_v=((tokens, picks), whole),
        who=((seqs, 8, LANES), whole),
        normed_one=((length, width), brain),
        up_att=((3 * rank, 3 * cols), brain),
        up_mem=((2 * rank, 2 * cols), brain),
        low_att=((length, 3 * rank), brain),
        low_mem=((length, 2 * rank), brain),
        proj=((length, 3 * cols), brain),
        proj_grad=((length, 3 * cols), brain),
        probs=((cols // HEAD_DIM, length, length), floating),
        att_out=((length, cols), brain),
        sum_send=((parts, quarter, width + SIDE), brain),
        sum_got=((parts - 1, quarter, width + SIDE), brain),
        qkv=((3, width, cols), brain),
        col_down=(given.col_down_in.shape, brain),
        col_up=(given.col_up_in.shape, brain),
        row_down=(given.row_down_in.shape, brain),
        row_up=(given.row_up_in.shape, brain),
        cotangent=((length, width), brain),
        full_out=((parts, cols, width), brain),
        full_branch=((parts, cols, width), brain),
        full_gate=((parts, width, cols), brain),
        full_query=((parts, width, cols), brain),
        full_keys=((parts, *given.mem_keys.shape), brain),
        small=((parts, 4 * rank, cols), brain),
        att_all=((length, width), brain),
        low_out=((length, SIDE), brain),
        normed_two=((length, width), brain),
        gated=((length, width), brain),
        gate_grad=((length, width), brain),
        query_grad=((length, width), brain),
        mem_own=((length, cols), brain),
        mem_all=((length, width), brain),
        score_all=((parts, picks_here, length), brain),
        score_f=((picks, length), floating),
        sub_grads=((2, subs, length), brain),
        low_branch_grad=((length, SIDE), brain),
        gated_own=((length, cols), floating),
        resid=((length, width), floating),
        gath_in=((parts, quarter, width), brain),
        gath_low=((parts, quarter, SIDE), brain),
        weights_t=((picks_here, length), floating),
        weights_own=((picks_here, length), brain),
        w_all=((seqs, picks, length), brain),
        grads_own=((length, cols), brain),
        g_all=((tokens, width), brain),
        spread_v=((tokens, rows), brain),
        tiles=((block * pad, LANES), floating),
        lo_s=((block, picks), floating),
        hi_s=((block, picks), floating),
        w_s=((block, picks), floating),
        part_own=((chips, length, width), brain),
        part_sib=((chips, length, width), brain),
        got_core=((chips, length, width), brain),
        got_x=((3, length // 2, width), brain),
        got_y=((3, length // 2, width), brain),
        got_z=((parts - 1, length, cols), brain),
        ans_own=((chips, picks, length), brain),
        ans_sib=((chips, picks, length), brain),
        ans_core=((chips, picks, length), brain),
        ans_plane=((3, picks, length), brain),
        ans_z=((parts - 1, picks_here, length), brain),
        all_s=((length, max(rows, 2 * width)), floating),
        tg_v=((2, tg_block, width), brain),
        first_t=((picks, length), floating),
        second_t=((picks, length), floating),
        narrow=((seqs, 7 * rank, cols), brain),
        early=((seqs, 4 * rank, width), brain),
        late=((seqs, 3 * rank, width), brain),
    )
    semaphores = dict(
        local_sems=(14,),
        sems_i=(2, 12),
        sems_w=(2, 12),
        sems_g=(2, 12),
        sems_m=(2, 14),
        sems_a=(2, 8),
        sems_z=(7, 2, 4),
        sems_f=(5, 2, 12),
        sems_b=(3, 2, 12),
    )
    names = [*args, *outs, *scratch, *semaphores]
    return pl.pallas_call(
        functools.partial(block_kernel, names, seqs, parts),
        in_specs=[inside.get(name, anywhere) for name in args],
        out_specs=[anywhere if name == "table_grad" else vmem for name in outs],
        out_shape=[jax.ShapeDtypeStruct(*made) for made in outs.values()],
        scratch_shapes=[pltpu.VMEM(*made) for made in scratch.values()]
        + [pltpu.SemaphoreType.DMA(shape) for shape in semaphores.values()],
        compiler_params=pltpu.CompilerParams(
            collective_id=0, has_side_effects=True, vmem_limit_bytes=63 * 2**20
        ),
        name="whole_block",
    )(*args.values())


def pick_scores(picks, first, second, sub_count):
    columns = jnp.arange(sub_count, dtype=jnp.int32)
    hit_first = (picks // sub_count)[:, :, None] == columns
    hit_second = (picks % sub_count)[:, :, None] == columns
    scores = jnp.sum(jnp.where(hit_first, first[:, None, :], 0.0), axis=2)
    scores = scores + jnp.sum(jnp.where(hit_second, second[:, None, :], 0.0), axis=2)
    return (jax.nn.softmax(scores, axis=-1), hit_first, hit_second)


def per_device(
    block_in,
    cotangent,
    norm_gains,
    col_weights,
    row_weights,
    mem_keys,
    value_table,
    col_down,
    col_up,
    row_down,
    row_up,
    segment_ids,
    adapter_ids,
    pick_ids,
):
    floating = jnp.float32
    brain = jnp.bfloat16
    length = block_in.shape[0]
    col_width = col_weights.shape[2]
    heads_here = col_width // HEAD_DIM
    rows_here = value_table.shape[0]
    pick_tok = pick_ids[:, 0, :]
    query_rows = min(512, length)
    query_blocks = length // query_rows
    sub_count = mem_keys.shape[2]
    half_width = mem_keys.shape[3]
    adapter = adapter_ids[0]
    down_col = lax.dynamic_index_in_dim(col_down, adapter, 1, keepdims=False)
    up_col = lax.dynamic_index_in_dim(col_up, adapter, 1, keepdims=False)
    down_row = lax.dynamic_index_in_dim(row_down, adapter, 1, keepdims=False)
    up_row = lax.dynamic_index_in_dim(row_up, adapter, 1, keepdims=False)
    gain_one = norm_gains[0]
    gain_two = norm_gains[1]
    first_keys = mem_keys[0, 0]
    second_keys = mem_keys[1, 0]
    segments = segment_ids[0]
    positions = jnp.arange(length, dtype=jnp.int32)
    inputs = block_in.astype(floating)
    scale_one = rms_scale(inputs)
    normed_one = (inputs * scale_one * gain_one).astype(brain)
    low_att = jnp.einsum(
        "td,jrd->jtr", normed_one, down_col[:3], preferred_element_type=floating
    ).astype(brain)
    projected = jnp.einsum(
        "td,jde->jte", normed_one, col_weights[:3], preferred_element_type=floating
    )
    projected = projected + ADAPT_SCALE * jnp.einsum(
        "jtr,jre->jte", low_att, up_col[:3], preferred_element_type=floating
    )
    projected = projected.astype(brain)
    queries = projected[0].reshape(length, heads_here, HEAD_DIM)
    keys_here = projected[1].reshape(length, heads_here, HEAD_DIM)
    values_here = projected[2].reshape(length, heads_here, HEAD_DIM)

    def block_logits(start):
        rows_pos = start + jnp.arange(query_rows, dtype=jnp.int32)
        allowed = (segments[:, None] == segments[None, :]) & (
            positions[None, :] <= rows_pos[:, None]
        )
        logits = (
            jnp.einsum("thd,shd->hts", queries, keys_here, preferred_element_type=floating) * 0.125
        )
        return (queries, allowed, jnp.where(allowed[None], logits, -1e30))

    def attend(index):
        query_blk, allowed, logits = block_logits(index * query_rows)
        peak = jnp.max(logits, axis=-1, keepdims=True)
        expos = jnp.exp(logits - peak)
        total = jnp.sum(expos, axis=-1, keepdims=True)
        probs = expos / total
        mixed = jnp.einsum(
            "hts,shd->thd", probs.astype(brain), values_here, preferred_element_type=floating
        )
        return (
            mixed.reshape(query_rows, col_width).astype(brain),
            (peak + jnp.log(total))[:, :, 0],
        )

    att_out, log_totals = lax.map(attend, jnp.arange(query_blocks))
    att_out = att_out.reshape(length, col_width)
    att_part = matmul(att_out, row_weights[0])
    low_part = matmul_nt(att_out, down_row[0])
    att_sum, low_sum = lax.psum((att_part, low_part), "mp")
    low_out = low_sum.astype(brain)
    resid = inputs + att_sum + ADAPT_SCALE * matmul(low_out, up_row[0])
    scale_two = rms_scale(resid)
    normed_two = (resid * scale_two * gain_two).astype(brain)
    low_mem = jnp.einsum(
        "td,jrd->jtr", normed_two, down_col[3:], preferred_element_type=floating
    ).astype(brain)
    mem_query = (
        matmul(normed_two, col_weights[3]) + ADAPT_SCALE * matmul(low_mem[0], up_col[3])
    ).astype(brain)
    gate_pre = matmul(normed_two, col_weights[4]) + ADAPT_SCALE * matmul(low_mem[1], up_col[4])
    first_sub = matmul_nt(mem_query[:, :half_width], first_keys)
    second_sub = matmul_nt(mem_query[:, half_width:], second_keys)

    everyone = ("dp", "mp")
    base = (
        (lax.axis_index("dp") * lax.axis_size("mp") + lax.axis_index("mp")) * rows_here
    ).reshape(1)
    ids_all = lax.all_gather(
        lax.all_gather(pick_tok, "mp", axis=1, tiled=True), "dp", axis=0, tiled=True
    )
    weights, hit_first, hit_second = pick_scores(pick_tok, first_sub, second_sub, sub_count)
    weights_all = lax.all_gather(
        lax.all_gather(weights.astype(brain), "mp", axis=1, tiled=True), "dp", axis=0, tiled=True
    )
    gate_act = jax.nn.silu(gate_pre)
    low_branch_grad = (ADAPT_SCALE * matmul_nt(cotangent, up_row[1])).astype(brain)
    gated_grad = matmul_nt(cotangent, row_weights[1]) + matmul(low_branch_grad, down_row[1])
    mem_grad_cols = (gated_grad * gate_act).astype(brain)
    mem_grad = lax.all_gather(
        lax.all_gather(mem_grad_cols, "mp", axis=1, tiled=True), "dp", axis=0, tiled=True
    )
    spread_w = spread(ids_all, weights_all, base, rows_here)
    partial = matmul(spread_w, value_table).astype(brain)
    mem_cols = lax.psum_scatter(partial, "dp", scatter_dimension=0, tiled=True)
    mem_cols = lax.psum_scatter(mem_cols, "mp", scatter_dimension=1, tiled=True).astype(floating)
    answers = answer(ids_all, mem_grad, value_table, base)
    weight_grad = lax.psum_scatter(answers, "dp", scatter_dimension=0, tiled=True)
    weight_grad = lax.psum_scatter(weight_grad, "mp", scatter_dimension=1, tiled=True)
    table_grad = matmul_tn(spread_w, mem_grad)
    gated = (mem_cols * gate_act).astype(brain)
    branch_part = matmul(gated, row_weights[1])
    low_branch_part = matmul_nt(gated, down_row[1])
    branch_sum, low_branch_sum = (
        lax.psum(branch_part.astype(jnp.bfloat16), "mp").astype(jnp.float32),
        lax.psum(low_branch_part.astype(jnp.bfloat16), "mp").astype(jnp.float32),
    )
    low_branch = low_branch_sum.astype(brain)
    block_out = (resid + branch_sum + ADAPT_SCALE * matmul(low_branch, up_row[1])).astype(brain)
    out_grad = cotangent.astype(floating)
    grad_up_branch = ADAPT_SCALE * matmul_tn(low_branch, cotangent)
    grad_down_branch = matmul_tn(low_branch_grad, gated)
    gate_grad = (gated_grad * mem_cols * silu_slope(gate_pre)).astype(brain)
    score_grad = weights * (
        weight_grad - jnp.sum(weights * weight_grad, axis=-1, keepdims=True)
    )
    first_grad = jnp.sum(jnp.where(hit_first, score_grad[:, :, None], 0.0), axis=1).astype(brain)
    second_grad = jnp.sum(jnp.where(hit_second, score_grad[:, :, None], 0.0), axis=1).astype(brain)
    query_grad = jnp.concatenate(
        [matmul(first_grad, first_keys), matmul(second_grad, second_keys)], axis=1
    ).astype(brain)
    normed_two_part = matmul_nt(query_grad, col_weights[3]) + matmul_nt(gate_grad, col_weights[4])
    low_mem_part = ADAPT_SCALE * jnp.stack(
        [matmul_nt(query_grad, up_col[3]), matmul_nt(gate_grad, up_col[4])]
    )
    grad_up_mem = ADAPT_SCALE * jnp.stack(
        [matmul_tn(low_mem[0], query_grad), matmul_tn(low_mem[1], gate_grad)]
    )
    normed_two_grad, low_mem_grad = lax.psum((normed_two_part, low_mem_part), "mp")
    low_mem_grad = low_mem_grad.astype(brain)
    normed_two_grad = normed_two_grad + jnp.einsum(
        "jtr,jrd->td", low_mem_grad, down_col[3:], preferred_element_type=floating
    )
    grad_down_mem = jnp.einsum(
        "jtr,td->jrd", low_mem_grad, normed_two, preferred_element_type=floating
    )
    weighted_two = gain_two * normed_two_grad
    resid_grad = (
        out_grad
        + scale_two * weighted_two
        - resid * scale_two**3 * jnp.mean(resid * weighted_two, axis=-1, keepdims=True)
    )
    att_branch_grad = resid_grad.astype(brain)
    low_out_grad = (ADAPT_SCALE * matmul_nt(att_branch_grad, up_row[0])).astype(brain)
    grad_up_att = ADAPT_SCALE * matmul_tn(low_out, att_branch_grad)
    att_out_grad = (
        matmul_nt(att_branch_grad, row_weights[0]) + matmul(low_out_grad, down_row[0])
    ).astype(brain)
    grad_down_att = matmul_tn(low_out_grad, att_out)

    def attend_back(carry, index):
        key_acc, value_acc = carry
        start = index * query_rows
        query_blk, allowed, logits = block_logits(start)
        grad_blk = att_out_grad.reshape(query_rows, heads_here, HEAD_DIM)
        probs = jnp.where(allowed[None], jnp.exp(logits - log_totals[index][:, :, None]), 0.0)
        value_acc = value_acc + jnp.einsum(
            "hts,thd->shd", probs.astype(brain), grad_blk, preferred_element_type=floating
        )
        prob_grad = jnp.einsum(
            "thd,shd->hts", grad_blk, values_here, preferred_element_type=floating
        )
        logit_grad = (
            probs * (prob_grad - jnp.sum(probs * prob_grad, axis=-1, keepdims=True))
        ).astype(brain)
        query_part = 0.125 * jnp.einsum(
            "hts,shd->thd", logit_grad, keys_here, preferred_element_type=floating
        )
        key_acc = key_acc + 0.125 * jnp.einsum(
            "hts,thd->shd", logit_grad, query_blk, preferred_element_type=floating
        )
        return ((key_acc, value_acc), query_part.reshape(query_rows, col_width).astype(brain))

    empty = jnp.zeros((length, heads_here, HEAD_DIM), floating)
    (key_grad, value_grad), query_parts = lax.scan(
        attend_back, (empty, empty), jnp.arange(query_blocks)
    )
    proj_grad = jnp.stack(
        [
            query_parts.reshape(length, col_width),
            key_grad.reshape(length, col_width).astype(brain),
            value_grad.reshape(length, col_width).astype(brain),
        ]
    )
    normed_one_part = jnp.einsum(
        "jte,jde->td", proj_grad, col_weights[:3], preferred_element_type=floating
    )
    low_att_part = ADAPT_SCALE * jnp.einsum(
        "jte,jre->jtr", proj_grad, up_col[:3], preferred_element_type=floating
    )
    grad_up_qkv = ADAPT_SCALE * jnp.einsum(
        "jtr,jte->jre", low_att, proj_grad, preferred_element_type=floating
    )
    normed_one_grad, low_att_grad = (
        lax.psum(normed_one_part.astype(jnp.bfloat16), "mp").astype(jnp.float32),
        lax.psum(low_att_part.astype(jnp.bfloat16), "mp").astype(jnp.float32),
    )
    low_att_grad = low_att_grad.astype(brain)
    normed_one_grad = normed_one_grad + jnp.einsum(
        "jtr,jrd->td", low_att_grad, down_col[:3], preferred_element_type=floating
    )
    grad_down_qkv = jnp.einsum(
        "jtr,td->jrd", low_att_grad, normed_one, preferred_element_type=floating
    )
    weighted_one = gain_one * normed_one_grad
    input_grad = (
        resid_grad
        + scale_one * weighted_one
        - inputs * scale_one**3 * jnp.mean(inputs * weighted_one, axis=-1, keepdims=True)
    )
    chosen = (jnp.arange(col_down.shape[1], dtype=jnp.int32) == adapter).astype(floating)
    down_cols_all = (
        jnp.concatenate([grad_down_qkv, grad_down_mem], axis=0)[:, None]
        * chosen[None, :, None, None]
    )
    up_cols_all = (
        jnp.concatenate([grad_up_qkv, grad_up_mem], axis=0)[:, None] * chosen[None, :, None, None]
    )
    down_rows_all = (
        jnp.stack([grad_down_att, grad_down_branch])[:, None] * chosen[None, :, None, None]
    )
    up_rows_all = jnp.stack([grad_up_att, grad_up_branch])[:, None] * chosen[None, :, None, None]
    down_cols_sum, up_cols_sum, down_rows_sum, up_rows_sum = (
        lax.psum(down_cols_all.astype(jnp.bfloat16), "dp").astype(jnp.float32),
        lax.psum(up_cols_all.astype(jnp.bfloat16), "dp").astype(jnp.float32),
        lax.psum(down_rows_all.astype(jnp.bfloat16), "dp").astype(jnp.float32),
        lax.psum(up_rows_all.astype(jnp.bfloat16), "dp").astype(jnp.float32),
    )
    return (
        block_out,
        input_grad,
        table_grad,
        down_cols_sum,
        up_cols_sum,
        down_rows_sum,
        up_rows_sum,
    )


def widen_kernel(count, *refs):
    refs[count][...] = refs[0][...].astype(jnp.float32)

    @pl.when(pl.program_id(0) == 0)
    def _():
        for given, made in zip(refs[1:count], refs[count + 1 :]):
            made[...] = given[...].astype(jnp.float32)


def widen(table, *others):
    rows, width = table.shape
    block = min(256, rows)
    split = pl.BlockSpec((block, width), lambda i: (i, 0))
    flat = [other.reshape(-1, other.shape[-1]) for other in others]
    specs = [split] + [pl.BlockSpec(other.shape, lambda i: (0, 0)) for other in flat]
    made = pl.pallas_call(
        functools.partial(widen_kernel, 1 + len(flat)),
        grid=(rows // block,),
        in_specs=specs,
        out_specs=specs,
        out_shape=[jax.ShapeDtypeStruct(a.shape, jnp.float32) for a in (table, *flat)],
        compiler_params=pltpu.CompilerParams(vmem_limit_bytes=60 * 2**20),
        name="widen",
    )(table, *flat)
    return [made[0]] + [out.reshape(other.shape) for out, other in zip(made[1:], others)]


def fused(
    block_in,
    cotangent,
    norm_gains,
    col_weights,
    row_weights,
    mem_keys,
    value_table,
    col_down,
    col_up,
    row_down,
    row_up,
    segment_ids,
    adapter_ids,
    pick_ids,
):
    args = dict(
        block_in=block_in,
        cotangent_in=cotangent,
        norm_gains=norm_gains,
        col_weights=col_weights,
        row_weights=row_weights,
        mem_keys=mem_keys.reshape(-1, mem_keys.shape[3]),
        table=value_table,
        col_down_in=col_down,
        col_up_in=col_up,
        row_down_in=row_down,
        row_up_in=row_up,
        segment_ids=segment_ids,
        adapter_ids=adapter_ids,
        pick_ids=pick_ids[:, 0, :],
    )
    outs = whole_block(args, lax.axis_size("dp"), lax.axis_size("mp"))
    table_grad, input_grad, *others = widen(outs[2], outs[1], *outs[3:])
    return (outs[0], input_grad, table_grad, *others)


def solution(mesh):
    in_specs = (
        P("dp", None),
        P("dp", None),
        P(),
        P(None, None, "mp"),
        P(None, "mp", None),
        P(None, "mp", None, None),
        P(("dp", "mp"), None),
        P(),
        P(None, None, None, "mp"),
        P(None, None, None, "mp"),
        P(),
        P("dp", None),
        P("dp"),
        P("dp", "mp", None),
    )
    out_specs = (
        P("dp", None),
        P("dp", None),
        P(("dp", "mp"), None),
        P(),
        P(None, None, None, "mp"),
        P(None, None, None, "mp"),
        P(),
    )
    step = fused if mesh.shape["dp"] == 8 else per_device
    return jax.shard_map(
        step, mesh=mesh, in_specs=in_specs, out_specs=out_specs, check_vma=False
    )
```

```python
import functools
import jax
import jax.numpy as jnp
from jax import lax
from jax.experimental import pallas as pl
from jax.experimental.pallas import tpu as pltpu
from jax.sharding import PartitionSpec as P

HEAD_DIM = 64
LANES = 128


EPSILON = 1e-05
ADAPT_SCALE = 0.5


def matmul(left, right):
    return jnp.dot(left, right, preferred_element_type=jnp.float32)


def matmul_nt(left, right):
    return lax.dot_general(
        left, right, (((1,), (1,)), ((), ())), preferred_element_type=jnp.float32
    )


def matmul_tn(left, right):
    return lax.dot_general(
        left, right, (((0,), (0,)), ((), ())), preferred_element_type=jnp.float32
    )


def rms_scale(values):
    return lax.rsqrt(jnp.mean(values * values, axis=-1, keepdims=True) + EPSILON)


def silu_slope(gate):
    sigma = jax.nn.sigmoid(gate)
    return sigma * (1.0 + gate * (1.0 - sigma))


NT = (((1,), (1,)), ((), ()))
TN = (((0,), (0,)), ((), ()))


def split_rows(ids, base, rows):
    local = ids - base
    here = (local >= 0) & (local < rows)
    return jnp.where(here, local & (LANES - 1), 0), jnp.where(here, local >> 7, -1)


def spread_kernel(unroll, base_ref, ids_ref, w_ref, out_ref, lo_s, hi_s, w_s, tiles):
    brain = jnp.bfloat16
    tokens, rows = out_ref.shape
    high = rows // LANES
    pad = max(high, 16)
    lo, hi = split_rows(ids_ref[...], base_ref[0], rows)
    lo_s[...] = lo.astype(jnp.float32)
    hi_s[...] = hi.astype(jnp.float32)
    w_s[...] = w_ref[...].astype(jnp.float32)
    picks = ids_ref.shape[1]
    low_at = lax.broadcasted_iota(jnp.int32, (LANES, picks), 0).astype(jnp.float32).astype(brain)
    high_at = lax.broadcasted_iota(jnp.int32, (pad, picks), 0).astype(jnp.float32)
    empty = jnp.zeros((pad, picks), brain)

    def hot(t):
        lo = jnp.broadcast_to(lo_s[pl.ds(t, 1), :], (LANES, picks)).astype(brain)
        hi = jnp.broadcast_to(hi_s[pl.ds(t, 1), :], (pad, picks))
        w = jnp.broadcast_to(w_s[pl.ds(t, 1), :], (pad, picks))
        low_hot = jnp.where(lo == low_at, brain(1), brain(0))
        high_hot = jnp.where(hi == high_at, w, 0.0).astype(brain)
        return high_hot, low_hot

    def step(i, carry):
        for u in range(0, unroll, 2):
            t = i * unroll + u
            high_0, low_0 = hot(t)
            high_1, low_1 = hot(t + 1)
            left = jnp.concatenate(
                [
                    jnp.concatenate([high_0, empty], axis=1),
                    jnp.concatenate([empty, high_1], axis=1),
                ],
                axis=0,
            )
            right = jnp.concatenate([low_0, low_1], axis=1)
            tiles[pl.ds(t * pad, 2 * pad), :] = lax.dot_general(
                left, right, NT, preferred_element_type=jnp.float32
            )
        return carry

    lax.fori_loop(0, tokens // unroll, step, 0)
    for a in range(high):
        out_ref[:, a * LANES : (a + 1) * LANES] = tiles[pl.ds(a, tokens, stride=pad), :].astype(
            brain
        )


def spread(ids, weights, base, rows, block=128, unroll=32):
    tokens, picks = ids.shape
    pad = max(rows // LANES, 16)
    return pl.pallas_call(
        functools.partial(spread_kernel, unroll),
        grid=(tokens // block,),
        in_specs=[
            pl.BlockSpec(memory_space=pltpu.SMEM),
            pl.BlockSpec((block, picks), lambda i: (i, 0)),
            pl.BlockSpec((block, picks), lambda i: (i, 0)),
        ],
        out_specs=pl.BlockSpec((block, rows), lambda i: (i, 0)),
        out_shape=jax.ShapeDtypeStruct((tokens, rows), jnp.bfloat16),
        scratch_shapes=[pltpu.VMEM((block, picks), jnp.float32)] * 3
        + [pltpu.VMEM((block * pad, LANES), jnp.float32)],
        name="spread",
    )(base, ids, weights)


def answer_kernel(base_ref, grad_ref, table_ref, ids_ref, out_ref, all_s):
    rows = table_ref.shape[0]
    all_s[...] = lax.dot_general(
        grad_ref[...], table_ref[...], NT, preferred_element_type=jnp.float32
    )
    lo, hi = split_rows(ids_ref[...], base_ref[0], rows)
    total = jnp.zeros(ids_ref.shape, jnp.float32)
    for a in range(rows // LANES):
        found = jnp.take_along_axis(
            all_s[:, a * LANES : (a + 1) * LANES], lo, axis=1, mode="promise_in_bounds"
        )
        total = jnp.where(hi == a, found, total)
    out_ref[...] = total.astype(out_ref.dtype)


def answer(ids, grads, table, base, block=256):
    tokens, picks = ids.shape
    rows, width = table.shape
    return pl.pallas_call(
        answer_kernel,
        grid=(tokens // block,),
        in_specs=[
            pl.BlockSpec(memory_space=pltpu.SMEM),
            pl.BlockSpec((block, width), lambda i: (i, 0)),
            pl.BlockSpec((rows, width), lambda i: (0, 0)),
            pl.BlockSpec((block, picks), lambda i: (i, 0)),
        ],
        out_specs=pl.BlockSpec((block, picks), lambda i: (i, 0)),
        out_shape=jax.ShapeDtypeStruct((tokens, picks), jnp.float32),
        scratch_shapes=[pltpu.VMEM((block, rows), jnp.float32)],
        name="answer",
    )(base, grads, table, ids)


MESH = pl.DeviceIdType.MESH
SIDE = 128


class Refs:
    pass


def partner(index, bit):
    return index + bit - 2 * bit * ((index // bit) % 2)


def remote(src, dst, sems, slot, device):
    return pltpu.make_async_remote_copy(
        src_ref=src,
        dst_ref=dst,
        send_sem=sems.at[0, slot],
        recv_sem=sems.at[1, slot],
        device_id=device,
        device_id_type=MESH,
    )


def greet(devices):
    barrier = pltpu.get_barrier_semaphore()
    for device in devices:
        pl.semaphore_signal(barrier, inc=1, device_id=device, device_id_type=MESH)
    pl.semaphore_wait(barrier, len(devices))


def start(copies):
    for c in copies:
        c.start()


def arrive(copies):
    for c in copies:
        c.wait_recv()


def nt(left, right):
    return lax.dot_general(left, right, NT, preferred_element_type=jnp.float32)


def tn(left, right):
    return lax.dot_general(left, right, TN, preferred_element_type=jnp.float32)


def padded(values, rows=SIDE):
    return jnp.concatenate(
        [values, jnp.zeros((rows - values.shape[0], values.shape[1]), values.dtype)], axis=0
    )


def hot_rows(lo_s, hi_s, w_s, tiles, tokens, pad):
    brain = jnp.bfloat16
    picks = lo_s.shape[1]
    low_at = lax.broadcasted_iota(jnp.int32, (LANES, picks), 0).astype(jnp.float32).astype(brain)
    high_at = lax.broadcasted_iota(jnp.int32, (pad, picks), 0).astype(jnp.float32)
    empty = jnp.zeros((pad, picks), brain)

    def hot(t):
        lo = jnp.broadcast_to(lo_s[t : t + 1, :], (LANES, picks)).astype(brain)
        hi = jnp.broadcast_to(hi_s[t : t + 1, :], (pad, picks))
        w = jnp.broadcast_to(w_s[t : t + 1, :], (pad, picks))
        low_hot = jnp.where(lo == low_at, brain(1), brain(0))
        high_hot = jnp.where(hi == high_at, w, 0.0).astype(brain)
        return high_hot, low_hot

    for t in range(0, tokens, 2):
        high_0, low_0 = hot(t)
        high_1, low_1 = hot(t + 1)
        left = jnp.concatenate(
            [
                jnp.concatenate([high_0, empty], axis=1),
                jnp.concatenate([empty, high_1], axis=1),
            ],
            axis=0,
        )
        right = jnp.concatenate([low_0, low_1], axis=1)
        tiles[t * pad : (t + 2) * pad, :] = lax.dot_general(
            left, right, NT, preferred_element_type=jnp.float32
        )


def block_kernel(names, seqs, parts, *refs):
    n = Refs()
    for name, ref in zip(names, refs):
        setattr(n, name, ref)
    floating, brain = jnp.float32, jnp.bfloat16
    d = lax.axis_index("dp")
    m = lax.axis_index("mp")
    length, width = n.block_in.shape
    cols = width // parts
    quarter = length // parts
    rows = n.table_v.shape[0]
    picks_here = n.pick_ids.shape[1]
    picks = picks_here * parts
    half = length // 2
    subs = n.mem_keys.shape[0] // 2
    half_width = n.mem_keys.shape[1]
    heads = cols // HEAD_DIM

    core, x_side, y_side = partner(d, 1), partner(d, 2), partner(d, 4)
    corner = partner(x_side, 4)
    mine, chip_x, chip_y, chip_d = d // 2, x_side // 2, y_side // 2, corner // 2
    z_of = [lax.rem(m + k, parts) for k in range(parts)]
    sent = []

    def at(place):
        return {"dp": place, "mp": m}

    def deep(k):
        return {"dp": d, "mp": z_of[k]}

    def go(copies):
        start(copies)
        sent.extend(copies)
        return copies

    def z_scatter(send, got, sems):
        return go([remote(send.at[z_of[k]], got.at[k - 1], sems, k, deep(k)) for k in range(1, parts)])

    def z_gather(ref, sems, slot=0):
        return go([remote(ref.at[m], ref.at[m], sems, slot + k, deep(k)) for k in range(1, parts)])

    def near_gather(ref, sems):
        places = (x_side, y_side, corner, core)
        return go([remote(ref.at[d], ref.at[d], sems, 4 + i, at(p)) for i, p in enumerate(places)])

    def core_gather(ref, sems):
        places = (x_side, y_side, corner)
        return go([remote(ref.at[p], ref.at[p], sems, 8 + i, at(core)) for i, p in enumerate(places)])

    slot_of = [lax.rem(c - m + parts, parts) for c in range(parts)]

    def local(src, dst, slot):
        copy = pltpu.make_async_copy(src, dst, n.local_sems.at[slot])
        copy.start()
        return copy

    devices = [deep(k) for k in range(1, parts)] + [at(p) for p in (x_side, y_side, corner, core)]
    barrier = pltpu.get_barrier_semaphore()
    for device in devices:
        pl.semaphore_signal(barrier, inc=1, device_id=device, device_id_type=MESH)
    down_in = local(n.col_down_in, n.col_down, 9)
    qkv_in = local(n.col_weights.at[pl.ds(0, 3)], n.qkv, 0)
    own_out_in = local(n.row_weights.at[0], n.full_out.at[0], 1)
    factors_in = [
        local(ref, held, 10 + i)
        for i, (ref, held) in enumerate(
            (
                (n.row_down_in, n.row_down),
                (n.row_up_in, n.row_up),
                (n.col_up_in, n.col_up),
            )
        )
    ]
    cotangent_in = local(n.cotangent_in, n.cotangent, 13)
    adapter = n.adapter_ids[0]
    rank = n.col_down.shape[2]

    n.pick_wide[...] = jnp.zeros(n.pick_wide.shape, jnp.int32)
    n.pick_wide[:, :picks_here] = n.pick_ids[...]
    pick_rows = pl.ds(pl.multiple_of(m * picks_here, 16), picks_here)
    n.picks_own[...] = (
        jnp.transpose(n.pick_wide[...].astype(floating))[:picks_here].astype(jnp.int32)
        + adapter * 65536
    )
    for copy in factors_in:
        copy.wait()
    factors = (n.row_down[0, adapter], n.col_up[3, adapter], n.col_up[4, adapter], n.row_down[1, adapter])
    for i, factor in enumerate(factors):
        n.small[m, i * rank : (i + 1) * rank, :] = factor
    pl.semaphore_wait(barrier, len(devices))

    class Plane:
        def __init__(self, sems, whole, half):
            self.sems, self.whole, self.half = sems, whole, half

        def one(self):
            places = (x_side, y_side, core)
            self.a = go(
                [
                    remote(self.whole(d), self.whole(d), self.sems, 4 + i, at(p))
                    for i, p in enumerate(places)
                ]
            )

        def two(self):
            arrive(self.a[:2])
            moves = (
                (self.half(y_side, 0), x_side),
                (self.half(x_side, 1), y_side),
                (self.whole(x_side), core),
                (self.whole(y_side), core),
            )
            self.b = go(
                [remote(ref, ref, self.sems, 7 + i, at(p)) for i, (ref, p) in enumerate(moves)]
            )

        def three(self):
            arrive(self.b[:2])
            ref = self.whole(corner)
            self.c = go([remote(ref, ref, self.sems, 11, at(core))])

        def done(self):
            arrive(self.a[2:] + self.b[2:] + self.c)

    class Weights(Plane):
        def __init__(self, sems, own, full):
            chunk = full.shape[1] // seqs
            self.own, self.full, self.chunk = own, full, chunk

            def rows_of(p, h, count):
                return pl.ds(pl.multiple_of(p * chunk + h * (chunk // 2), 16), count)

            super().__init__(
                sems,
                lambda p: full.at[pl.ds(1, parts - 1), rows_of(p, 0, chunk), :],
                lambda p, h: full.at[pl.ds(1, parts - 1), rows_of(p, h, chunk // 2), :],
            )
            self.here = rows_of(d, 0, chunk)

        def deep(self):
            self.z = go(
                [
                    remote(
                        self.own.at[self.here],
                        self.full.at[parts - k, self.here],
                        self.sems,
                        k,
                        deep(k),
                    )
                    for k in range(1, parts)
                ]
            )

        def one(self):
            arrive(self.z)
            super().one()

    out_w = Weights(n.sems_f.at[0], n.row_weights.at[0], n.full_out)
    branch_w = Weights(n.sems_f.at[1], n.row_weights.at[1], n.full_branch)
    gate_w = Weights(n.sems_f.at[2], n.col_weights.at[4], n.full_gate)
    query_w = Weights(n.sems_f.at[3], n.col_weights.at[3], n.full_query)
    keys_w = Weights(n.sems_f.at[4], n.mem_keys, n.full_keys)

    def small_gather(first, last, slot):
        ref = n.small.at[m, pl.ds(first * rank, (last - first) * rank)]
        return go([remote(ref, ref, n.sems_z.at[0], slot + k, deep(k)) for k in range(1, parts)])

    out_w.deep()
    small_z = small_gather(0, 1, 0)
    i_z = go(
        [
            remote(n.picks_own, n.ids_t.at[d, pick_rows, :], n.sems_i, k, deep(k))
            for k in range(1, parts)
        ]
    )
    n.ids_t[d, pick_rows, :] = n.picks_own[...]

    inputs = n.block_in[...].astype(floating)
    down_in.wait()
    gain_one, gain_two = n.norm_gains[0:1, :], n.norm_gains[1:2, :]
    scale_one = lax.rsqrt(jnp.mean(inputs * inputs, axis=1, keepdims=True) + EPSILON)
    normed_one = (inputs * scale_one * gain_one).astype(brain)
    n.normed_one[...] = normed_one
    down_att = jnp.concatenate([n.col_down[j, adapter] for j in range(3)], axis=0)
    down_mem = jnp.concatenate([n.col_down[j, adapter] for j in (3, 4)], axis=0)
    n.up_att[...] = jnp.zeros(n.up_att.shape, brain)
    n.up_mem[...] = jnp.zeros(n.up_mem.shape, brain)
    for j in range(3):
        n.up_att[j * rank : (j + 1) * rank, j * cols : (j + 1) * cols] = n.col_up[j, adapter]
    for j in range(2):
        n.up_mem[j * rank : (j + 1) * rank, j * cols : (j + 1) * cols] = n.col_up[3 + j, adapter]
    low_att = nt(normed_one, down_att).astype(brain)
    n.low_att[...] = low_att
    qkv_in.wait()
    for j in range(3):
        n.proj[:, j * cols : (j + 1) * cols] = (
            jnp.dot(normed_one, n.qkv[j], preferred_element_type=floating)
            + ADAPT_SCALE
            * jnp.dot(low_att, n.up_att[:, j * cols : (j + 1) * cols], preferred_element_type=floating)
        ).astype(brain)
    out_w.one()
    arrive(i_z)
    i_near = near_gather(n.ids_t, n.sems_i)
    segment = jnp.broadcast_to(n.segment_ids[...].astype(floating), (length, length))
    ahead = lax.broadcasted_iota(jnp.int32, (length, length), 1) <= lax.broadcasted_iota(
        jnp.int32, (length, length), 0
    )
    allowed = (segment == jnp.transpose(segment)) & ahead
    lane = lax.broadcasted_iota(jnp.int32, (length, LANES), 1)
    sides = LANES // HEAD_DIM

    def pair_of(which, pair):
        first = which * cols + pair * LANES
        return n.proj[:, first : first + LANES]

    for pair in range(heads // sides):
        query2, key2, value2 = (pair_of(w, pair) for w in range(3))
        mixed = jnp.zeros((length, LANES), floating)
        for side in range(sides):
            own = lane // HEAD_DIM == side
            logits = 0.125 * nt(jnp.where(own, query2, brain(0)), key2)
            logits = jnp.where(allowed, logits, -1e30)
            expos = jnp.exp(logits - jnp.max(logits, axis=1, keepdims=True))
            probs = expos / jnp.sum(expos, axis=1, keepdims=True)
            n.probs[pair * sides + side] = probs
            out = jnp.dot(probs.astype(brain), value2, preferred_element_type=floating)
            mixed = jnp.where(own, out, mixed)
        n.att_out[:, pair * LANES : (pair + 1) * LANES] = mixed.astype(brain)
    my_cols = pl.ds(pl.multiple_of(m * cols, LANES), cols)
    att_z = go(
        [
            remote(n.att_out, n.att_all.at[:, my_cols], n.sems_z.at[1], k, deep(k))
            for k in range(1, parts)
        ]
    )
    n.att_all[:, my_cols] = n.att_out[...]
    own_in = [
        local(n.col_weights.at[3], n.full_query.at[0], 4),
        local(n.mem_keys, n.full_keys.at[0], 5),
        local(n.row_weights.at[1], n.full_branch.at[0], 2),
        local(n.col_weights.at[4], n.full_gate.at[0], 3),
    ]
    table_in = local(n.table, n.table_v, 6)
    out_w.two()
    row_down = [n.row_down[j, adapter] for j in range(2)]
    row_up = [n.row_up[j, adapter] for j in range(2)]

    cotangent_in.wait()
    cotangent = n.cotangent[...]
    low_branch_grad = (ADAPT_SCALE * nt(cotangent, padded(row_up[1]))).astype(brain)
    n.low_branch_grad[...] = low_branch_grad
    own_in[2].wait()
    n.gated_own[...] = nt(cotangent, n.full_branch[0]) + jnp.dot(
        low_branch_grad, padded(row_down[1]), preferred_element_type=floating
    )
    out_w.three()
    arrive(i_near[:3])
    i_core = core_gather(n.ids_t, n.sems_i)
    base = (d * parts + m) * rows

    def turn(s, carry):
        local = n.ids_t[s] % 65536 - base
        here = (local >= 0) & (local < rows)
        turned = jnp.transpose(jnp.where(here, local, -1).astype(floating)).astype(jnp.int32)
        n.ids_v[pl.ds(pl.multiple_of(s * length, 16), length), :] = turned
        n.who[s] = n.ids_t[s, 0:8, 0:LANES] // 65536
        return carry

    arrive(small_z)

    def over_slots(values, full):
        total = jnp.zeros((values.shape[0], width), floating)
        for c in range(parts):
            total = total + jnp.dot(
                values[:, c * cols : (c + 1) * cols],
                full[slot_of[c]],
                preferred_element_type=floating,
            )
        return total

    out_w.done()

    def small_of(i):
        return padded(
            jnp.concatenate(
                [n.small[c, i * rank : (i + 1) * rank, :] for c in range(parts)], axis=1
            )
        )

    arrive(att_z)
    own_out_in.wait()
    att_all = n.att_all[...]
    low_out = nt(att_all, small_of(0)).astype(brain)
    n.low_out[...] = low_out
    resid = (
        n.block_in[...].astype(floating)
        + over_slots(att_all, n.full_out)
        + ADAPT_SCALE * jnp.dot(low_out, padded(row_up[0]), preferred_element_type=floating)
    )
    n.resid[...] = resid
    scale_two = lax.rsqrt(jnp.mean(resid * resid, axis=1, keepdims=True) + EPSILON)
    normed_two = (resid * scale_two * gain_two).astype(brain)
    n.normed_two[...] = normed_two

    own_in[0].wait()
    own_in[1].wait()
    low_mem = nt(normed_two, down_mem).astype(brain)
    n.low_mem[...] = low_mem
    mem_query = (
        jnp.dot(normed_two, n.full_query[0], preferred_element_type=floating)
        + ADAPT_SCALE * jnp.dot(low_mem, n.up_mem[:, :cols], preferred_element_type=floating)
    ).astype(brain)
    sub_one = nt(mem_query[:, :half_width], n.full_keys[0, :subs])
    sub_two = nt(mem_query[:, half_width:], n.full_keys[0, subs:])
    wide = n.pick_wide[...]

    def chosen(table, index):
        found = jnp.zeros(index.shape, floating)
        for c in range(subs // LANES):
            taken = jnp.take_along_axis(
                table[:, c * LANES : (c + 1) * LANES],
                index % LANES,
                axis=1,
                mode="promise_in_bounds",
            )
            found = jnp.where(index // LANES == c, taken, found)
        return found

    scores = chosen(sub_one, wide // subs) + chosen(sub_two, wide % subs)
    scores = jnp.where(lane < picks_here, scores, -1e30)
    expos = jnp.exp(scores - jnp.max(scores, axis=1, keepdims=True))
    weights = expos / jnp.sum(expos, axis=1, keepdims=True)
    n.weights_own[...] = jnp.transpose(weights)[:picks_here].astype(brain)
    w_z = go(
        [
            remote(n.weights_own, n.w_all.at[d, pick_rows, :], n.sems_w, k, deep(k))
            for k in range(1, parts)
        ]
    )
    n.w_all[d, pick_rows, :] = n.weights_own[...]
    own_in[3].wait()
    gate_pre = jnp.dot(
        normed_two, n.full_gate[0], preferred_element_type=floating
    ) + ADAPT_SCALE * jnp.dot(low_mem, n.up_mem[:, cols:], preferred_element_type=floating)
    sigma = 1.0 / (1.0 + jnp.exp(-gate_pre))
    n.grads_own[...] = (n.gated_own[...] * (gate_pre * sigma)).astype(brain)

    def seq_rows(s):
        return pl.ds(pl.multiple_of(s * length, 16), length)

    g_z = go(
        [
            remote(n.grads_own, n.g_all.at[seq_rows(d), my_cols], n.sems_g, k, deep(k))
            for k in range(1, parts)
        ]
    )
    n.g_all[seq_rows(d), my_cols] = n.grads_own[...]
    arrive(i_near[3:])
    arrive(i_core)
    lax.fori_loop(0, seqs, turn, 0)

    block = n.lo_s.shape[0]
    pad = n.tiles.shape[0] // block

    per_seq = length // block

    def build(i, carry):
        order = i // per_seq
        mask = (2 * order) % seqs + (2 * order) // seqs
        seq = sum(((d // b + mask // b) % 2) * b for b in (1, 2, 4))
        first = (i % per_seq) * block
        here = pl.ds(pl.multiple_of(seq * length + first, block), block)
        local = n.ids_v[here, :]
        n.lo_s[...] = jnp.where(local < 0, 0, local & (LANES - 1)).astype(floating)
        n.hi_s[...] = (local >> 7).astype(floating)
        w_t = n.w_all[seq, :, pl.ds(pl.multiple_of(first, block), block)]
        n.w_s[...] = jnp.transpose(w_t.astype(floating))
        hot_rows(n.lo_s, n.hi_s, n.w_s, n.tiles, block, pad)
        for a in range(rows // LANES):
            n.spread_v[here, a * LANES : (a + 1) * LANES] = n.tiles[
                pl.ds(a, block, stride=pad), :
            ].astype(brain)
        return carry

    blocks = seqs * per_seq
    grads_g = Plane(
        n.sems_g,
        lambda s: n.g_all.at[seq_rows(s)],
        lambda s, h: n.g_all.at[pl.ds(pl.multiple_of(s * length + h * half, 16), half)],
    )
    arrive(w_z)
    w_near = near_gather(n.w_all, n.sems_w)
    lax.fori_loop(0 * per_seq, 1 * per_seq, build, 0)
    arrive(w_near[:3])
    w_core = core_gather(n.w_all, n.sems_w)
    lax.fori_loop(1 * per_seq, 2 * per_seq, build, 0)
    arrive(w_near[3:])
    arrive(w_core)
    lax.fori_loop(2 * per_seq, 3 * per_seq, build, 0)
    arrive(g_z)
    grads_g.one()
    branch_w.deep()
    lax.fori_loop(3 * per_seq, 4 * per_seq, build, 0)
    gate_w.deep()
    small_z = small_gather(1, 4, 4)
    lax.fori_loop(4 * per_seq, 5 * per_seq, build, 0)
    query_w.deep()
    keys_w.deep()
    branch_w.one()
    lax.fori_loop(5 * per_seq, 6 * per_seq, build, 0)
    lax.fori_loop(6 * per_seq, 7 * per_seq, build, 0)
    grads_g.two()
    lax.fori_loop(7 * per_seq, 8 * per_seq, build, 0)
    gate_w.one()
    branch_w.two()

    table_in.wait()
    sib_core = core % 2

    def partial_of(seq):
        return jnp.dot(
            n.spread_v[seq_rows(seq), :], n.table_v[...], preferred_element_type=floating
        ).astype(brain)

    to_core = []
    for i, chip in enumerate((chip_d, chip_x, chip_y, mine)):
        n.part_sib[chip] = partial_of(2 * chip + sib_core)
        to_core += go(
            [remote(n.part_sib.at[chip], n.got_core.at[chip], n.sems_m.at[0], i, at(core))]
        )

    steps = 2
    piece = half // steps

    def spot(t, side):
        return pl.ds(t * 2 * piece + side * piece, piece)

    def stretch(t):
        return pl.ds(t * 2 * piece, 2 * piece)

    def add_to(chip, where, *got):
        total = n.part_own[chip, where].astype(floating)
        for more in got:
            total = total + more.astype(floating)
        n.part_own[chip, where] = total.astype(brain)

    def plane_move(t, i, chip, side, got, slot, to):
        return remote(
            n.part_own.at[chip, spot(t, side)],
            got.at[slot, t],
            n.sems_m.at[1 + t],
            i,
            at(to),
        )

    def plane_one(t):
        return go(
            [
                plane_move(t, 0, chip_d, 0, n.got_x, 0, x_side),
                plane_move(t, 1, chip_d, 1, n.got_y, 0, y_side),
                plane_move(t, 2, chip_x, 0, n.got_x, 1, x_side),
                plane_move(t, 3, chip_y, 1, n.got_y, 1, y_side),
            ]
        )

    def plane_two(t, one):
        arrive(one[:2])
        add_to(chip_y, spot(t, 0), n.got_x[0, t])
        add_to(chip_x, spot(t, 1), n.got_y[0, t])
        return go(
            [
                plane_move(t, 4, chip_x, 1, n.got_x, 2, x_side),
                plane_move(t, 5, chip_y, 0, n.got_y, 2, y_side),
            ]
        )

    def cols_of(k):
        return pl.ds(pl.multiple_of(z_of[k] * cols, LANES), cols)

    def plane_done(t, one, two):
        arrive(one[2:])
        arrive(two)
        add_to(mine, spot(t, 0), n.got_x[1, t], n.got_y[2, t])
        add_to(mine, spot(t, 1), n.got_x[2, t], n.got_y[1, t])
        return go(
            [
                remote(
                    n.part_own.at[mine, stretch(t), cols_of(k)],
                    n.got_z.at[k - 1, stretch(t)],
                    n.sems_m.at[1 + t],
                    5 + k,
                    deep(k),
                )
                for k in range(1, parts)
            ]
        )

    def spread_memory(t, moved):
        arrive(moved)
        memory = n.part_own[mine, stretch(t), my_cols].astype(floating)
        for k in range(parts - 1):
            memory = memory + n.got_z[k, stretch(t)].astype(floating)
        n.mem_own[stretch(t)] = memory.astype(brain)
        n.mem_all[stretch(t), my_cols] = n.mem_own[stretch(t)]
        return go(
            [
                remote(
                    n.mem_own.at[stretch(t)],
                    n.mem_all.at[stretch(t), my_cols],
                    n.sems_z.at[3],
                    4 * t + k,
                    deep(k),
                )
                for k in range(1, parts)
            ]
        )

    for i, chip in enumerate((chip_d, chip_x, chip_y, mine)):
        n.part_own[chip] = partial_of(2 * chip + d % 2)
        arrive(to_core[i : i + 1])
        add_to(chip, slice(None), n.got_core[chip])
        if i == 2:
            one_0 = plane_one(0)

    grads_g.three()
    def answers_of(seq):
        n.all_s[:, :rows] = nt(n.g_all[seq_rows(seq), :], n.table_v[...])
        local = n.ids_v[seq_rows(seq), :]
        lo, hi = jnp.where(local < 0, 0, local & (LANES - 1)), local >> 7
        total = jnp.zeros((length, picks), floating)
        for a in range(rows // LANES):
            found = jnp.take_along_axis(
                n.all_s[:, a * LANES : (a + 1) * LANES], lo, axis=1, mode="promise_in_bounds"
            )
            total = jnp.where(hi == a, found, total)
        return jnp.transpose(total).astype(brain)

    def answers_for(order, held, side):
        def body(i, carry):
            chip = sum(((d // (2 * b) + i // b) % 2) * b for b in (1, 2))
            held[chip] = answers_of(2 * chip + side)
            return carry

        lax.fori_loop(*order, body, 0)

    arrive(grads_g.a[2:] + grads_g.b[2:])
    answers_for((0, 3), n.ans_sib, sib_core)
    two_0 = plane_two(0, one_0)
    one_1 = plane_one(1)
    branch_w.three()
    gate_w.two()
    arrive(grads_g.c)
    answers_for((3, 4), n.ans_sib, sib_core)
    a_core = go([remote(n.ans_sib, n.ans_core, n.sems_a, 0, at(core))])
    answers_for((0, 1), n.ans_own, d % 2)
    m_0 = plane_done(0, one_0, two_0)
    query_w.one()
    keys_w.one()
    gate_w.three()
    answers_for((1, 2), n.ans_own, d % 2)
    two_1 = plane_two(1, one_1)
    answers_for((2, 4), n.ans_own, d % 2)
    arrive(a_core)
    n.ans_own[...] = (n.ans_own[...].astype(floating) + n.ans_core[...].astype(floating)).astype(
        brain
    )
    a_plane = go(
        [
            remote(n.ans_own.at[chip], n.ans_plane.at[i], n.sems_a, 1 + i, at(p))
            for i, (chip, p) in enumerate(((chip_x, x_side), (chip_y, y_side), (chip_d, corner)))
        ]
    )
    m_1 = plane_done(1, one_1, two_1)
    mem_0 = spread_memory(0, m_0)
    query_w.two()
    keys_w.two()

    tg_block = n.tg_v.shape[1]
    tg_steps = rows // tg_block

    def tg_out(i):
        return pltpu.make_async_copy(
            n.tg_v.at[i % 2],
            n.table_grad.at[pl.ds(i * tg_block, tg_block)],
            n.local_sems.at[7 + i % 2],
        )

    def table_grad_steps(first, last):
        for i in range(first, last):
            if i >= 2:
                tg_out(i - 2).wait()
            n.tg_v[i % 2] = tn(
                n.spread_v[:, i * tg_block : (i + 1) * tg_block], n.g_all[...]
            ).astype(brain)
            tg_out(i).start()

    weave = iter(range(tg_steps))

    def table_grad_some(count):
        for _ in range(count):
            i = next(weave)
            table_grad_steps(i, i + 1)

    table_grad_some(0)
    arrive(a_plane)
    answered = n.ans_own[mine].astype(floating)
    for k in range(3):
        answered = answered + n.ans_plane[k].astype(floating)
    n.ans_own[mine] = answered.astype(brain)
    a_z = go(
        [remote(n.ans_own.at[mine], n.ans_z.at[k - 1], n.sems_a, 3 + k, deep(k)) for k in range(1, parts)]
    )
    query_w.three()
    keys_w.three()
    arrive(small_z)
    table_grad_some(0)
    mem_1 = spread_memory(1, m_1)
    arrive(a_z)
    weight_grad = n.ans_own[mine].astype(floating)
    for k in range(parts - 1):
        weight_grad = weight_grad + n.ans_z[k].astype(floating)
    weights_t = n.w_all[d].astype(floating)
    for h in range(parts):
        here = slice(h * picks_here, (h + 1) * picks_here)
        weighed = weights_t[here] * weight_grad[here]
        n.score_f[here, :] = weighed - weights_t[here] * jnp.sum(weighed, axis=0, keepdims=True)
    rows_picked = n.ids_t[d] % 65536
    n.first_t[...] = (rows_picked // subs).astype(floating)
    n.second_t[...] = (rows_picked % subs).astype(floating)
    sub_block = subs // 2

    def gather_subs(head, carry):
        for top in range(0, subs, sub_block):
            key_at = (
                (lax.broadcasted_iota(jnp.int32, (sub_block, length), 0) + top)
                .astype(floating)
                .astype(brain)
            )
            ones = jnp.zeros((sub_block, length), brain)
            twos = jnp.zeros((sub_block, length), brain)
            for p in range(picks_here):
                row = pl.ds(head * picks_here + p, 1)
                score = jnp.broadcast_to(n.score_f[row, :], key_at.shape).astype(brain)
                one = jnp.broadcast_to(n.first_t[row, :], key_at.shape).astype(brain)
                two = jnp.broadcast_to(n.second_t[row, :], key_at.shape).astype(brain)
                ones = ones + jnp.where(key_at == one, score, brain(0))
                twos = twos + jnp.where(key_at == two, score, brain(0))
            n.sub_grads[0, top : top + sub_block, :] = ones
            n.sub_grads[1, top : top + sub_block, :] = twos
        for i in range(2):
            first = pl.multiple_of(head * cols + i * half_width, LANES)
            n.query_grad[:, pl.ds(first, half_width)] = tn(
                n.sub_grads[i], n.full_keys[lax.rem(head - m + parts, parts), i * subs : (i + 1) * subs]
            ).astype(brain)
        return carry

    keys_w.done()
    lax.fori_loop(0, parts, gather_subs, 0)
    branch_w.done()
    gate_w.done()
    cotangent = n.cotangent[...]
    normed_two = n.normed_two[...]
    low_branch_grad = n.low_branch_grad[...]
    low_mem = n.low_mem[...]
    for c in range(parts):
        n.all_s[:, c * cols : (c + 1) * cols] = nt(
            cotangent, n.full_branch[slot_of[c]]
        ) + jnp.dot(
            low_branch_grad,
            padded(n.small[c, 3 * rank : 4 * rank, :]),
            preferred_element_type=floating,
        )
    for c in range(parts):
        n.all_s[:, width + c * cols : width + (c + 1) * cols] = jnp.dot(
            normed_two, n.full_gate[slot_of[c]], preferred_element_type=floating
        ) + ADAPT_SCALE * jnp.dot(
            low_mem[:, rank:],
            n.small[c, 2 * rank : 3 * rank, :],
            preferred_element_type=floating,
        )
    table_grad_some(0)
    arrive(mem_0)
    arrive(mem_1)
    for c in range(parts):
        here = slice(c * cols, (c + 1) * cols)
        memory = n.mem_all[:, here].astype(floating)
        gate_pre = n.all_s[:, width + c * cols : width + (c + 1) * cols]
        sigma = 1.0 / (1.0 + jnp.exp(-gate_pre))
        n.gated[:, here] = (memory * (gate_pre * sigma)).astype(brain)
        n.gate_grad[:, here] = (
            n.all_s[:, here] * memory * (sigma * (1.0 + gate_pre * (1.0 - sigma)))
        ).astype(brain)
    query_w.done()
    query_grad, gate_grad, gated = n.query_grad[...], n.gate_grad[...], n.gated[...]
    low_mem_grads = [
        (ADAPT_SCALE * nt(grads, small_of(1 + i))).astype(brain)
        for i, grads in enumerate((query_grad, gate_grad))
    ]
    two_grad = jnp.dot(
        low_mem_grads[0], padded(n.col_down[3, adapter]), preferred_element_type=floating
    ) + jnp.dot(low_mem_grads[1], padded(n.col_down[4, adapter]), preferred_element_type=floating)
    for c in range(parts):
        here = slice(c * cols, (c + 1) * cols)
        two_grad = two_grad + nt(query_grad[:, here], n.full_query[slot_of[c]])
        two_grad = two_grad + nt(gate_grad[:, here], n.full_gate[slot_of[c]])
    resid = n.resid[...]
    scale_two = lax.rsqrt(jnp.mean(resid * resid, axis=1, keepdims=True) + EPSILON)
    weighted = gain_two * two_grad
    resid_grad = (
        cotangent.astype(floating)
        + scale_two * weighted
        - resid * scale_two**3 * jnp.mean(resid * weighted, axis=1, keepdims=True)
    )
    n.all_s[:, :width] = resid_grad
    branch_grad = resid_grad.astype(brain)
    n.att_all[...] = branch_grad

    low_out_grad = (ADAPT_SCALE * nt(branch_grad, padded(row_up[0]))).astype(brain)
    att_out_grad = (
        nt(branch_grad, n.full_out[0])
        + jnp.dot(low_out_grad, padded(row_down[0]), preferred_element_type=floating)
    ).astype(brain)
    for pair in range(heads // sides):
        query2, key2, value2 = (pair_of(w, pair) for w in range(3))
        out2 = att_out_grad[:, pair * LANES : (pair + 1) * LANES]
        grads2 = [jnp.zeros((length, LANES), floating)] * 3
        for side in range(sides):
            own = lane // HEAD_DIM == side
            probs = n.probs[pair * sides + side]
            prob_grad = nt(jnp.where(own, out2, brain(0)), value2)
            logit_grad = (
                probs * (prob_grad - jnp.sum(probs * prob_grad, axis=1, keepdims=True))
            ).astype(brain)
            made = (
                0.125 * jnp.dot(logit_grad, key2, preferred_element_type=floating),
                0.125 * tn(logit_grad, query2),
                tn(probs.astype(brain), out2),
            )
            grads2 = [jnp.where(own, new, old) for new, old in zip(made, grads2)]
        for w in range(3):
            first = w * cols + pair * LANES
            n.proj_grad[:, first : first + LANES] = grads2[w].astype(brain)
    proj_grad = n.proj_grad[...]
    low_att_part = ADAPT_SCALE * nt(proj_grad, padded(n.up_att[...]))
    one_part = jnp.dot(low_att_part.astype(brain), padded(down_att), preferred_element_type=floating)
    for j in range(3):
        one_part = one_part + nt(n.proj_grad[:, j * cols : (j + 1) * cols], n.qkv[j])
    n.sum_send[:, :, :width] = one_part.astype(brain).reshape(parts, quarter, width)
    n.sum_send[:, :, width:] = low_att_part.astype(brain).reshape(parts, quarter, SIDE)
    last = quarter // 2

    def tail_rows(h):
        return pl.ds(h * last, last)

    r_one = [
        go(
            [
                remote(
                    n.sum_send.at[z_of[k], tail_rows(h)],
                    n.sum_got.at[k - 1, tail_rows(h)],
                    n.sems_z.at[4],
                    4 * h + k,
                    deep(k),
                )
                for k in range(1, parts)
            ]
        )
        for h in range(2)
    ]

    branch_grad, gated = n.att_all[...], n.gated[...]
    low_branch = nt(gated, small_of(3)).astype(brain)
    branch = over_slots(gated, n.full_branch)
    branch = branch + ADAPT_SCALE * jnp.dot(
        low_branch, padded(row_up[1]), preferred_element_type=floating
    )
    n.block_out[...] = (n.resid[...] + branch).astype(brain)
    n.early[d, 3 * rank :, :] = (ADAPT_SCALE * tn(low_branch, n.cotangent[...]))[:rank].astype(brain)
    up_att_grad = ADAPT_SCALE * tn(n.low_att[...], proj_grad)
    for j in range(3):
        n.narrow[d, j * rank : (j + 1) * rank, :] = up_att_grad[
            j * rank : (j + 1) * rank, j * cols : (j + 1) * cols
        ].astype(brain)
    for j, grads in enumerate((n.query_grad, n.gate_grad)):
        n.narrow[d, (3 + j) * rank : (4 + j) * rank, :] = (
            ADAPT_SCALE * tn(n.low_mem[...], grads[:, my_cols])
        )[j * rank : (j + 1) * rank].astype(brain)
    n.narrow[d, 5 * rank : 6 * rank, :] = tn(low_out_grad, n.att_out[...])[:rank].astype(brain)
    n.narrow[d, 6 * rank : 7 * rank, :] = tn(n.low_branch_grad[...], n.gated[:, my_cols])[
        :rank
    ].astype(brain)
    for j in range(2):
        n.early[d, j * rank : (j + 1) * rank, :] = tn(low_mem_grads[j], n.normed_two[...])[
            :rank
        ].astype(brain)
    n.early[d, 2 * rank : 3 * rank, :] = (ADAPT_SCALE * tn(n.low_out[...], branch_grad))[
        :rank
    ].astype(brain)
    n_near = near_gather(n.narrow, n.sems_b.at[0])
    e_near = near_gather(n.early, n.sems_b.at[1])
    table_grad_some(4)
    q_low_att, q_in = [], []
    for h in range(2):
        arrive(r_one[h])
        total = n.sum_send[m, tail_rows(h)].astype(floating)
        for k in range(parts - 1):
            total = total + n.sum_got[k, tail_rows(h)].astype(floating)
        n.gath_low[m, tail_rows(h)] = total[:, width:].astype(brain)
        my_rows = pl.ds(pl.multiple_of(m * quarter + h * last, 16), last)
        weighted = gain_one * total[:, :width]
        inputs = n.block_in[my_rows, :].astype(floating)
        scale_one = lax.rsqrt(jnp.mean(inputs * inputs, axis=1, keepdims=True) + EPSILON)
        n.gath_in[m, tail_rows(h)] = (
            n.all_s[my_rows, :width]
            + scale_one * weighted
            - inputs * scale_one**3 * jnp.mean(inputs * weighted, axis=1, keepdims=True)
        ).astype(brain)
        for ref, sems, out in ((n.gath_low, n.sems_z.at[5], q_low_att), (n.gath_in, n.sems_z.at[6], q_in)):
            view = ref.at[m, tail_rows(h)]
            out += go([remote(view, view, sems, 4 * h + k, deep(k)) for k in range(1, parts)])
    arrive(n_near[:3])
    arrive(e_near[:3])
    n_core = core_gather(n.narrow, n.sems_b.at[0])
    e_core = core_gather(n.early, n.sems_b.at[1])
    arrive(q_low_att)
    low_att_grad = n.gath_low[...].reshape(length, SIDE)
    n.late[d] = tn(low_att_grad, n.normed_one[...])[: 3 * rank].astype(brain)
    l_near = near_gather(n.late, n.sems_b.at[2])
    table_grad_some(4)
    arrive(n_near[3:] + e_near[3:] + n_core + e_core)
    arrive(l_near[:3])
    l_core = core_gather(n.late, n.sems_b.at[2])
    arrive(l_near[3:])
    arrive(l_core)

    def place(a, carry):
        wide_late = jnp.zeros(n.late.shape[1:], brain)
        wide_early = jnp.zeros(n.early.shape[1:], brain)
        thin = jnp.zeros(n.narrow.shape[1:], brain)
        for s in range(seqs):
            is_it = (n.who[s, 0:1, 0:1] == a).astype(floating).astype(brain)
            wide_late = wide_late + n.late[s] * is_it
            wide_early = wide_early + n.early[s] * is_it
            thin = thin + n.narrow[s] * is_it
        for j in range(3):
            n.col_down_grad[j, a] = wide_late[j * rank : (j + 1) * rank]
            n.col_up_grad[j, a] = thin[j * rank : (j + 1) * rank]
        for j in range(2):
            n.col_down_grad[3 + j, a] = wide_early[j * rank : (j + 1) * rank]
            n.col_up_grad[3 + j, a] = thin[(3 + j) * rank : (4 + j) * rank]
            n.row_down_grad[j, a] = thin[(5 + j) * rank : (6 + j) * rank]
            n.row_up_grad[j, a] = wide_early[(2 + j) * rank : (3 + j) * rank]
        return carry

    lax.fori_loop(0, n.col_down.shape[1], place, 0)
    arrive(q_in)
    n.input_grad[...] = n.gath_in[...].reshape(length, width)
    for i in range(max(tg_steps - 2, 0), tg_steps):
        tg_out(i).wait()
    for c in sent:
        c.wait_send()


def whole_block(args, seqs, parts):
    floating, brain, whole = jnp.float32, jnp.bfloat16, jnp.int32
    given = Refs()
    given.__dict__.update(args)
    length, width = given.block_in.shape
    rows = given.table.shape[0]
    cols, quarter = width // parts, length // parts
    picks_here = given.pick_ids.shape[1]
    picks = picks_here * parts
    rank = given.col_down_in.shape[2]
    subs = given.mem_keys.shape[0] // 2
    tokens = seqs * length
    block, tg_block = 128, 256
    pad = max(rows // LANES, 16)
    vmem = pl.BlockSpec(memory_space=pltpu.VMEM)
    anywhere = pl.BlockSpec(memory_space=pl.ANY)
    inside = dict(
        adapter_ids=pl.BlockSpec(memory_space=pltpu.SMEM),
        block_in=vmem,
        norm_gains=vmem,
        segment_ids=vmem,
        pick_ids=vmem,
    )
    outs = dict(
        block_out=((length, width), brain),
        input_grad=((length, width), brain),
        table_grad=((rows, width), brain),
        col_down_grad=(given.col_down_in.shape, brain),
        col_up_grad=(given.col_up_in.shape, brain),
        row_down_grad=(given.row_down_in.shape, brain),
        row_up_grad=(given.row_up_in.shape, brain),
    )
    chips = seqs // 2
    scratch = dict(
        table_v=((rows, width), brain),
        pick_wide=((length, LANES), whole),
        picks_own=((picks_here, length), whole),
        ids_t=((seqs, picks, length), whole),
        ids_v=((tokens, picks), whole),
        who=((seqs, 8, LANES), whole),
        normed_one=((length, width), brain),
        up_att=((3 * rank, 3 * cols), brain),
        up_mem=((2 * rank, 2 * cols), brain),
        low_att=((length, 3 * rank), brain),
        low_mem=((length, 2 * rank), brain),
        proj=((length, 3 * cols), brain),
        proj_grad=((length, 3 * cols), brain),
        probs=((cols // HEAD_DIM, length, length), floating),
        att_out=((length, cols), brain),
        sum_send=((parts, quarter, width + SIDE), brain),
        sum_got=((parts - 1, quarter, width + SIDE), brain),
        qkv=((3, width, cols), brain),
        col_down=(given.col_down_in.shape, brain),
        col_up=(given.col_up_in.shape, brain),
        row_down=(given.row_down_in.shape, brain),
        row_up=(given.row_up_in.shape, brain),
        cotangent=((length, width), brain),
        full_out=((parts, cols, width), brain),
        full_branch=((parts, cols, width), brain),
        full_gate=((parts, width, cols), brain),
        full_query=((parts, width, cols), brain),
        full_keys=((parts, *given.mem_keys.shape), brain),
        small=((parts, 4 * rank, cols), brain),
        att_all=((length, width), brain),
        low_out=((length, SIDE), brain),
        normed_two=((length, width), brain),
        gated=((length, width), brain),
        gate_grad=((length, width), brain),
        query_grad=((length, width), brain),
        mem_own=((length, cols), brain),
        mem_all=((length, width), brain),
        score_f=((picks, length), floating),
        sub_grads=((2, subs, length), brain),
        low_branch_grad=((length, SIDE), brain),
        gated_own=((length, cols), floating),
        resid=((length, width), floating),
        gath_in=((parts, quarter, width), brain),
        gath_low=((parts, quarter, SIDE), brain),
        weights_own=((picks_here, length), brain),
        w_all=((seqs, picks, length), brain),
        grads_own=((length, cols), brain),
        g_all=((tokens, width), brain),
        spread_v=((tokens, rows), brain),
        tiles=((block * pad, LANES), floating),
        lo_s=((block, picks), floating),
        hi_s=((block, picks), floating),
        w_s=((block, picks), floating),
        part_own=((chips, length, width), brain),
        part_sib=((chips, length, width), brain),
        got_core=((chips, length, width), brain),
        got_x=((3, 2, length // 4, width), brain),
        got_y=((3, 2, length // 4, width), brain),
        got_z=((parts - 1, length, cols), brain),
        ans_own=((chips, picks, length), brain),
        ans_sib=((chips, picks, length), brain),
        ans_core=((chips, picks, length), brain),
        ans_plane=((3, picks, length), brain),
        ans_z=((parts - 1, picks, length), brain),
        all_s=((length, max(rows, 2 * width)), floating),
        tg_v=((2, tg_block, width), brain),
        first_t=((picks, length), floating),
        second_t=((picks, length), floating),
        narrow=((seqs, 7 * rank, cols), brain),
        early=((seqs, 4 * rank, width), brain),
        late=((seqs, 3 * rank, width), brain),
    )
    semaphores = dict(
        local_sems=(14,),
        sems_i=(2, 12),
        sems_w=(2, 12),
        sems_g=(2, 12),
        sems_m=(3, 2, 10),
        sems_a=(2, 8),
        sems_z=(9, 2, 8),
        sems_f=(5, 2, 12),
        sems_b=(3, 2, 12),
    )
    names = [*args, *outs, *scratch, *semaphores]
    return pl.pallas_call(
        functools.partial(block_kernel, names, seqs, parts),
        in_specs=[inside.get(name, anywhere) for name in args],
        out_specs=[anywhere if name == "table_grad" else vmem for name in outs],
        out_shape=[jax.ShapeDtypeStruct(*made) for made in outs.values()],
        scratch_shapes=[pltpu.VMEM(*made) for made in scratch.values()]
        + [pltpu.SemaphoreType.DMA(shape) for shape in semaphores.values()],
        compiler_params=pltpu.CompilerParams(
            collective_id=0, has_side_effects=True, vmem_limit_bytes=63 * 2**20
        ),
        name="whole_block",
    )(*args.values())


def pick_scores(picks, first, second, sub_count):
    columns = jnp.arange(sub_count, dtype=jnp.int32)
    hit_first = (picks // sub_count)[:, :, None] == columns
    hit_second = (picks % sub_count)[:, :, None] == columns
    scores = jnp.sum(jnp.where(hit_first, first[:, None, :], 0.0), axis=2)
    scores = scores + jnp.sum(jnp.where(hit_second, second[:, None, :], 0.0), axis=2)
    return (jax.nn.softmax(scores, axis=-1), hit_first, hit_second)


def per_device(
    block_in,
    cotangent,
    norm_gains,
    col_weights,
    row_weights,
    mem_keys,
    value_table,
    col_down,
    col_up,
    row_down,
    row_up,
    segment_ids,
    adapter_ids,
    pick_ids,
):
    floating = jnp.float32
    brain = jnp.bfloat16
    length = block_in.shape[0]
    col_width = col_weights.shape[2]
    heads_here = col_width // HEAD_DIM
    rows_here = value_table.shape[0]
    pick_tok = pick_ids[:, 0, :]
    query_rows = min(512, length)
    query_blocks = length // query_rows
    sub_count = mem_keys.shape[2]
    half_width = mem_keys.shape[3]
    adapter = adapter_ids[0]
    down_col = lax.dynamic_index_in_dim(col_down, adapter, 1, keepdims=False)
    up_col = lax.dynamic_index_in_dim(col_up, adapter, 1, keepdims=False)
    down_row = lax.dynamic_index_in_dim(row_down, adapter, 1, keepdims=False)
    up_row = lax.dynamic_index_in_dim(row_up, adapter, 1, keepdims=False)
    gain_one = norm_gains[0]
    gain_two = norm_gains[1]
    first_keys = mem_keys[0, 0]
    second_keys = mem_keys[1, 0]
    segments = segment_ids[0]
    positions = jnp.arange(length, dtype=jnp.int32)
    inputs = block_in.astype(floating)
    scale_one = rms_scale(inputs)
    normed_one = (inputs * scale_one * gain_one).astype(brain)
    low_att = jnp.einsum(
        "td,jrd->jtr", normed_one, down_col[:3], preferred_element_type=floating
    ).astype(brain)
    projected = jnp.einsum(
        "td,jde->jte", normed_one, col_weights[:3], preferred_element_type=floating
    )
    projected = projected + ADAPT_SCALE * jnp.einsum(
        "jtr,jre->jte", low_att, up_col[:3], preferred_element_type=floating
    )
    projected = projected.astype(brain)
    queries = projected[0].reshape(length, heads_here, HEAD_DIM)
    keys_here = projected[1].reshape(length, heads_here, HEAD_DIM)
    values_here = projected[2].reshape(length, heads_here, HEAD_DIM)

    def block_logits(start):
        rows_pos = start + jnp.arange(query_rows, dtype=jnp.int32)
        allowed = (segments[:, None] == segments[None, :]) & (
            positions[None, :] <= rows_pos[:, None]
        )
        logits = (
            jnp.einsum("thd,shd->hts", queries, keys_here, preferred_element_type=floating) * 0.125
        )
        return (queries, allowed, jnp.where(allowed[None], logits, -1e30))

    def attend(index):
        query_blk, allowed, logits = block_logits(index * query_rows)
        peak = jnp.max(logits, axis=-1, keepdims=True)
        expos = jnp.exp(logits - peak)
        total = jnp.sum(expos, axis=-1, keepdims=True)
        probs = expos / total
        mixed = jnp.einsum(
            "hts,shd->thd", probs.astype(brain), values_here, preferred_element_type=floating
        )
        return (
            mixed.reshape(query_rows, col_width).astype(brain),
            (peak + jnp.log(total))[:, :, 0],
        )

    att_out, log_totals = lax.map(attend, jnp.arange(query_blocks))
    att_out = att_out.reshape(length, col_width)
    att_part = matmul(att_out, row_weights[0])
    low_part = matmul_nt(att_out, down_row[0])
    att_sum, low_sum = lax.psum((att_part, low_part), "mp")
    low_out = low_sum.astype(brain)
    resid = inputs + att_sum + ADAPT_SCALE * matmul(low_out, up_row[0])
    scale_two = rms_scale(resid)
    normed_two = (resid * scale_two * gain_two).astype(brain)
    low_mem = jnp.einsum(
        "td,jrd->jtr", normed_two, down_col[3:], preferred_element_type=floating
    ).astype(brain)
    mem_query = (
        matmul(normed_two, col_weights[3]) + ADAPT_SCALE * matmul(low_mem[0], up_col[3])
    ).astype(brain)
    gate_pre = matmul(normed_two, col_weights[4]) + ADAPT_SCALE * matmul(low_mem[1], up_col[4])
    first_sub = matmul_nt(mem_query[:, :half_width], first_keys)
    second_sub = matmul_nt(mem_query[:, half_width:], second_keys)

    everyone = ("dp", "mp")
    base = (
        (lax.axis_index("dp") * lax.axis_size("mp") + lax.axis_index("mp")) * rows_here
    ).reshape(1)
    ids_all = lax.all_gather(
        lax.all_gather(pick_tok, "mp", axis=1, tiled=True), "dp", axis=0, tiled=True
    )
    weights, hit_first, hit_second = pick_scores(pick_tok, first_sub, second_sub, sub_count)
    weights_all = lax.all_gather(
        lax.all_gather(weights.astype(brain), "mp", axis=1, tiled=True), "dp", axis=0, tiled=True
    )
    gate_act = jax.nn.silu(gate_pre)
    low_branch_grad = (ADAPT_SCALE * matmul_nt(cotangent, up_row[1])).astype(brain)
    gated_grad = matmul_nt(cotangent, row_weights[1]) + matmul(low_branch_grad, down_row[1])
    mem_grad_cols = (gated_grad * gate_act).astype(brain)
    mem_grad = lax.all_gather(
        lax.all_gather(mem_grad_cols, "mp", axis=1, tiled=True), "dp", axis=0, tiled=True
    )
    spread_w = spread(ids_all, weights_all, base, rows_here)
    partial = matmul(spread_w, value_table).astype(brain)
    mem_cols = lax.psum_scatter(partial, "dp", scatter_dimension=0, tiled=True)
    mem_cols = lax.psum_scatter(mem_cols, "mp", scatter_dimension=1, tiled=True).astype(floating)
    answers = answer(ids_all, mem_grad, value_table, base)
    weight_grad = lax.psum_scatter(answers, "dp", scatter_dimension=0, tiled=True)
    weight_grad = lax.psum_scatter(weight_grad, "mp", scatter_dimension=1, tiled=True)
    table_grad = matmul_tn(spread_w, mem_grad)
    gated = (mem_cols * gate_act).astype(brain)
    branch_part = matmul(gated, row_weights[1])
    low_branch_part = matmul_nt(gated, down_row[1])
    branch_sum, low_branch_sum = (
        lax.psum(branch_part.astype(jnp.bfloat16), "mp").astype(jnp.float32),
        lax.psum(low_branch_part.astype(jnp.bfloat16), "mp").astype(jnp.float32),
    )
    low_branch = low_branch_sum.astype(brain)
    block_out = (resid + branch_sum + ADAPT_SCALE * matmul(low_branch, up_row[1])).astype(brain)
    out_grad = cotangent.astype(floating)
    grad_up_branch = ADAPT_SCALE * matmul_tn(low_branch, cotangent)
    grad_down_branch = matmul_tn(low_branch_grad, gated)
    gate_grad = (gated_grad * mem_cols * silu_slope(gate_pre)).astype(brain)
    score_grad = weights * (
        weight_grad - jnp.sum(weights * weight_grad, axis=-1, keepdims=True)
    )
    first_grad = jnp.sum(jnp.where(hit_first, score_grad[:, :, None], 0.0), axis=1).astype(brain)
    second_grad = jnp.sum(jnp.where(hit_second, score_grad[:, :, None], 0.0), axis=1).astype(brain)
    query_grad = jnp.concatenate(
        [matmul(first_grad, first_keys), matmul(second_grad, second_keys)], axis=1
    ).astype(brain)
    normed_two_part = matmul_nt(query_grad, col_weights[3]) + matmul_nt(gate_grad, col_weights[4])
    low_mem_part = ADAPT_SCALE * jnp.stack(
        [matmul_nt(query_grad, up_col[3]), matmul_nt(gate_grad, up_col[4])]
    )
    grad_up_mem = ADAPT_SCALE * jnp.stack(
        [matmul_tn(low_mem[0], query_grad), matmul_tn(low_mem[1], gate_grad)]
    )
    normed_two_grad, low_mem_grad = lax.psum((normed_two_part, low_mem_part), "mp")
    low_mem_grad = low_mem_grad.astype(brain)
    normed_two_grad = normed_two_grad + jnp.einsum(
        "jtr,jrd->td", low_mem_grad, down_col[3:], preferred_element_type=floating
    )
    grad_down_mem = jnp.einsum(
        "jtr,td->jrd", low_mem_grad, normed_two, preferred_element_type=floating
    )
    weighted_two = gain_two * normed_two_grad
    resid_grad = (
        out_grad
        + scale_two * weighted_two
        - resid * scale_two**3 * jnp.mean(resid * weighted_two, axis=-1, keepdims=True)
    )
    att_branch_grad = resid_grad.astype(brain)
    low_out_grad = (ADAPT_SCALE * matmul_nt(att_branch_grad, up_row[0])).astype(brain)
    grad_up_att = ADAPT_SCALE * matmul_tn(low_out, att_branch_grad)
    att_out_grad = (
        matmul_nt(att_branch_grad, row_weights[0]) + matmul(low_out_grad, down_row[0])
    ).astype(brain)
    grad_down_att = matmul_tn(low_out_grad, att_out)

    def attend_back(carry, index):
        key_acc, value_acc = carry
        start = index * query_rows
        query_blk, allowed, logits = block_logits(start)
        grad_blk = att_out_grad.reshape(query_rows, heads_here, HEAD_DIM)
        probs = jnp.where(allowed[None], jnp.exp(logits - log_totals[index][:, :, None]), 0.0)
        value_acc = value_acc + jnp.einsum(
            "hts,thd->shd", probs.astype(brain), grad_blk, preferred_element_type=floating
        )
        prob_grad = jnp.einsum(
            "thd,shd->hts", grad_blk, values_here, preferred_element_type=floating
        )
        logit_grad = (
            probs * (prob_grad - jnp.sum(probs * prob_grad, axis=-1, keepdims=True))
        ).astype(brain)
        query_part = 0.125 * jnp.einsum(
            "hts,shd->thd", logit_grad, keys_here, preferred_element_type=floating
        )
        key_acc = key_acc + 0.125 * jnp.einsum(
            "hts,thd->shd", logit_grad, query_blk, preferred_element_type=floating
        )
        return ((key_acc, value_acc), query_part.reshape(query_rows, col_width).astype(brain))

    empty = jnp.zeros((length, heads_here, HEAD_DIM), floating)
    (key_grad, value_grad), query_parts = lax.scan(
        attend_back, (empty, empty), jnp.arange(query_blocks)
    )
    proj_grad = jnp.stack(
        [
            query_parts.reshape(length, col_width),
            key_grad.reshape(length, col_width).astype(brain),
            value_grad.reshape(length, col_width).astype(brain),
        ]
    )
    normed_one_part = jnp.einsum(
        "jte,jde->td", proj_grad, col_weights[:3], preferred_element_type=floating
    )
    low_att_part = ADAPT_SCALE * jnp.einsum(
        "jte,jre->jtr", proj_grad, up_col[:3], preferred_element_type=floating
    )
    grad_up_qkv = ADAPT_SCALE * jnp.einsum(
        "jtr,jte->jre", low_att, proj_grad, preferred_element_type=floating
    )
    normed_one_grad, low_att_grad = (
        lax.psum(normed_one_part.astype(jnp.bfloat16), "mp").astype(jnp.float32),
        lax.psum(low_att_part.astype(jnp.bfloat16), "mp").astype(jnp.float32),
    )
    low_att_grad = low_att_grad.astype(brain)
    normed_one_grad = normed_one_grad + jnp.einsum(
        "jtr,jrd->td", low_att_grad, down_col[:3], preferred_element_type=floating
    )
    grad_down_qkv = jnp.einsum(
        "jtr,td->jrd", low_att_grad, normed_one, preferred_element_type=floating
    )
    weighted_one = gain_one * normed_one_grad
    input_grad = (
        resid_grad
        + scale_one * weighted_one
        - inputs * scale_one**3 * jnp.mean(inputs * weighted_one, axis=-1, keepdims=True)
    )
    chosen = (jnp.arange(col_down.shape[1], dtype=jnp.int32) == adapter).astype(floating)
    down_cols_all = (
        jnp.concatenate([grad_down_qkv, grad_down_mem], axis=0)[:, None]
        * chosen[None, :, None, None]
    )
    up_cols_all = (
        jnp.concatenate([grad_up_qkv, grad_up_mem], axis=0)[:, None] * chosen[None, :, None, None]
    )
    down_rows_all = (
        jnp.stack([grad_down_att, grad_down_branch])[:, None] * chosen[None, :, None, None]
    )
    up_rows_all = jnp.stack([grad_up_att, grad_up_branch])[:, None] * chosen[None, :, None, None]
    down_cols_sum, up_cols_sum, down_rows_sum, up_rows_sum = (
        lax.psum(down_cols_all.astype(jnp.bfloat16), "dp").astype(jnp.float32),
        lax.psum(up_cols_all.astype(jnp.bfloat16), "dp").astype(jnp.float32),
        lax.psum(down_rows_all.astype(jnp.bfloat16), "dp").astype(jnp.float32),
        lax.psum(up_rows_all.astype(jnp.bfloat16), "dp").astype(jnp.float32),
    )
    return (
        block_out,
        input_grad,
        table_grad,
        down_cols_sum,
        up_cols_sum,
        down_rows_sum,
        up_rows_sum,
    )


def fused(
    block_in,
    cotangent,
    norm_gains,
    col_weights,
    row_weights,
    mem_keys,
    value_table,
    col_down,
    col_up,
    row_down,
    row_up,
    segment_ids,
    adapter_ids,
    pick_ids,
):
    args = dict(
        block_in=block_in,
        cotangent_in=cotangent,
        norm_gains=norm_gains,
        col_weights=col_weights,
        row_weights=row_weights,
        mem_keys=mem_keys.reshape(-1, mem_keys.shape[3]),
        table=value_table,
        col_down_in=col_down,
        col_up_in=col_up,
        row_down_in=row_down,
        row_up_in=row_up,
        segment_ids=segment_ids,
        adapter_ids=adapter_ids,
        pick_ids=pick_ids[:, 0, :],
    )
    outs = whole_block(args, lax.axis_size("dp"), lax.axis_size("mp"))
    return (outs[0], *(out.astype(jnp.float32) for out in outs[1:]))


def solution(mesh):
    in_specs = (
        P("dp", None),
        P("dp", None),
        P(),
        P(None, None, "mp"),
        P(None, "mp", None),
        P(None, "mp", None, None),
        P(("dp", "mp"), None),
        P(),
        P(None, None, None, "mp"),
        P(None, None, None, "mp"),
        P(),
        P("dp", None),
        P("dp"),
        P("dp", "mp", None),
    )
    out_specs = (
        P("dp", None),
        P("dp", None),
        P(("dp", "mp"), None),
        P(),
        P(None, None, None, "mp"),
        P(None, None, None, "mp"),
        P(),
    )
    step = fused if mesh.shape["dp"] == 8 else per_device
    return jax.shard_map(
        step, mesh=mesh, in_specs=in_specs, out_specs=out_specs, check_vma=False
    )
```

```python
import functools
import jax
import jax.numpy as jnp
from jax import lax
from jax.experimental import pallas as pl
from jax.experimental.pallas import tpu as pltpu
from jax.sharding import PartitionSpec as P

HEAD_DIM = 64
LANES = 128


EPSILON = 1e-05
ADAPT_SCALE = 0.5


def matmul(left, right):
    return jnp.dot(left, right, preferred_element_type=jnp.float32)


def matmul_nt(left, right):
    return lax.dot_general(
        left, right, (((1,), (1,)), ((), ())), preferred_element_type=jnp.float32
    )


def matmul_tn(left, right):
    return lax.dot_general(
        left, right, (((0,), (0,)), ((), ())), preferred_element_type=jnp.float32
    )


def rms_scale(values):
    return lax.rsqrt(jnp.mean(values * values, axis=-1, keepdims=True) + EPSILON)


def silu_slope(gate):
    sigma = jax.nn.sigmoid(gate)
    return sigma * (1.0 + gate * (1.0 - sigma))


NT = (((1,), (1,)), ((), ()))
TN = (((0,), (0,)), ((), ()))


def split_rows(ids, base, rows):
    local = ids - base
    here = (local >= 0) & (local < rows)
    return jnp.where(here, local & (LANES - 1), 0), jnp.where(here, local >> 7, -1)


def spread_kernel(unroll, base_ref, ids_ref, w_ref, out_ref, lo_s, hi_s, w_s, tiles):
    brain = jnp.bfloat16
    tokens, rows = out_ref.shape
    high = rows // LANES
    pad = max(high, 16)
    lo, hi = split_rows(ids_ref[...], base_ref[0], rows)
    lo_s[...] = lo.astype(jnp.float32)
    hi_s[...] = hi.astype(jnp.float32)
    w_s[...] = w_ref[...].astype(jnp.float32)
    picks = ids_ref.shape[1]
    low_at = lax.broadcasted_iota(jnp.int32, (LANES, picks), 0).astype(jnp.float32).astype(brain)
    high_at = lax.broadcasted_iota(jnp.int32, (pad, picks), 0).astype(jnp.float32)
    empty = jnp.zeros((pad, picks), brain)

    def hot(t):
        lo = jnp.broadcast_to(lo_s[pl.ds(t, 1), :], (LANES, picks)).astype(brain)
        hi = jnp.broadcast_to(hi_s[pl.ds(t, 1), :], (pad, picks))
        w = jnp.broadcast_to(w_s[pl.ds(t, 1), :], (pad, picks))
        low_hot = jnp.where(lo == low_at, brain(1), brain(0))
        high_hot = jnp.where(hi == high_at, w, 0.0).astype(brain)
        return high_hot, low_hot

    def step(i, carry):
        for u in range(0, unroll, 2):
            t = i * unroll + u
            high_0, low_0 = hot(t)
            high_1, low_1 = hot(t + 1)
            left = jnp.concatenate(
                [
                    jnp.concatenate([high_0, empty], axis=1),
                    jnp.concatenate([empty, high_1], axis=1),
                ],
                axis=0,
            )
            right = jnp.concatenate([low_0, low_1], axis=1)
            tiles[pl.ds(t * pad, 2 * pad), :] = lax.dot_general(
                left, right, NT, preferred_element_type=jnp.float32
            )
        return carry

    lax.fori_loop(0, tokens // unroll, step, 0)
    for a in range(high):
        out_ref[:, a * LANES : (a + 1) * LANES] = tiles[pl.ds(a, tokens, stride=pad), :].astype(
            brain
        )


def spread(ids, weights, base, rows, block=128, unroll=32):
    tokens, picks = ids.shape
    pad = max(rows // LANES, 16)
    return pl.pallas_call(
        functools.partial(spread_kernel, unroll),
        grid=(tokens // block,),
        in_specs=[
            pl.BlockSpec(memory_space=pltpu.SMEM),
            pl.BlockSpec((block, picks), lambda i: (i, 0)),
            pl.BlockSpec((block, picks), lambda i: (i, 0)),
        ],
        out_specs=pl.BlockSpec((block, rows), lambda i: (i, 0)),
        out_shape=jax.ShapeDtypeStruct((tokens, rows), jnp.bfloat16),
        scratch_shapes=[pltpu.VMEM((block, picks), jnp.float32)] * 3
        + [pltpu.VMEM((block * pad, LANES), jnp.float32)],
        name="spread",
    )(base, ids, weights)


def answer_kernel(base_ref, grad_ref, table_ref, ids_ref, out_ref, all_s):
    rows = table_ref.shape[0]
    all_s[...] = lax.dot_general(
        grad_ref[...], table_ref[...], NT, preferred_element_type=jnp.float32
    )
    lo, hi = split_rows(ids_ref[...], base_ref[0], rows)
    total = jnp.zeros(ids_ref.shape, jnp.float32)
    for a in range(rows // LANES):
        found = jnp.take_along_axis(
            all_s[:, a * LANES : (a + 1) * LANES], lo, axis=1, mode="promise_in_bounds"
        )
        total = jnp.where(hi == a, found, total)
    out_ref[...] = total.astype(out_ref.dtype)


def answer(ids, grads, table, base, block=256):
    tokens, picks = ids.shape
    rows, width = table.shape
    return pl.pallas_call(
        answer_kernel,
        grid=(tokens // block,),
        in_specs=[
            pl.BlockSpec(memory_space=pltpu.SMEM),
            pl.BlockSpec((block, width), lambda i: (i, 0)),
            pl.BlockSpec((rows, width), lambda i: (0, 0)),
            pl.BlockSpec((block, picks), lambda i: (i, 0)),
        ],
        out_specs=pl.BlockSpec((block, picks), lambda i: (i, 0)),
        out_shape=jax.ShapeDtypeStruct((tokens, picks), jnp.float32),
        scratch_shapes=[pltpu.VMEM((block, rows), jnp.float32)],
        name="answer",
    )(base, grads, table, ids)


MESH = pl.DeviceIdType.MESH
SIDE = 128


class Refs:
    pass


def partner(index, bit):
    return index + bit - 2 * bit * ((index // bit) % 2)


def remote(src, dst, sems, slot, device):
    return pltpu.make_async_remote_copy(
        src_ref=src,
        dst_ref=dst,
        send_sem=sems.at[0, slot],
        recv_sem=sems.at[1, slot],
        device_id=device,
        device_id_type=MESH,
    )


def greet(devices):
    barrier = pltpu.get_barrier_semaphore()
    for device in devices:
        pl.semaphore_signal(barrier, inc=1, device_id=device, device_id_type=MESH)
    pl.semaphore_wait(barrier, len(devices))


def start(copies):
    for c in copies:
        c.start()


def arrive(copies):
    for c in copies:
        c.wait_recv()


def nt(left, right):
    return lax.dot_general(left, right, NT, preferred_element_type=jnp.float32)


def tn(left, right):
    return lax.dot_general(left, right, TN, preferred_element_type=jnp.float32)


def padded(values, rows=SIDE):
    return jnp.concatenate(
        [values, jnp.zeros((rows - values.shape[0], values.shape[1]), values.dtype)], axis=0
    )


def hot_rows(lo_s, hi_s, w_s, tiles, tokens, pad):
    brain = jnp.bfloat16
    picks = lo_s.shape[1]
    low_at = lax.broadcasted_iota(jnp.int32, (LANES, picks), 0).astype(jnp.float32).astype(brain)
    high_at = lax.broadcasted_iota(jnp.int32, (pad, picks), 0).astype(jnp.float32).astype(brain)
    empty = jnp.zeros((pad, picks), brain)

    def hot(t):
        lo = jnp.broadcast_to(lo_s[t : t + 1, :], (LANES, picks)).astype(brain)
        hi = jnp.broadcast_to(hi_s[t : t + 1, :], (pad, picks)).astype(brain)
        w = jnp.broadcast_to(w_s[t : t + 1, :], (pad, picks)).astype(brain)
        low_hot = jnp.where(lo == low_at, brain(1), brain(0))
        high_hot = jnp.where(hi == high_at, w, brain(0))
        return high_hot, low_hot

    def pair(t):
        high_0, low_0 = hot(t)
        high_1, low_1 = hot(t + 1)
        left = [
            jnp.concatenate([high_0, empty], axis=1),
            jnp.concatenate([empty, high_1], axis=1),
        ]
        return left, jnp.concatenate([low_0, low_1], axis=1)

    for t in range(0, tokens, 4):
        left_0, right_0 = pair(t)
        left_1, right_1 = pair(t + 2)
        four = nt(
            jnp.concatenate(left_0 + left_1, axis=0), jnp.concatenate([right_0, right_1], axis=0)
        )
        tiles[t * pad : (t + 2) * pad, :] = four[: 2 * pad, :LANES]
        tiles[(t + 2) * pad : (t + 4) * pad, :] = four[2 * pad :, LANES:]


def block_kernel(names, seqs, parts, *refs):
    n = Refs()
    for name, ref in zip(names, refs):
        setattr(n, name, ref)
    floating, brain = jnp.float32, jnp.bfloat16
    d = lax.axis_index("dp")
    m = lax.axis_index("mp")
    length, width = n.block_in.shape
    cols = width // parts
    quarter = length // parts
    rows = n.table_v.shape[0]
    picks_here = n.pick_ids.shape[1]
    picks = picks_here * parts
    half = length // 2
    subs = n.mem_keys.shape[0] // 2
    half_width = n.mem_keys.shape[1]
    heads = cols // HEAD_DIM

    core, x_side, y_side = partner(d, 1), partner(d, 2), partner(d, 4)
    corner = partner(x_side, 4)
    mine, chip_x, chip_y, chip_d = d // 2, x_side // 2, y_side // 2, corner // 2
    z_of = [lax.rem(m + k, parts) for k in range(parts)]
    sent = []

    def at(place):
        return {"dp": place, "mp": m}

    def deep(k):
        return {"dp": d, "mp": z_of[k]}

    def go(copies):
        start(copies)
        sent.extend(copies)
        return copies

    def z_scatter(send, got, sems):
        return go([remote(send.at[z_of[k]], got.at[k - 1], sems, k, deep(k)) for k in range(1, parts)])

    def z_gather(ref, sems, slot=0):
        return go([remote(ref.at[m], ref.at[m], sems, slot + k, deep(k)) for k in range(1, parts)])

    def near_gather(ref, sems):
        places = (x_side, y_side, corner, core)
        return go([remote(ref.at[d], ref.at[d], sems, 4 + i, at(p)) for i, p in enumerate(places)])

    def core_gather(ref, sems):
        places = (x_side, y_side, corner)
        return go([remote(ref.at[p], ref.at[p], sems, 8 + i, at(core)) for i, p in enumerate(places)])

    slot_of = [lax.rem(c - m + parts, parts) for c in range(parts)]

    def local(src, dst, slot):
        copy = pltpu.make_async_copy(src, dst, n.local_sems.at[slot])
        copy.start()
        return copy

    devices = [deep(k) for k in range(1, parts)] + [at(p) for p in (x_side, y_side, corner, core)]
    barrier = pltpu.get_barrier_semaphore()
    for device in devices:
        pl.semaphore_signal(barrier, inc=1, device_id=device, device_id_type=MESH)
    down_in = local(n.col_down_in, n.col_down, 9)
    qkv_in = local(n.col_weights.at[pl.ds(0, 3)], n.qkv, 0)
    own_out_in = local(n.row_weights.at[0], n.full_out.at[0], 1)
    factors_in = [
        local(ref, held, 10 + i)
        for i, (ref, held) in enumerate(
            (
                (n.row_down_in, n.row_down),
                (n.row_up_in, n.row_up),
                (n.col_up_in, n.col_up),
            )
        )
    ]
    cotangent_in = local(n.cotangent_in, n.cotangent, 13)
    adapter = n.adapter_ids[0]
    rank = n.col_down.shape[2]

    n.pick_wide[...] = jnp.zeros(n.pick_wide.shape, jnp.int32)
    n.pick_wide[:, :picks_here] = n.pick_ids[...]
    pick_rows = pl.ds(pl.multiple_of(m * picks_here, 16), picks_here)
    n.picks_own[...] = (
        jnp.transpose(n.pick_wide[...].astype(floating))[:picks_here].astype(jnp.int32)
        + adapter * 65536
    )
    for copy in factors_in:
        copy.wait()
    factors = (n.row_down[0, adapter], n.col_up[3, adapter], n.col_up[4, adapter], n.row_down[1, adapter])
    for i, factor in enumerate(factors):
        n.small[m, i * rank : (i + 1) * rank, :] = factor
    pl.semaphore_wait(barrier, len(devices))

    class Plane:
        def __init__(self, sems, whole, half):
            self.sems, self.whole, self.half = sems, whole, half

        def one(self):
            places = (x_side, y_side, core)
            self.a = go(
                [
                    remote(self.whole(d), self.whole(d), self.sems, 4 + i, at(p))
                    for i, p in enumerate(places)
                ]
            )

        def two(self):
            arrive(self.a[:2])
            moves = (
                (self.half(y_side, 0), x_side),
                (self.half(x_side, 1), y_side),
                (self.whole(x_side), core),
                (self.whole(y_side), core),
            )
            self.b = go(
                [remote(ref, ref, self.sems, 7 + i, at(p)) for i, (ref, p) in enumerate(moves)]
            )

        def three(self):
            arrive(self.b[:2])
            ref = self.whole(corner)
            self.c = go([remote(ref, ref, self.sems, 11, at(core))])

        def done(self):
            arrive(self.a[2:] + self.b[2:] + self.c)

    class Weights(Plane):
        def __init__(self, sems, own, full):
            chunk = full.shape[1] // seqs
            self.own, self.full, self.chunk = own, full, chunk

            def rows_of(p, h, count):
                return pl.ds(pl.multiple_of(p * chunk + h * (chunk // 2), 16), count)

            super().__init__(
                sems,
                lambda p: full.at[pl.ds(1, parts - 1), rows_of(p, 0, chunk), :],
                lambda p, h: full.at[pl.ds(1, parts - 1), rows_of(p, h, chunk // 2), :],
            )
            self.here = rows_of(d, 0, chunk)

        def deep(self):
            self.z = go(
                [
                    remote(
                        self.own.at[self.here],
                        self.full.at[parts - k, self.here],
                        self.sems,
                        k,
                        deep(k),
                    )
                    for k in range(1, parts)
                ]
            )

        def one(self):
            arrive(self.z)
            super().one()

    out_w = Weights(n.sems_f.at[0], n.row_weights.at[0], n.full_out)
    branch_w = Weights(n.sems_f.at[1], n.row_weights.at[1], n.full_branch)
    gate_w = Weights(n.sems_f.at[2], n.col_weights.at[4], n.full_gate)
    query_w = Weights(n.sems_f.at[3], n.col_weights.at[3], n.full_query)
    keys_w = Weights(n.sems_f.at[4], n.mem_keys, n.full_keys)

    def small_gather(first, last, slot):
        ref = n.small.at[m, pl.ds(first * rank, (last - first) * rank)]
        return go([remote(ref, ref, n.sems_z.at[0], slot + k, deep(k)) for k in range(1, parts)])

    out_w.deep()
    small_z = small_gather(0, 1, 0)
    i_z = go(
        [
            remote(n.picks_own, n.ids_t.at[d, pick_rows, :], n.sems_i, k, deep(k))
            for k in range(1, parts)
        ]
    )
    n.ids_t[d, pick_rows, :] = n.picks_own[...]

    inputs = n.block_in[...].astype(floating)
    down_in.wait()
    gain_one, gain_two = n.norm_gains[0:1, :], n.norm_gains[1:2, :]
    scale_one = lax.rsqrt(jnp.mean(inputs * inputs, axis=1, keepdims=True) + EPSILON)
    normed_one = (inputs * scale_one * gain_one).astype(brain)
    n.normed_one[...] = normed_one
    down_att = jnp.concatenate([n.col_down[j, adapter] for j in range(3)], axis=0)
    down_mem = jnp.concatenate([n.col_down[j, adapter] for j in (3, 4)], axis=0)
    n.up_att[...] = jnp.zeros(n.up_att.shape, brain)
    n.up_mem[...] = jnp.zeros(n.up_mem.shape, brain)
    for j in range(3):
        n.up_att[j * rank : (j + 1) * rank, j * cols : (j + 1) * cols] = n.col_up[j, adapter]
    for j in range(2):
        n.up_mem[j * rank : (j + 1) * rank, j * cols : (j + 1) * cols] = n.col_up[3 + j, adapter]
    low_att = nt(normed_one, down_att).astype(brain)
    n.low_att[...] = low_att
    qkv_in.wait()
    for j in range(3):
        n.proj[:, j * cols : (j + 1) * cols] = (
            jnp.dot(normed_one, n.qkv[j], preferred_element_type=floating)
            + ADAPT_SCALE
            * jnp.dot(low_att, n.up_att[:, j * cols : (j + 1) * cols], preferred_element_type=floating)
        ).astype(brain)
    out_w.one()
    arrive(i_z)
    i_near = near_gather(n.ids_t, n.sems_i)
    segment = jnp.broadcast_to(n.segment_ids[...].astype(floating), (length, length))
    ahead = lax.broadcasted_iota(jnp.int32, (length, length), 1) <= lax.broadcasted_iota(
        jnp.int32, (length, length), 0
    )
    allowed = (segment == jnp.transpose(segment)) & ahead
    lane = lax.broadcasted_iota(jnp.int32, (length, LANES), 1)
    sides = LANES // HEAD_DIM

    def pair_of(which, pair):
        first = which * cols + pair * LANES
        return n.proj[:, first : first + LANES]

    for pair in range(heads // sides):
        query2, key2, value2 = (pair_of(w, pair) for w in range(3))
        mixed = jnp.zeros((length, LANES), floating)
        for side in range(sides):
            own = lane // HEAD_DIM == side
            logits = 0.125 * nt(jnp.where(own, query2, brain(0)), key2)
            logits = jnp.where(allowed, logits, -1e30)
            expos = jnp.exp(logits - jnp.max(logits, axis=1, keepdims=True))
            probs = expos / jnp.sum(expos, axis=1, keepdims=True)
            n.probs[pair * sides + side] = probs
            out = jnp.dot(probs.astype(brain), value2, preferred_element_type=floating)
            mixed = jnp.where(own, out, mixed)
        n.att_out[:, pair * LANES : (pair + 1) * LANES] = mixed.astype(brain)
    my_cols = pl.ds(pl.multiple_of(m * cols, LANES), cols)
    att_z = go(
        [
            remote(n.att_out, n.att_all.at[:, my_cols], n.sems_z.at[1], k, deep(k))
            for k in range(1, parts)
        ]
    )
    n.att_all[:, my_cols] = n.att_out[...]
    own_in = [
        local(n.col_weights.at[3], n.full_query.at[0], 4),
        local(n.mem_keys, n.full_keys.at[0], 5),
        local(n.row_weights.at[1], n.full_branch.at[0], 2),
        local(n.col_weights.at[4], n.full_gate.at[0], 3),
    ]
    table_in = local(n.table, n.table_v, 6)
    out_w.two()
    row_down = [n.row_down[j, adapter] for j in range(2)]
    row_up = [n.row_up[j, adapter] for j in range(2)]

    cotangent_in.wait()
    cotangent = n.cotangent[...]
    low_branch_grad = (ADAPT_SCALE * nt(cotangent, padded(row_up[1]))).astype(brain)
    n.low_branch_grad[...] = low_branch_grad
    own_in[2].wait()
    n.gated_own[...] = nt(cotangent, n.full_branch[0]) + jnp.dot(
        low_branch_grad, padded(row_down[1]), preferred_element_type=floating
    )
    out_w.three()
    arrive(i_near[:3])
    i_core = core_gather(n.ids_t, n.sems_i)
    base = (d * parts + m) * rows

    def turn(s, carry):
        local = n.ids_t[s] % 65536 - base
        here = (local >= 0) & (local < rows)
        turned = jnp.transpose(jnp.where(here, local, -1).astype(floating)).astype(jnp.int32)
        n.ids_v[pl.ds(pl.multiple_of(s * length, 16), length), :] = turned
        n.who[s] = n.ids_t[s, 0:8, 0:LANES] // 65536
        return carry

    arrive(small_z)

    def over_slots(values, full):
        total = jnp.zeros((values.shape[0], width), floating)
        for c in range(parts):
            total = total + jnp.dot(
                values[:, c * cols : (c + 1) * cols],
                full[slot_of[c]],
                preferred_element_type=floating,
            )
        return total

    out_w.done()

    def small_of(i):
        return padded(
            jnp.concatenate(
                [n.small[c, i * rank : (i + 1) * rank, :] for c in range(parts)], axis=1
            )
        )

    arrive(att_z)
    own_out_in.wait()
    att_all = n.att_all[...]
    low_out = nt(att_all, small_of(0)).astype(brain)
    n.low_out[...] = low_out
    resid = (
        n.block_in[...].astype(floating)
        + over_slots(att_all, n.full_out)
        + ADAPT_SCALE * jnp.dot(low_out, padded(row_up[0]), preferred_element_type=floating)
    )
    n.resid[...] = resid
    scale_two = lax.rsqrt(jnp.mean(resid * resid, axis=1, keepdims=True) + EPSILON)
    normed_two = (resid * scale_two * gain_two).astype(brain)
    n.normed_two[...] = normed_two

    own_in[0].wait()
    own_in[1].wait()
    low_mem = nt(normed_two, down_mem).astype(brain)
    n.low_mem[...] = low_mem
    mem_query = (
        jnp.dot(normed_two, n.full_query[0], preferred_element_type=floating)
        + ADAPT_SCALE * jnp.dot(low_mem, n.up_mem[:, :cols], preferred_element_type=floating)
    ).astype(brain)
    sub_one = nt(mem_query[:, :half_width], n.full_keys[0, :subs])
    sub_two = nt(mem_query[:, half_width:], n.full_keys[0, subs:])
    wide = n.pick_wide[...]

    def chosen(table, index):
        found = jnp.zeros(index.shape, floating)
        for c in range(subs // LANES):
            taken = jnp.take_along_axis(
                table[:, c * LANES : (c + 1) * LANES],
                index % LANES,
                axis=1,
                mode="promise_in_bounds",
            )
            found = jnp.where(index // LANES == c, taken, found)
        return found

    scores = chosen(sub_one, wide // subs) + chosen(sub_two, wide % subs)
    scores = jnp.where(lane < picks_here, scores, -1e30)
    expos = jnp.exp(scores - jnp.max(scores, axis=1, keepdims=True))
    weights = expos / jnp.sum(expos, axis=1, keepdims=True)
    n.weights_own[...] = jnp.transpose(weights)[:picks_here].astype(brain)
    w_z = go(
        [
            remote(n.weights_own, n.w_all.at[d, pick_rows, :], n.sems_w, k, deep(k))
            for k in range(1, parts)
        ]
    )
    n.w_all[d, pick_rows, :] = n.weights_own[...]
    own_in[3].wait()
    gate_pre = jnp.dot(
        normed_two, n.full_gate[0], preferred_element_type=floating
    ) + ADAPT_SCALE * jnp.dot(low_mem, n.up_mem[:, cols:], preferred_element_type=floating)
    sigma = 1.0 / (1.0 + jnp.exp(-gate_pre))
    n.grads_own[...] = (n.gated_own[...] * (gate_pre * sigma)).astype(brain)

    def seq_rows(s):
        return pl.ds(pl.multiple_of(s * length, 16), length)

    g_z = go(
        [
            remote(n.grads_own, n.g_all.at[seq_rows(d), my_cols], n.sems_g, k, deep(k))
            for k in range(1, parts)
        ]
    )
    n.g_all[seq_rows(d), my_cols] = n.grads_own[...]
    arrive(i_near[3:])
    arrive(i_core)
    lax.fori_loop(0, seqs, turn, 0)

    block = n.lo_s.shape[0]
    pad = n.tiles.shape[0] // block

    per_seq = length // block

    def build(i, carry):
        order = i // per_seq
        mask = (2 * order) % seqs + (2 * order) // seqs
        seq = sum(((d // b + mask // b) % 2) * b for b in (1, 2, 4))
        first = (i % per_seq) * block
        here = pl.ds(pl.multiple_of(seq * length + first, block), block)
        local = n.ids_v[here, :]
        n.lo_s[...] = jnp.where(local < 0, 0, local & (LANES - 1)).astype(floating)
        n.hi_s[...] = (local >> 7).astype(floating)
        w_t = n.w_all[seq, :, pl.ds(pl.multiple_of(first, block), block)]
        n.w_s[...] = jnp.transpose(w_t.astype(floating))
        hot_rows(n.lo_s, n.hi_s, n.w_s, n.tiles, block, pad)
        for a in range(rows // LANES):
            n.spread_v[here, a * LANES : (a + 1) * LANES] = n.tiles[
                pl.ds(a, block, stride=pad), :
            ].astype(brain)
        return carry

    blocks = seqs * per_seq
    grads_g = Plane(
        n.sems_g,
        lambda s: n.g_all.at[seq_rows(s)],
        lambda s, h: n.g_all.at[pl.ds(pl.multiple_of(s * length + h * half, 16), half)],
    )
    arrive(w_z)
    w_near = near_gather(n.w_all, n.sems_w)
    lax.fori_loop(0 * per_seq, 1 * per_seq, build, 0)
    arrive(w_near[:3])
    w_core = core_gather(n.w_all, n.sems_w)
    lax.fori_loop(1 * per_seq, 2 * per_seq, build, 0)
    arrive(w_near[3:])
    arrive(w_core)
    lax.fori_loop(2 * per_seq, 3 * per_seq, build, 0)
    arrive(g_z)
    grads_g.one()
    branch_w.deep()
    lax.fori_loop(3 * per_seq, 4 * per_seq, build, 0)
    gate_w.deep()
    small_z = small_gather(1, 4, 4)
    lax.fori_loop(4 * per_seq, 5 * per_seq, build, 0)
    query_w.deep()
    keys_w.deep()
    branch_w.one()
    lax.fori_loop(5 * per_seq, 6 * per_seq, build, 0)
    lax.fori_loop(6 * per_seq, 7 * per_seq, build, 0)
    grads_g.two()
    lax.fori_loop(7 * per_seq, 8 * per_seq, build, 0)
    gate_w.one()
    branch_w.two()

    table_in.wait()
    sib_core = core % 2

    def partial_of(seq):
        return jnp.dot(
            n.spread_v[seq_rows(seq), :], n.table_v[...], preferred_element_type=floating
        ).astype(brain)

    to_core = []
    for i, chip in enumerate((chip_d, chip_x, chip_y, mine)):
        n.part_sib[chip] = partial_of(2 * chip + sib_core)
        to_core += go(
            [remote(n.part_sib.at[chip], n.got_core.at[chip], n.sems_m.at[0], i, at(core))]
        )

    steps = 2
    piece = half // steps

    def spot(t, side):
        return pl.ds(t * 2 * piece + side * piece, piece)

    def stretch(t):
        return pl.ds(t * 2 * piece, 2 * piece)

    def add_to(chip, where, *got):
        total = n.part_own[chip, where].astype(floating)
        for more in got:
            total = total + more.astype(floating)
        n.part_own[chip, where] = total.astype(brain)

    def plane_move(t, i, chip, side, got, slot, to):
        return remote(
            n.part_own.at[chip, spot(t, side)],
            got.at[slot, t],
            n.sems_m.at[1 + t],
            i,
            at(to),
        )

    def plane_one(t):
        return go(
            [
                plane_move(t, 0, chip_d, 0, n.got_x, 0, x_side),
                plane_move(t, 1, chip_d, 1, n.got_y, 0, y_side),
                plane_move(t, 2, chip_x, 0, n.got_x, 1, x_side),
                plane_move(t, 3, chip_y, 1, n.got_y, 1, y_side),
            ]
        )

    def plane_two(t, one):
        arrive(one[:2])
        add_to(chip_y, spot(t, 0), n.got_x[0, t])
        add_to(chip_x, spot(t, 1), n.got_y[0, t])
        return go(
            [
                plane_move(t, 4, chip_x, 1, n.got_x, 2, x_side),
                plane_move(t, 5, chip_y, 0, n.got_y, 2, y_side),
            ]
        )

    def cols_of(k):
        return pl.ds(pl.multiple_of(z_of[k] * cols, LANES), cols)

    def plane_done(t, one, two):
        arrive(one[2:])
        arrive(two)
        add_to(mine, spot(t, 0), n.got_x[1, t], n.got_y[2, t])
        add_to(mine, spot(t, 1), n.got_x[2, t], n.got_y[1, t])
        return go(
            [
                remote(
                    n.part_own.at[mine, stretch(t), cols_of(k)],
                    n.got_z.at[k - 1, stretch(t)],
                    n.sems_m.at[1 + t],
                    5 + k,
                    deep(k),
                )
                for k in range(1, parts)
            ]
        )

    def spread_memory(t, moved):
        arrive(moved)
        memory = n.part_own[mine, stretch(t), my_cols].astype(floating)
        for k in range(parts - 1):
            memory = memory + n.got_z[k, stretch(t)].astype(floating)
        n.mem_own[stretch(t)] = memory.astype(brain)
        n.mem_all[stretch(t), my_cols] = n.mem_own[stretch(t)]
        return go(
            [
                remote(
                    n.mem_own.at[stretch(t)],
                    n.mem_all.at[stretch(t), my_cols],
                    n.sems_z.at[3],
                    4 * t + k,
                    deep(k),
                )
                for k in range(1, parts)
            ]
        )

    for i, chip in enumerate((chip_d, chip_x, chip_y, mine)):
        n.part_own[chip] = partial_of(2 * chip + d % 2)
        arrive(to_core[i : i + 1])
        add_to(chip, slice(None), n.got_core[chip])
        if i == 2:
            one_0 = plane_one(0)

    grads_g.three()
    def answers_of(seq):
        n.all_s[:, :rows] = nt(n.g_all[seq_rows(seq), :], n.table_v[...])
        local = n.ids_v[seq_rows(seq), :]
        lo, hi = jnp.where(local < 0, 0, local & (LANES - 1)), local >> 7
        total = jnp.zeros((length, picks), floating)
        for a in range(rows // LANES):
            found = jnp.take_along_axis(
                n.all_s[:, a * LANES : (a + 1) * LANES], lo, axis=1, mode="promise_in_bounds"
            )
            total = jnp.where(hi == a, found, total)
        return jnp.transpose(total).astype(brain)

    def answers_for(order, held, side):
        def body(i, carry):
            chip = sum(((d // (2 * b) + i // b) % 2) * b for b in (1, 2))
            held[chip] = answers_of(2 * chip + side)
            return carry

        lax.fori_loop(*order, body, 0)

    arrive(grads_g.a[2:] + grads_g.b[2:])
    answers_for((0, 3), n.ans_sib, sib_core)
    two_0 = plane_two(0, one_0)
    one_1 = plane_one(1)
    branch_w.three()
    gate_w.two()
    arrive(grads_g.c)
    answers_for((3, 4), n.ans_sib, sib_core)
    a_core = go([remote(n.ans_sib, n.ans_core, n.sems_a, 0, at(core))])
    answers_for((0, 1), n.ans_own, d % 2)
    m_0 = plane_done(0, one_0, two_0)
    query_w.one()
    keys_w.one()
    gate_w.three()
    answers_for((1, 2), n.ans_own, d % 2)
    two_1 = plane_two(1, one_1)
    answers_for((2, 4), n.ans_own, d % 2)
    arrive(a_core)
    n.ans_own[...] = (n.ans_own[...].astype(floating) + n.ans_core[...].astype(floating)).astype(
        brain
    )
    a_plane = go(
        [
            remote(n.ans_own.at[chip], n.ans_plane.at[i], n.sems_a, 1 + i, at(p))
            for i, (chip, p) in enumerate(((chip_x, x_side), (chip_y, y_side), (chip_d, corner)))
        ]
    )
    m_1 = plane_done(1, one_1, two_1)
    mem_0 = spread_memory(0, m_0)
    query_w.two()
    keys_w.two()

    tg_block = n.tg_v.shape[1]
    tg_steps = rows // tg_block

    def tg_out(i):
        return pltpu.make_async_copy(
            n.tg_v.at[i % 2],
            n.table_grad.at[pl.ds(i * tg_block, tg_block)],
            n.local_sems.at[7 + i % 2],
        )

    def table_grad_steps(first, last):
        for i in range(first, last):
            if i >= 2:
                tg_out(i - 2).wait()
            n.tg_v[i % 2] = tn(
                n.spread_v[:, i * tg_block : (i + 1) * tg_block], n.g_all[...]
            ).astype(brain)
            tg_out(i).start()

    weave = iter(range(tg_steps))

    def table_grad_some(count):
        for _ in range(count):
            i = next(weave)
            table_grad_steps(i, i + 1)

    table_grad_some(0)
    arrive(a_plane)
    answered = n.ans_own[mine].astype(floating)
    for k in range(3):
        answered = answered + n.ans_plane[k].astype(floating)
    n.ans_own[mine] = answered.astype(brain)
    a_z = go(
        [remote(n.ans_own.at[mine], n.ans_z.at[k - 1], n.sems_a, 3 + k, deep(k)) for k in range(1, parts)]
    )
    query_w.three()
    keys_w.three()
    arrive(small_z)
    table_grad_some(1)
    mem_1 = spread_memory(1, m_1)
    arrive(a_z)
    weight_grad = n.ans_own[mine].astype(floating)
    for k in range(parts - 1):
        weight_grad = weight_grad + n.ans_z[k].astype(floating)
    weights_t = n.w_all[d].astype(floating)
    for h in range(parts):
        here = slice(h * picks_here, (h + 1) * picks_here)
        weighed = weights_t[here] * weight_grad[here]
        n.score_f[here, :] = weighed - weights_t[here] * jnp.sum(weighed, axis=0, keepdims=True)
    rows_picked = n.ids_t[d] % 65536
    n.first_t[...] = (rows_picked // subs).astype(floating)
    n.second_t[...] = (rows_picked % subs).astype(floating)
    sub_block = subs // 2

    def gather_subs(head, carry):
        for top in range(0, subs, sub_block):
            key_at = (
                (lax.broadcasted_iota(jnp.int32, (sub_block, length), 0) + top)
                .astype(floating)
                .astype(brain)
            )
            ones = jnp.zeros((sub_block, length), brain)
            twos = jnp.zeros((sub_block, length), brain)
            for p in range(picks_here):
                row = pl.ds(head * picks_here + p, 1)
                score = jnp.broadcast_to(n.score_f[row, :], key_at.shape).astype(brain)
                one = jnp.broadcast_to(n.first_t[row, :], key_at.shape).astype(brain)
                two = jnp.broadcast_to(n.second_t[row, :], key_at.shape).astype(brain)
                ones = ones + jnp.where(key_at == one, score, brain(0))
                twos = twos + jnp.where(key_at == two, score, brain(0))
            n.sub_grads[0, top : top + sub_block, :] = ones
            n.sub_grads[1, top : top + sub_block, :] = twos
        for i in range(2):
            first = pl.multiple_of(head * cols + i * half_width, LANES)
            n.query_grad[:, pl.ds(first, half_width)] = tn(
                n.sub_grads[i], n.full_keys[lax.rem(head - m + parts, parts), i * subs : (i + 1) * subs]
            ).astype(brain)
        return carry

    keys_w.done()
    lax.fori_loop(0, parts, gather_subs, 0)
    branch_w.done()
    gate_w.done()
    cotangent = n.cotangent[...]
    normed_two = n.normed_two[...]
    low_branch_grad = n.low_branch_grad[...]
    low_mem = n.low_mem[...]
    for c in range(parts):
        n.all_s[:, c * cols : (c + 1) * cols] = nt(
            cotangent, n.full_branch[slot_of[c]]
        ) + jnp.dot(
            low_branch_grad,
            padded(n.small[c, 3 * rank : 4 * rank, :]),
            preferred_element_type=floating,
        )
    for c in range(parts):
        n.all_s[:, width + c * cols : width + (c + 1) * cols] = jnp.dot(
            normed_two, n.full_gate[slot_of[c]], preferred_element_type=floating
        ) + ADAPT_SCALE * jnp.dot(
            low_mem[:, rank:],
            n.small[c, 2 * rank : 3 * rank, :],
            preferred_element_type=floating,
        )
    table_grad_some(0)
    arrive(mem_0)
    arrive(mem_1)
    for c in range(parts):
        here = slice(c * cols, (c + 1) * cols)
        memory = n.mem_all[:, here].astype(floating)
        gate_pre = n.all_s[:, width + c * cols : width + (c + 1) * cols]
        sigma = 1.0 / (1.0 + jnp.exp(-gate_pre))
        n.gated[:, here] = (memory * (gate_pre * sigma)).astype(brain)
        n.gate_grad[:, here] = (
            n.all_s[:, here] * memory * (sigma * (1.0 + gate_pre * (1.0 - sigma)))
        ).astype(brain)
    query_w.done()
    query_grad, gate_grad, gated = n.query_grad[...], n.gate_grad[...], n.gated[...]
    low_mem_grads = [
        (ADAPT_SCALE * nt(grads, small_of(1 + i))).astype(brain)
        for i, grads in enumerate((query_grad, gate_grad))
    ]
    two_grad = jnp.dot(
        low_mem_grads[0], padded(n.col_down[3, adapter]), preferred_element_type=floating
    ) + jnp.dot(low_mem_grads[1], padded(n.col_down[4, adapter]), preferred_element_type=floating)
    for c in range(parts):
        here = slice(c * cols, (c + 1) * cols)
        two_grad = two_grad + nt(query_grad[:, here], n.full_query[slot_of[c]])
        two_grad = two_grad + nt(gate_grad[:, here], n.full_gate[slot_of[c]])
    resid = n.resid[...]
    scale_two = lax.rsqrt(jnp.mean(resid * resid, axis=1, keepdims=True) + EPSILON)
    weighted = gain_two * two_grad
    resid_grad = (
        cotangent.astype(floating)
        + scale_two * weighted
        - resid * scale_two**3 * jnp.mean(resid * weighted, axis=1, keepdims=True)
    )
    n.all_s[:, :width] = resid_grad
    branch_grad = resid_grad.astype(brain)
    n.att_all[...] = branch_grad

    low_out_grad = (ADAPT_SCALE * nt(branch_grad, padded(row_up[0]))).astype(brain)
    att_out_grad = (
        nt(branch_grad, n.full_out[0])
        + jnp.dot(low_out_grad, padded(row_down[0]), preferred_element_type=floating)
    ).astype(brain)
    for pair in range(heads // sides):
        query2, key2, value2 = (pair_of(w, pair) for w in range(3))
        out2 = att_out_grad[:, pair * LANES : (pair + 1) * LANES]
        grads2 = [jnp.zeros((length, LANES), floating)] * 3
        for side in range(sides):
            own = lane // HEAD_DIM == side
            probs = n.probs[pair * sides + side]
            prob_grad = nt(jnp.where(own, out2, brain(0)), value2)
            logit_grad = (
                probs * (prob_grad - jnp.sum(probs * prob_grad, axis=1, keepdims=True))
            ).astype(brain)
            made = (
                0.125 * jnp.dot(logit_grad, key2, preferred_element_type=floating),
                0.125 * tn(logit_grad, query2),
                tn(probs.astype(brain), out2),
            )
            grads2 = [jnp.where(own, new, old) for new, old in zip(made, grads2)]
        for w in range(3):
            first = w * cols + pair * LANES
            n.proj_grad[:, first : first + LANES] = grads2[w].astype(brain)
    proj_grad = n.proj_grad[...]
    low_att_part = ADAPT_SCALE * nt(proj_grad, padded(n.up_att[...]))
    one_part = jnp.dot(low_att_part.astype(brain), padded(down_att), preferred_element_type=floating)
    for j in range(3):
        one_part = one_part + nt(n.proj_grad[:, j * cols : (j + 1) * cols], n.qkv[j])
    n.sum_send[:, :, :width] = one_part.astype(brain).reshape(parts, quarter, width)
    n.sum_send[:, :, width:] = low_att_part.astype(brain).reshape(parts, quarter, SIDE)
    last = quarter // 2

    def tail_rows(h):
        return pl.ds(h * last, last)

    r_one = [
        go(
            [
                remote(
                    n.sum_send.at[z_of[k], tail_rows(h)],
                    n.sum_got.at[k - 1, tail_rows(h)],
                    n.sems_z.at[4],
                    4 * h + k,
                    deep(k),
                )
                for k in range(1, parts)
            ]
        )
        for h in range(2)
    ]

    branch_grad, gated = n.att_all[...], n.gated[...]
    low_branch = nt(gated, small_of(3)).astype(brain)
    branch = over_slots(gated, n.full_branch)
    branch = branch + ADAPT_SCALE * jnp.dot(
        low_branch, padded(row_up[1]), preferred_element_type=floating
    )
    n.block_out[...] = (n.resid[...] + branch).astype(brain)
    n.early[d, 3 * rank :, :] = (ADAPT_SCALE * tn(low_branch, n.cotangent[...]))[:rank].astype(brain)
    up_att_grad = ADAPT_SCALE * tn(n.low_att[...], proj_grad)
    for j in range(3):
        n.narrow[d, j * rank : (j + 1) * rank, :] = up_att_grad[
            j * rank : (j + 1) * rank, j * cols : (j + 1) * cols
        ].astype(brain)
    for j, grads in enumerate((n.query_grad, n.gate_grad)):
        n.narrow[d, (3 + j) * rank : (4 + j) * rank, :] = (
            ADAPT_SCALE * tn(n.low_mem[...], grads[:, my_cols])
        )[j * rank : (j + 1) * rank].astype(brain)
    n.narrow[d, 5 * rank : 6 * rank, :] = tn(low_out_grad, n.att_out[...])[:rank].astype(brain)
    n.narrow[d, 6 * rank : 7 * rank, :] = tn(n.low_branch_grad[...], n.gated[:, my_cols])[
        :rank
    ].astype(brain)
    for j in range(2):
        n.early[d, j * rank : (j + 1) * rank, :] = tn(low_mem_grads[j], n.normed_two[...])[
            :rank
        ].astype(brain)
    n.early[d, 2 * rank : 3 * rank, :] = (ADAPT_SCALE * tn(n.low_out[...], branch_grad))[
        :rank
    ].astype(brain)
    n_near = near_gather(n.narrow, n.sems_b.at[0])
    e_near = near_gather(n.early, n.sems_b.at[1])
    table_grad_some(4)
    q_low_att, q_in = [], []
    for h in range(2):
        arrive(r_one[h])
        total = n.sum_send[m, tail_rows(h)].astype(floating)
        for k in range(parts - 1):
            total = total + n.sum_got[k, tail_rows(h)].astype(floating)
        n.gath_low[m, tail_rows(h)] = total[:, width:].astype(brain)
        my_rows = pl.ds(pl.multiple_of(m * quarter + h * last, 16), last)
        weighted = gain_one * total[:, :width]
        inputs = n.block_in[my_rows, :].astype(floating)
        scale_one = lax.rsqrt(jnp.mean(inputs * inputs, axis=1, keepdims=True) + EPSILON)
        n.gath_in[m, tail_rows(h)] = (
            n.all_s[my_rows, :width]
            + scale_one * weighted
            - inputs * scale_one**3 * jnp.mean(inputs * weighted, axis=1, keepdims=True)
        ).astype(brain)
        for ref, sems, out in ((n.gath_low, n.sems_z.at[5], q_low_att), (n.gath_in, n.sems_z.at[6], q_in)):
            view = ref.at[m, tail_rows(h)]
            out += go([remote(view, view, sems, 4 * h + k, deep(k)) for k in range(1, parts)])
    arrive(n_near[:3])
    arrive(e_near[:3])
    n_core = core_gather(n.narrow, n.sems_b.at[0])
    e_core = core_gather(n.early, n.sems_b.at[1])
    table_grad_some(1)
    arrive(q_low_att)
    low_att_grad = n.gath_low[...].reshape(length, SIDE)
    n.late[d] = tn(low_att_grad, n.normed_one[...])[: 3 * rank].astype(brain)
    l_near = near_gather(n.late, n.sems_b.at[2])
    table_grad_some(1)
    arrive(n_near[3:] + e_near[3:] + n_core + e_core)
    arrive(l_near[:3])
    l_core = core_gather(n.late, n.sems_b.at[2])
    table_grad_some(1)
    arrive(l_near[3:])
    arrive(l_core)

    def place(a, carry):
        wide_late = jnp.zeros(n.late.shape[1:], brain)
        wide_early = jnp.zeros(n.early.shape[1:], brain)
        thin = jnp.zeros(n.narrow.shape[1:], brain)
        for s in range(seqs):
            is_it = (n.who[s, 0:1, 0:1] == a).astype(floating).astype(brain)
            wide_late = wide_late + n.late[s] * is_it
            wide_early = wide_early + n.early[s] * is_it
            thin = thin + n.narrow[s] * is_it
        for j in range(3):
            n.col_down_grad[j, a] = wide_late[j * rank : (j + 1) * rank]
            n.col_up_grad[j, a] = thin[j * rank : (j + 1) * rank]
        for j in range(2):
            n.col_down_grad[3 + j, a] = wide_early[j * rank : (j + 1) * rank]
            n.col_up_grad[3 + j, a] = thin[(3 + j) * rank : (4 + j) * rank]
            n.row_down_grad[j, a] = thin[(5 + j) * rank : (6 + j) * rank]
            n.row_up_grad[j, a] = wide_early[(2 + j) * rank : (3 + j) * rank]
        return carry

    lax.fori_loop(0, n.col_down.shape[1], place, 0)
    arrive(q_in)
    n.input_grad[...] = n.gath_in[...].reshape(length, width)
    for i in range(max(tg_steps - 2, 0), tg_steps):
        tg_out(i).wait()
    for c in sent:
        c.wait_send()


def whole_block(args, seqs, parts):
    floating, brain, whole = jnp.float32, jnp.bfloat16, jnp.int32
    given = Refs()
    given.__dict__.update(args)
    length, width = given.block_in.shape
    rows = given.table.shape[0]
    cols, quarter = width // parts, length // parts
    picks_here = given.pick_ids.shape[1]
    picks = picks_here * parts
    rank = given.col_down_in.shape[2]
    subs = given.mem_keys.shape[0] // 2
    tokens = seqs * length
    block, tg_block = 128, 256
    pad = max(rows // LANES, 16)
    vmem = pl.BlockSpec(memory_space=pltpu.VMEM)
    anywhere = pl.BlockSpec(memory_space=pl.ANY)
    inside = dict(
        adapter_ids=pl.BlockSpec(memory_space=pltpu.SMEM),
        block_in=vmem,
        norm_gains=vmem,
        segment_ids=vmem,
        pick_ids=vmem,
    )
    outs = dict(
        block_out=((length, width), brain),
        input_grad=((length, width), brain),
        table_grad=((rows, width), brain),
        col_down_grad=(given.col_down_in.shape, brain),
        col_up_grad=(given.col_up_in.shape, brain),
        row_down_grad=(given.row_down_in.shape, brain),
        row_up_grad=(given.row_up_in.shape, brain),
    )
    chips = seqs // 2
    scratch = dict(
        table_v=((rows, width), brain),
        pick_wide=((length, LANES), whole),
        picks_own=((picks_here, length), whole),
        ids_t=((seqs, picks, length), whole),
        ids_v=((tokens, picks), whole),
        who=((seqs, 8, LANES), whole),
        normed_one=((length, width), brain),
        up_att=((3 * rank, 3 * cols), brain),
        up_mem=((2 * rank, 2 * cols), brain),
        low_att=((length, 3 * rank), brain),
        low_mem=((length, 2 * rank), brain),
        proj=((length, 3 * cols), brain),
        proj_grad=((length, 3 * cols), brain),
        probs=((cols // HEAD_DIM, length, length), floating),
        att_out=((length, cols), brain),
        sum_send=((parts, quarter, width + SIDE), brain),
        sum_got=((parts - 1, quarter, width + SIDE), brain),
        qkv=((3, width, cols), brain),
        col_down=(given.col_down_in.shape, brain),
        col_up=(given.col_up_in.shape, brain),
        row_down=(given.row_down_in.shape, brain),
        row_up=(given.row_up_in.shape, brain),
        cotangent=((length, width), brain),
        full_out=((parts, cols, width), brain),
        full_branch=((parts, cols, width), brain),
        full_gate=((parts, width, cols), brain),
        full_query=((parts, width, cols), brain),
        full_keys=((parts, *given.mem_keys.shape), brain),
        small=((parts, 4 * rank, cols), brain),
        att_all=((length, width), brain),
        low_out=((length, SIDE), brain),
        normed_two=((length, width), brain),
        gated=((length, width), brain),
        gate_grad=((length, width), brain),
        query_grad=((length, width), brain),
        mem_own=((length, cols), brain),
        mem_all=((length, width), brain),
        score_f=((picks, length), floating),
        sub_grads=((2, subs, length), brain),
        low_branch_grad=((length, SIDE), brain),
        gated_own=((length, cols), floating),
        resid=((length, width), floating),
        gath_in=((parts, quarter, width), brain),
        gath_low=((parts, quarter, SIDE), brain),
        weights_own=((picks_here, length), brain),
        w_all=((seqs, picks, length), brain),
        grads_own=((length, cols), brain),
        g_all=((tokens, width), brain),
        spread_v=((tokens, rows), brain),
        tiles=((block * pad, LANES), floating),
        lo_s=((block, picks), floating),
        hi_s=((block, picks), floating),
        w_s=((block, picks), floating),
        part_own=((chips, length, width), brain),
        part_sib=((chips, length, width), brain),
        got_core=((chips, length, width), brain),
        got_x=((3, 2, length // 4, width), brain),
        got_y=((3, 2, length // 4, width), brain),
        got_z=((parts - 1, length, cols), brain),
        ans_own=((chips, picks, length), brain),
        ans_sib=((chips, picks, length), brain),
        ans_core=((chips, picks, length), brain),
        ans_plane=((3, picks, length), brain),
        ans_z=((parts - 1, picks, length), brain),
        all_s=((length, max(rows, 2 * width)), floating),
        tg_v=((2, tg_block, width), brain),
        first_t=((picks, length), floating),
        second_t=((picks, length), floating),
        narrow=((seqs, 7 * rank, cols), brain),
        early=((seqs, 4 * rank, width), brain),
        late=((seqs, 3 * rank, width), brain),
    )
    semaphores = dict(
        local_sems=(14,),
        sems_i=(2, 12),
        sems_w=(2, 12),
        sems_g=(2, 12),
        sems_m=(3, 2, 10),
        sems_a=(2, 8),
        sems_z=(9, 2, 8),
        sems_f=(5, 2, 12),
        sems_b=(3, 2, 12),
    )
    names = [*args, *outs, *scratch, *semaphores]
    return pl.pallas_call(
        functools.partial(block_kernel, names, seqs, parts),
        in_specs=[inside.get(name, anywhere) for name in args],
        out_specs=[anywhere if name == "table_grad" else vmem for name in outs],
        out_shape=[jax.ShapeDtypeStruct(*made) for made in outs.values()],
        scratch_shapes=[pltpu.VMEM(*made) for made in scratch.values()]
        + [pltpu.SemaphoreType.DMA(shape) for shape in semaphores.values()],
        compiler_params=pltpu.CompilerParams(
            collective_id=0, has_side_effects=True, vmem_limit_bytes=63 * 2**20
        ),
        name="whole_block",
    )(*args.values())


def pick_scores(picks, first, second, sub_count):
    columns = jnp.arange(sub_count, dtype=jnp.int32)
    hit_first = (picks // sub_count)[:, :, None] == columns
    hit_second = (picks % sub_count)[:, :, None] == columns
    scores = jnp.sum(jnp.where(hit_first, first[:, None, :], 0.0), axis=2)
    scores = scores + jnp.sum(jnp.where(hit_second, second[:, None, :], 0.0), axis=2)
    return (jax.nn.softmax(scores, axis=-1), hit_first, hit_second)


def per_device(
    block_in,
    cotangent,
    norm_gains,
    col_weights,
    row_weights,
    mem_keys,
    value_table,
    col_down,
    col_up,
    row_down,
    row_up,
    segment_ids,
    adapter_ids,
    pick_ids,
):
    floating = jnp.float32
    brain = jnp.bfloat16
    length = block_in.shape[0]
    col_width = col_weights.shape[2]
    heads_here = col_width // HEAD_DIM
    rows_here = value_table.shape[0]
    pick_tok = pick_ids[:, 0, :]
    query_rows = min(512, length)
    query_blocks = length // query_rows
    sub_count = mem_keys.shape[2]
    half_width = mem_keys.shape[3]
    adapter = adapter_ids[0]
    down_col = lax.dynamic_index_in_dim(col_down, adapter, 1, keepdims=False)
    up_col = lax.dynamic_index_in_dim(col_up, adapter, 1, keepdims=False)
    down_row = lax.dynamic_index_in_dim(row_down, adapter, 1, keepdims=False)
    up_row = lax.dynamic_index_in_dim(row_up, adapter, 1, keepdims=False)
    gain_one = norm_gains[0]
    gain_two = norm_gains[1]
    first_keys = mem_keys[0, 0]
    second_keys = mem_keys[1, 0]
    segments = segment_ids[0]
    positions = jnp.arange(length, dtype=jnp.int32)
    inputs = block_in.astype(floating)
    scale_one = rms_scale(inputs)
    normed_one = (inputs * scale_one * gain_one).astype(brain)
    low_att = jnp.einsum(
        "td,jrd->jtr", normed_one, down_col[:3], preferred_element_type=floating
    ).astype(brain)
    projected = jnp.einsum(
        "td,jde->jte", normed_one, col_weights[:3], preferred_element_type=floating
    )
    projected = projected + ADAPT_SCALE * jnp.einsum(
        "jtr,jre->jte", low_att, up_col[:3], preferred_element_type=floating
    )
    projected = projected.astype(brain)
    queries = projected[0].reshape(length, heads_here, HEAD_DIM)
    keys_here = projected[1].reshape(length, heads_here, HEAD_DIM)
    values_here = projected[2].reshape(length, heads_here, HEAD_DIM)

    def block_logits(start):
        rows_pos = start + jnp.arange(query_rows, dtype=jnp.int32)
        allowed = (segments[:, None] == segments[None, :]) & (
            positions[None, :] <= rows_pos[:, None]
        )
        logits = (
            jnp.einsum("thd,shd->hts", queries, keys_here, preferred_element_type=floating) * 0.125
        )
        return (queries, allowed, jnp.where(allowed[None], logits, -1e30))

    def attend(index):
        query_blk, allowed, logits = block_logits(index * query_rows)
        peak = jnp.max(logits, axis=-1, keepdims=True)
        expos = jnp.exp(logits - peak)
        total = jnp.sum(expos, axis=-1, keepdims=True)
        probs = expos / total
        mixed = jnp.einsum(
            "hts,shd->thd", probs.astype(brain), values_here, preferred_element_type=floating
        )
        return (
            mixed.reshape(query_rows, col_width).astype(brain),
            (peak + jnp.log(total))[:, :, 0],
        )

    att_out, log_totals = lax.map(attend, jnp.arange(query_blocks))
    att_out = att_out.reshape(length, col_width)
    att_part = matmul(att_out, row_weights[0])
    low_part = matmul_nt(att_out, down_row[0])
    att_sum, low_sum = lax.psum((att_part, low_part), "mp")
    low_out = low_sum.astype(brain)
    resid = inputs + att_sum + ADAPT_SCALE * matmul(low_out, up_row[0])
    scale_two = rms_scale(resid)
    normed_two = (resid * scale_two * gain_two).astype(brain)
    low_mem = jnp.einsum(
        "td,jrd->jtr", normed_two, down_col[3:], preferred_element_type=floating
    ).astype(brain)
    mem_query = (
        matmul(normed_two, col_weights[3]) + ADAPT_SCALE * matmul(low_mem[0], up_col[3])
    ).astype(brain)
    gate_pre = matmul(normed_two, col_weights[4]) + ADAPT_SCALE * matmul(low_mem[1], up_col[4])
    first_sub = matmul_nt(mem_query[:, :half_width], first_keys)
    second_sub = matmul_nt(mem_query[:, half_width:], second_keys)

    everyone = ("dp", "mp")
    base = (
        (lax.axis_index("dp") * lax.axis_size("mp") + lax.axis_index("mp")) * rows_here
    ).reshape(1)
    ids_all = lax.all_gather(
        lax.all_gather(pick_tok, "mp", axis=1, tiled=True), "dp", axis=0, tiled=True
    )
    weights, hit_first, hit_second = pick_scores(pick_tok, first_sub, second_sub, sub_count)
    weights_all = lax.all_gather(
        lax.all_gather(weights.astype(brain), "mp", axis=1, tiled=True), "dp", axis=0, tiled=True
    )
    gate_act = jax.nn.silu(gate_pre)
    low_branch_grad = (ADAPT_SCALE * matmul_nt(cotangent, up_row[1])).astype(brain)
    gated_grad = matmul_nt(cotangent, row_weights[1]) + matmul(low_branch_grad, down_row[1])
    mem_grad_cols = (gated_grad * gate_act).astype(brain)
    mem_grad = lax.all_gather(
        lax.all_gather(mem_grad_cols, "mp", axis=1, tiled=True), "dp", axis=0, tiled=True
    )
    spread_w = spread(ids_all, weights_all, base, rows_here)
    partial = matmul(spread_w, value_table).astype(brain)
    mem_cols = lax.psum_scatter(partial, "dp", scatter_dimension=0, tiled=True)
    mem_cols = lax.psum_scatter(mem_cols, "mp", scatter_dimension=1, tiled=True).astype(floating)
    answers = answer(ids_all, mem_grad, value_table, base)
    weight_grad = lax.psum_scatter(answers, "dp", scatter_dimension=0, tiled=True)
    weight_grad = lax.psum_scatter(weight_grad, "mp", scatter_dimension=1, tiled=True)
    table_grad = matmul_tn(spread_w, mem_grad)
    gated = (mem_cols * gate_act).astype(brain)
    branch_part = matmul(gated, row_weights[1])
    low_branch_part = matmul_nt(gated, down_row[1])
    branch_sum, low_branch_sum = (
        lax.psum(branch_part.astype(jnp.bfloat16), "mp").astype(jnp.float32),
        lax.psum(low_branch_part.astype(jnp.bfloat16), "mp").astype(jnp.float32),
    )
    low_branch = low_branch_sum.astype(brain)
    block_out = (resid + branch_sum + ADAPT_SCALE * matmul(low_branch, up_row[1])).astype(brain)
    out_grad = cotangent.astype(floating)
    grad_up_branch = ADAPT_SCALE * matmul_tn(low_branch, cotangent)
    grad_down_branch = matmul_tn(low_branch_grad, gated)
    gate_grad = (gated_grad * mem_cols * silu_slope(gate_pre)).astype(brain)
    score_grad = weights * (
        weight_grad - jnp.sum(weights * weight_grad, axis=-1, keepdims=True)
    )
    first_grad = jnp.sum(jnp.where(hit_first, score_grad[:, :, None], 0.0), axis=1).astype(brain)
    second_grad = jnp.sum(jnp.where(hit_second, score_grad[:, :, None], 0.0), axis=1).astype(brain)
    query_grad = jnp.concatenate(
        [matmul(first_grad, first_keys), matmul(second_grad, second_keys)], axis=1
    ).astype(brain)
    normed_two_part = matmul_nt(query_grad, col_weights[3]) + matmul_nt(gate_grad, col_weights[4])
    low_mem_part = ADAPT_SCALE * jnp.stack(
        [matmul_nt(query_grad, up_col[3]), matmul_nt(gate_grad, up_col[4])]
    )
    grad_up_mem = ADAPT_SCALE * jnp.stack(
        [matmul_tn(low_mem[0], query_grad), matmul_tn(low_mem[1], gate_grad)]
    )
    normed_two_grad, low_mem_grad = lax.psum((normed_two_part, low_mem_part), "mp")
    low_mem_grad = low_mem_grad.astype(brain)
    normed_two_grad = normed_two_grad + jnp.einsum(
        "jtr,jrd->td", low_mem_grad, down_col[3:], preferred_element_type=floating
    )
    grad_down_mem = jnp.einsum(
        "jtr,td->jrd", low_mem_grad, normed_two, preferred_element_type=floating
    )
    weighted_two = gain_two * normed_two_grad
    resid_grad = (
        out_grad
        + scale_two * weighted_two
        - resid * scale_two**3 * jnp.mean(resid * weighted_two, axis=-1, keepdims=True)
    )
    att_branch_grad = resid_grad.astype(brain)
    low_out_grad = (ADAPT_SCALE * matmul_nt(att_branch_grad, up_row[0])).astype(brain)
    grad_up_att = ADAPT_SCALE * matmul_tn(low_out, att_branch_grad)
    att_out_grad = (
        matmul_nt(att_branch_grad, row_weights[0]) + matmul(low_out_grad, down_row[0])
    ).astype(brain)
    grad_down_att = matmul_tn(low_out_grad, att_out)

    def attend_back(carry, index):
        key_acc, value_acc = carry
        start = index * query_rows
        query_blk, allowed, logits = block_logits(start)
        grad_blk = att_out_grad.reshape(query_rows, heads_here, HEAD_DIM)
        probs = jnp.where(allowed[None], jnp.exp(logits - log_totals[index][:, :, None]), 0.0)
        value_acc = value_acc + jnp.einsum(
            "hts,thd->shd", probs.astype(brain), grad_blk, preferred_element_type=floating
        )
        prob_grad = jnp.einsum(
            "thd,shd->hts", grad_blk, values_here, preferred_element_type=floating
        )
        logit_grad = (
            probs * (prob_grad - jnp.sum(probs * prob_grad, axis=-1, keepdims=True))
        ).astype(brain)
        query_part = 0.125 * jnp.einsum(
            "hts,shd->thd", logit_grad, keys_here, preferred_element_type=floating
        )
        key_acc = key_acc + 0.125 * jnp.einsum(
            "hts,thd->shd", logit_grad, query_blk, preferred_element_type=floating
        )
        return ((key_acc, value_acc), query_part.reshape(query_rows, col_width).astype(brain))

    empty = jnp.zeros((length, heads_here, HEAD_DIM), floating)
    (key_grad, value_grad), query_parts = lax.scan(
        attend_back, (empty, empty), jnp.arange(query_blocks)
    )
    proj_grad = jnp.stack(
        [
            query_parts.reshape(length, col_width),
            key_grad.reshape(length, col_width).astype(brain),
            value_grad.reshape(length, col_width).astype(brain),
        ]
    )
    normed_one_part = jnp.einsum(
        "jte,jde->td", proj_grad, col_weights[:3], preferred_element_type=floating
    )
    low_att_part = ADAPT_SCALE * jnp.einsum(
        "jte,jre->jtr", proj_grad, up_col[:3], preferred_element_type=floating
    )
    grad_up_qkv = ADAPT_SCALE * jnp.einsum(
        "jtr,jte->jre", low_att, proj_grad, preferred_element_type=floating
    )
    normed_one_grad, low_att_grad = (
        lax.psum(normed_one_part.astype(jnp.bfloat16), "mp").astype(jnp.float32),
        lax.psum(low_att_part.astype(jnp.bfloat16), "mp").astype(jnp.float32),
    )
    low_att_grad = low_att_grad.astype(brain)
    normed_one_grad = normed_one_grad + jnp.einsum(
        "jtr,jrd->td", low_att_grad, down_col[:3], preferred_element_type=floating
    )
    grad_down_qkv = jnp.einsum(
        "jtr,td->jrd", low_att_grad, normed_one, preferred_element_type=floating
    )
    weighted_one = gain_one * normed_one_grad
    input_grad = (
        resid_grad
        + scale_one * weighted_one
        - inputs * scale_one**3 * jnp.mean(inputs * weighted_one, axis=-1, keepdims=True)
    )
    chosen = (jnp.arange(col_down.shape[1], dtype=jnp.int32) == adapter).astype(floating)
    down_cols_all = (
        jnp.concatenate([grad_down_qkv, grad_down_mem], axis=0)[:, None]
        * chosen[None, :, None, None]
    )
    up_cols_all = (
        jnp.concatenate([grad_up_qkv, grad_up_mem], axis=0)[:, None] * chosen[None, :, None, None]
    )
    down_rows_all = (
        jnp.stack([grad_down_att, grad_down_branch])[:, None] * chosen[None, :, None, None]
    )
    up_rows_all = jnp.stack([grad_up_att, grad_up_branch])[:, None] * chosen[None, :, None, None]
    down_cols_sum, up_cols_sum, down_rows_sum, up_rows_sum = (
        lax.psum(down_cols_all.astype(jnp.bfloat16), "dp").astype(jnp.float32),
        lax.psum(up_cols_all.astype(jnp.bfloat16), "dp").astype(jnp.float32),
        lax.psum(down_rows_all.astype(jnp.bfloat16), "dp").astype(jnp.float32),
        lax.psum(up_rows_all.astype(jnp.bfloat16), "dp").astype(jnp.float32),
    )
    return (
        block_out,
        input_grad,
        table_grad,
        down_cols_sum,
        up_cols_sum,
        down_rows_sum,
        up_rows_sum,
    )


def widen_kernel(*refs):
    for given, made in zip(refs[: len(refs) // 2], refs[len(refs) // 2 :]):
        made[...] = given[...].astype(jnp.float32)


def widen(arrays, steps=8):
    flat = [a.reshape(-1, a.shape[-1]) for a in arrays]
    specs = [pl.BlockSpec((a.shape[0] // steps, a.shape[1]), lambda i: (i, 0)) for a in flat]
    made = pl.pallas_call(
        widen_kernel,
        grid=(steps,),
        in_specs=specs,
        out_specs=specs,
        out_shape=[jax.ShapeDtypeStruct(a.shape, jnp.float32) for a in flat],
        compiler_params=pltpu.CompilerParams(vmem_limit_bytes=60 * 2**20),
        name="widen",
    )(*flat)
    return [out.reshape(a.shape) for out, a in zip(made, arrays)]


def fused(
    block_in,
    cotangent,
    norm_gains,
    col_weights,
    row_weights,
    mem_keys,
    value_table,
    col_down,
    col_up,
    row_down,
    row_up,
    segment_ids,
    adapter_ids,
    pick_ids,
):
    args = dict(
        block_in=block_in,
        cotangent_in=cotangent,
        norm_gains=norm_gains,
        col_weights=col_weights,
        row_weights=row_weights,
        mem_keys=mem_keys.reshape(-1, mem_keys.shape[3]),
        table=value_table,
        col_down_in=col_down,
        col_up_in=col_up,
        row_down_in=row_down,
        row_up_in=row_up,
        segment_ids=segment_ids,
        adapter_ids=adapter_ids,
        pick_ids=pick_ids[:, 0, :],
    )
    outs = whole_block(args, lax.axis_size("dp"), lax.axis_size("mp"))
    return (outs[0], *widen(outs[1:]))


def solution(mesh):
    in_specs = (
        P("dp", None),
        P("dp", None),
        P(),
        P(None, None, "mp"),
        P(None, "mp", None),
        P(None, "mp", None, None),
        P(("dp", "mp"), None),
        P(),
        P(None, None, None, "mp"),
        P(None, None, None, "mp"),
        P(),
        P("dp", None),
        P("dp"),
        P("dp", "mp", None),
    )
    out_specs = (
        P("dp", None),
        P("dp", None),
        P(("dp", "mp"), None),
        P(),
        P(None, None, None, "mp"),
        P(None, None, None, "mp"),
        P(),
    )
    step = fused if mesh.shape["dp"] == 8 else per_device
    return jax.shard_map(
        step, mesh=mesh, in_specs=in_specs, out_specs=out_specs, check_vma=False
    )
```
